32 devices in a mesh: dp: 4 (over z), ctx: 4 (over y, x), heads: 2 (over core).
Axes of the slice: x: 2, y: 2, z: 4, core: 2. Of those that a mesh axis runs over, the one named last changes fastest.
Arguments:
- tokens: bfloat16 [8, 512, 768], P('dp', 'ctx'), may hold values from -6 to 6
- cotangent: bfloat16 [8, 512, 768], P('dp', 'ctx'), may hold values from -6 to 6
- lengths: int32 [8], replicated, may hold values from 256 to 512, as said below
- dealing: int32 [8], replicated, may hold values from 0 to 7, each once
- qkv_weight: bfloat16 [2, 768, 3, 768], P(None, 'dp', None, 'heads')
- out_weight: bfloat16 [2, 768, 768], P(None, 'dp', 'heads'), may hold values from -0.875 to 0.875
- glu_weight: bfloat16 [2, 768, 2, 3072], P(None, 'dp', None, 'heads'), may hold values from -0.21875 to 0.21875
- down_weight: bfloat16 [2, 768, 3072], P(None, 'dp', 'heads'), may hold values from -0.109375 to 0.109375
- biases: float32 [2, 6, 768], replicated, may hold values from -3 to 3
- gains: float32 [2, 2, 768], replicated, may hold values from 0.1 to 1.9
Outputs:
- outputs: bfloat16 [8, 512, 768], P('dp', 'ctx')
- grad_tokens: float32 [8, 512, 768], P('dp', 'ctx')
- grad_qkv: float32 [2, 768, 3, 768], P(None, 'dp', None, 'heads')
- grad_out: float32 [2, 768, 768], P(None, 'dp', 'heads')
- grad_glu: float32 [2, 768, 2, 3072], P(None, 'dp', None, 'heads')
- grad_down: float32 [2, 768, 3072], P(None, 'dp', 'heads')
- grad_biases: float32 [2, 6, 768], P(None, None, 'dp')
- grad_gains: float32 [2, 2, 768], P(None, None, 'dp')
- clipped_qk: float32 [2, 768, 2, 768], P(None, 'dp', None, 'heads')
The draws below stay inside these ranges and needn't reach their ends.
Inputs may be any that keep to these rules, and one draw needn't show every extreme that they name: `lengths`: at least one sequence has exactly 512 tokens. `dealing`: a permutation of the 8 sequences.
All inputs are finite; a program needn't handle non-finite values.
Results may differ from the reference program's by a relative error of at most 0.023.
Values may be sent and summed in bfloat16 or wider, within the bound.
No kernel may reach another device: no remote copies, remote signals or barrier semaphores. Data moves between devices by JAX's collectives and lax.ppermute only.
A program may use at most 192 MiB of HBM per device.

```python
import math
import jax
import jax.numpy as jnp
from jax import lax

D = 768
HEADS = 12
HEAD_DIM = 64
FF = 3072
LAYERS = 2
SEQ_LEN = 512
SEQS = 8


def draw_lengths(key, part):
    spread_key = jax.random.fold_in(key, 21)
    chosen_key = jax.random.fold_in(key, 22)
    spread = jax.random.randint(spread_key, (SEQS,), SEQ_LEN // 2, SEQ_LEN + 1)
    chosen = jax.random.randint(chosen_key, (), 0, SEQS)
    return jnp.where(jnp.arange(SEQS) == chosen, SEQ_LEN, spread).astype(jnp.int32)


def draw_qkv_weight(key, part):
    base_key = jax.random.fold_in(key, 11)
    scale_key = jax.random.fold_in(key, 12)
    base = jax.random.normal(base_key, (LAYERS, D, 3, HEADS, HEAD_DIM), jnp.float32)
    head_scale = jnp.exp(jax.random.uniform(scale_key, (LAYERS, 1, 2, HEADS, 1), jnp.float32, math.log(0.75), math.log(1.33)))
    full_scale = jnp.concatenate([head_scale, jnp.ones((LAYERS, 1, 1, HEADS, 1), jnp.float32)], axis=2)
    drawn = base * full_scale * D ** (-0.5)
    return drawn.reshape(LAYERS, D, 3, D).astype(jnp.bfloat16)


def block_levels(stream_key, dims, split, low, high):
    def one(axis_at, parts):
        draws = jax.random.uniform(jax.random.fold_in(jax.random.fold_in(stream_key, 6), axis_at), (parts,), jnp.float32, low / len(split), high / len(split))
        return jnp.repeat(jnp.exp(draws), dims[axis_at] // parts).reshape((-1,) + (1,) * (len(dims) - axis_at - 1))

    level = one(*split[0])
    for cut in split[1:]:
        level = level * one(*cut)
    return level


def normal_values(stream_key, dims, deviation, reach, shards=(), held_as=jnp.bfloat16):
    values = deviation * jax.random.normal(stream_key, dims, jnp.float32)
    if shards:
        values = values * block_levels(stream_key, dims, shards, -0.22, 0.18)
    return jnp.clip(values, -reach, reach).astype(held_as)


def setup_inputs(seed: int = 0) -> dict:
    key_list = jax.random.split(jax.random.key(seed), 11)
    return {
        "tokens": normal_values(key_list[0], (SEQS, SEQ_LEN, D), 1.0, 6.0, ((0, 4), (1, 4))),
        "cotangent": normal_values(key_list[1], (SEQS, SEQ_LEN, D), 1.0, 6.0, ((0, 4), (1, 4))),
        "lengths": draw_lengths(jax.random.fold_in(key_list[10], 71), 0),
        "dealing": jax.random.permutation(key_list[3], SEQS).astype(jnp.int32),
        "qkv_weight": draw_qkv_weight(jax.random.fold_in(key_list[10], 71), 0),
        "out_weight": normal_values(key_list[5], (LAYERS, D, D), (D // 16) ** -0.5, 0.875, ((1, 4), (2, 2))),
        "glu_weight": normal_values(key_list[6], (LAYERS, D, 2, FF), D ** -0.5, 0.21875, ((1, 4), (3, 2))),
        "down_weight": normal_values(key_list[7], (LAYERS, D, FF), FF ** -0.5, 0.109375, ((1, 4), (2, 2))),
        "biases": normal_values(key_list[8], (LAYERS, 6, D), 0.5, 3.0, (), jnp.float32),
        "gains": jnp.clip(1.0 + 0.18 * jax.random.normal(key_list[9], (LAYERS, 2, D), jnp.float32), 0.1, 1.9),
    }


EPSILON = 1e-12
NEGATIVE = -1e+30
CLIP_LIMIT = 4.0
STEP_SIZE = 0.0008

@jax.custom_vjp
def low(v):
    return lax.optimization_barrier(v.astype(jnp.bfloat16)).astype(jnp.float32)

@jax.custom_vjp
def low_back(v):
    return v

def low_keep(v):
    return (low(v), None)

def low_pass(kept, grad):
    return (grad,)

def back_keep(v):
    return (v, None)

def back_low(kept, grad):
    return (low(grad),)
low.defvjp(low_keep, low_pass)
low_back.defvjp(back_keep, back_low)

def power_slopes(head_count):
    first_slope = 2.0 ** (-8.0 / head_count)
    return [first_slope ** (position + 1) for position in range(head_count)]

def alibi_slopes(head_count):
    closest = 2 ** int(math.floor(math.log2(head_count)))
    slopes = power_slopes(closest)
    if closest < head_count:
        slopes = slopes + power_slopes(2 * closest)[0::2][:head_count - closest]
    return slopes

def layer_norm(values, gain_row, shift_row):
    average = lax.optimization_barrier(jnp.mean(values, axis=-1, keepdims=True))
    centred = values - average
    spread = lax.optimization_barrier(jnp.mean(centred * centred, axis=-1, keepdims=True))
    return centred * lax.rsqrt(spread + EPSILON) * gain_row + shift_row

def split_heads(values):
    return values.reshape(SEQ_LEN, HEADS, HEAD_DIM).transpose(1, 0, 2)

def forward(parameters, tokens_all, seq_lengths):
    qkv_weight, out_weight, glu_weight, down_weight, biases, gains = parameters
    slopes = jnp.array(alibi_slopes(HEADS), jnp.float32)
    positions = jnp.arange(SEQ_LEN, dtype=jnp.int32)
    distance = jnp.abs(positions[:, None] - positions[None, :]).astype(jnp.float32)
    score_scale = float(HEAD_DIM) ** (-0.5)
    highest = lax.Precision.HIGHEST

    def one_sequence(sequence, sequence_length):
        valid_rows = positions < sequence_length
        pair_valid = valid_rows[:, None] & valid_rows[None, :]
        residual = sequence
        top_list = []
        for layer_index in range(LAYERS):
            vectors = biases[layer_index]
            low_input = low(residual)
            projected = jnp.dot(low_input, qkv_weight[layer_index].reshape(D, 3 * D), precision=highest)
            queries = low_back(low(projected[:, :D] + vectors[0]))
            keys = low_back(low(projected[:, D:2 * D]))
            values = low_back(low(projected[:, 2 * D:] + vectors[1]))

            def attend(head_items):
                query_head, key_head, value_head, head_slope = head_items
                raw_scores = jnp.dot(query_head, key_head.T, precision=highest) * score_scale
                top_logit = jnp.max(jnp.where(pair_valid, raw_scores, NEGATIVE))
                scores = low_back(raw_scores - head_slope * distance)
                scores = jnp.where(valid_rows[None, :], scores, NEGATIVE)
                attn_probs = low(jax.nn.softmax(scores, axis=-1))
                return (jnp.dot(attn_probs, value_head, precision=highest), top_logit)
            mixed_heads, top_logits = lax.map(jax.checkpoint(attend), (split_heads(queries), split_heads(keys), split_heads(values), slopes))
            top_list.append(top_logits)
            mixed = low_back(low(mixed_heads.transpose(1, 0, 2).reshape(SEQ_LEN, D)))
            attention = low_back(jnp.dot(mixed, out_weight[layer_index].T, precision=highest) + vectors[2])
            hidden_in = layer_norm(residual + attention, gains[layer_index, 0], vectors[4])
            hidden_low = low(hidden_in)
            gate_up = low_back(jnp.dot(hidden_low, glu_weight[layer_index].reshape(D, 2 * FF), precision=highest))
            activated = low(jax.nn.gelu(gate_up[:, :FF], approximate=False) * gate_up[:, FF:])
            feed_out = low_back(jnp.dot(activated, down_weight[layer_index].T, precision=highest) + vectors[3])
            residual = layer_norm(hidden_in + feed_out, gains[layer_index, 1], vectors[5])
        return (residual * valid_rows[:, None].astype(jnp.float32), jnp.stack(top_list))

    def scan_step(carry, slot_items):
        sequence_out, sequence_tops = jax.checkpoint(one_sequence)(slot_items[0], slot_items[1])
        return (jnp.maximum(carry, sequence_tops), sequence_out)
    tops, outputs = lax.scan(scan_step, jnp.full((LAYERS, HEADS), NEGATIVE, jnp.float32), (tokens_all, seq_lengths))
    return (outputs, tops)

def reference(tokens, cotangent, lengths, dealing, qkv_weight, out_weight, glu_weight, down_weight, biases, gains):
    parameters = (qkv_weight.astype(jnp.float32), out_weight.astype(jnp.float32), glu_weight.astype(jnp.float32), down_weight.astype(jnp.float32), biases, gains)
    seq_lengths = lengths[dealing]

    def forward_fixed(param_tree, tokens_float):
        return forward(param_tree, tokens_float, seq_lengths)
    outputs, pullback, tops = jax.vjp(forward_fixed, parameters, tokens.astype(jnp.float32), has_aux=True)
    grad_params, grad_tokens = pullback(cotangent.astype(jnp.float32))
    grad_qkv, grad_out, grad_glu, grad_down, grad_biases, grad_gains = grad_params
    factor = CLIP_LIMIT / jnp.maximum(tops, CLIP_LIMIT)
    factor_cols = jnp.repeat(factor, HEAD_DIM, axis=1)
    clipped_qk = (parameters[0][:, :, :2, :] - STEP_SIZE * grad_qkv[:, :, :2, :]) * factor_cols[:, None, None, :]
    return (outputs.astype(jnp.bfloat16), grad_tokens, grad_qkv, grad_out, grad_glu, grad_down, grad_biases, grad_gains, clipped_qk)
```

```python
import functools
import math

import jax
import jax.numpy as jnp
from jax import lax
from jax.experimental import pallas as pl
from jax.experimental.pallas import tpu as pltpu
from jax.sharding import PartitionSpec as P

HEADS = 12
HEAD_DIM = 64


EPSILON = 1e-12
NEGATIVE = -1e30
CLIP_LIMIT = 4.0
STEP_SIZE = 0.0008
VMEM_LIMIT = 48 * 1024 * 1024


def power_slopes(head_count):
    first_slope = 2.0 ** (-8.0 / head_count)
    return [first_slope ** (position + 1) for position in range(head_count)]


def alibi_slopes(head_count):
    closest = 2 ** int(math.floor(math.log2(head_count)))
    slopes = power_slopes(closest)
    slopes = slopes + power_slopes(2 * closest)[0::2][: head_count - closest]
    return slopes


def dot(a, b):
    return jnp.dot(a, b, preferred_element_type=jnp.float32)


def contract_rows(former, latter):
    return lax.dot_general(
        former, latter, (((0,), (0,)), ((), ())), preferred_element_type=jnp.float32
    )


def contract_cols(former, latter):
    return lax.dot_general(
        former, latter, (((1,), (1,)), ((), ())), preferred_element_type=jnp.float32
    )


def norm_forward(z, gain, shift):
    mean = jnp.mean(z, axis=-1, keepdims=True)
    centred = z - mean
    var = jnp.mean(centred * centred, axis=-1, keepdims=True)
    rstd = lax.rsqrt(var + EPSILON)
    n = centred * rstd
    return n * gain + shift, n, rstd


def norm_backward(grad, n, rstd, gain):
    scaled = grad * gain
    mean_one = jnp.mean(scaled, axis=-1, keepdims=True)
    mean_two = jnp.mean(scaled * n, axis=-1, keepdims=True)
    dz = (scaled - mean_one - n * mean_two) * rstd
    return dz, jnp.sum(grad * n, axis=0), jnp.sum(grad, axis=0)


def cdf(x):
    return 0.5 * (1.0 + lax.erf(x * (0.5**0.5)))


def positions_of(shape, axis, rows, part):
    index = lax.broadcasted_iota(jnp.int32, shape, axis)
    shift = rows.bit_length() - 1
    return (((index >> shift) ^ part) << shift) | (index & (rows - 1))


def attend_kernel(rows, info_ref, slope_ref, qkv_ref, mixed_ref, probs_ref, top_ref):
    total = qkv_ref.shape[0]
    cols = qkv_ref.shape[1] // 3
    part = info_ref[0]
    length = info_ref[1]
    key_pos = positions_of((1, total), 1, rows, part)
    key_ok = key_pos < length
    tops = []
    for h in range(cols // HEAD_DIM):
        lo = h * HEAD_DIM
        key = qkv_ref[:, cols + lo : cols + lo + HEAD_DIM]
        value = qkv_ref[:, 2 * cols + lo : 2 * cols + lo + HEAD_DIM]
        slope = slope_ref[h]
        top = jnp.full((1, 1), NEGATIVE, jnp.float32)
        for b in range(total // rows):
            span = slice(b * rows, (b + 1) * rows)
            query = qkv_ref[span, lo : lo + HEAD_DIM] * jnp.bfloat16(HEAD_DIM**-0.5)
            raw = contract_cols(query, key)
            pos = ((b ^ part) * rows) + lax.broadcasted_iota(jnp.int32, (rows, 1), 0)
            masked = jnp.where(key_ok, raw, NEGATIVE)
            block_top = jnp.max(masked, axis=1, keepdims=True)
            block_top = jnp.where(pos < length, block_top, NEGATIVE)
            top = jnp.maximum(top, jnp.max(block_top, axis=0, keepdims=True))
            distance = jnp.abs(pos - key_pos).astype(jnp.float32)
            scores = masked - slope * distance
            row_max = jnp.max(scores, axis=1, keepdims=True)
            exponent = jnp.exp(scores - row_max)
            totals = jnp.sum(exponent, axis=1, keepdims=True)
            probs = (exponent * (1.0 / totals)).astype(jnp.bfloat16)
            probs_ref[h, span, :] = probs
            mixed_ref[span, lo : lo + HEAD_DIM] = dot(probs, value).astype(jnp.bfloat16)
        tops.append(top)
    lane = lax.broadcasted_iota(jnp.int32, (8, 128), 1)
    packed = jnp.full((8, 128), NEGATIVE, jnp.float32)
    for h, top in enumerate(tops):
        packed = jnp.where(lane == h, top, packed)
    top_ref[...] = packed


def attend(info, slopes, qkv, rows):
    total, width = qkv.shape
    cols = width // 3
    heads = cols // HEAD_DIM
    smem = pl.BlockSpec(memory_space=pltpu.SMEM)
    vmem = pl.BlockSpec(memory_space=pltpu.VMEM)
    return pl.pallas_call(
        functools.partial(attend_kernel, rows),
        out_shape=(
            jax.ShapeDtypeStruct((total, cols), jnp.bfloat16),
            jax.ShapeDtypeStruct((heads, total, total), jnp.bfloat16),
            jax.ShapeDtypeStruct((8, 128), jnp.float32),
        ),
        in_specs=[smem, smem, vmem],
        out_specs=(vmem, vmem, vmem),
        compiler_params=pltpu.CompilerParams(vmem_limit_bytes=VMEM_LIMIT),
        cost_estimate=pl.CostEstimate(
            flops=4 * heads * total * total * HEAD_DIM * 4,
            bytes_accessed=total * width * 2 + heads * total * total * 2,
            transcendentals=heads * total * total,
        ),
        name="attend",
    )(info, slopes, qkv)


def attend_back_kernel(rows, qkv_ref, probs_ref, grad_ref, out_ref, gs_ref):
    total = qkv_ref.shape[0]
    cols = qkv_ref.shape[1] // 3
    scale = HEAD_DIM**-0.5
    for h in range(cols // HEAD_DIM):
        lo = h * HEAD_DIM
        query = qkv_ref[:, lo : lo + HEAD_DIM]
        key = qkv_ref[:, cols + lo : cols + lo + HEAD_DIM]
        value = qkv_ref[:, 2 * cols + lo : 2 * cols + lo + HEAD_DIM]
        grad = grad_ref[:, lo : lo + HEAD_DIM]
        for b in range(total // rows):
            span = slice(b * rows, (b + 1) * rows)
            probs = probs_ref[h, span, :].astype(jnp.float32)
            grad_probs = contract_cols(grad_ref[span, lo : lo + HEAD_DIM], value)
            inner = jnp.sum(grad_probs * probs, axis=1, keepdims=True)
            grad_scores = (probs * (grad_probs - inner)).astype(jnp.bfloat16)
            gs_ref[span, :] = grad_scores
            out_ref[span, lo : lo + HEAD_DIM] = (dot(grad_scores, key) * scale).astype(
                jnp.bfloat16
            )
        out_ref[:, cols + lo : cols + lo + HEAD_DIM] = (
            contract_rows(gs_ref[...], query) * scale
        ).astype(jnp.bfloat16)
        out_ref[:, 2 * cols + lo : 2 * cols + lo + HEAD_DIM] = contract_rows(
            probs_ref[h], grad
        ).astype(jnp.bfloat16)


def attend_back(qkv, probs, grad_mixed, rows):
    total, width = qkv.shape
    heads = probs.shape[0]
    vmem = pl.BlockSpec(memory_space=pltpu.VMEM)
    return pl.pallas_call(
        functools.partial(attend_back_kernel, rows),
        out_shape=jax.ShapeDtypeStruct((total, width), jnp.bfloat16),
        in_specs=[vmem, vmem, vmem],
        out_specs=vmem,
        scratch_shapes=[pltpu.VMEM((total, total), jnp.bfloat16)],
        compiler_params=pltpu.CompilerParams(vmem_limit_bytes=VMEM_LIMIT),
        cost_estimate=pl.CostEstimate(
            flops=8 * heads * total * total * HEAD_DIM * 4,
            bytes_accessed=total * width * 4 + heads * total * total * 2,
            transcendentals=0,
        ),
        name="attend_back",
    )(qkv, probs, grad_mixed)


def shards(
    tokens,
    cotangent,
    lengths,
    dealing,
    qkv_weight,
    out_weight,
    glu_weight,
    down_weight,
    biases,
    gains,
):
    slots, rows, width = tokens.shape
    layers = qkv_weight.shape[0]
    parts = lax.axis_size("ctx")
    cores = lax.axis_size("heads")
    groups = lax.axis_size("dp")
    part = lax.axis_index("ctx")
    core = lax.axis_index("heads")
    group = lax.axis_index("dp")
    local_rows = qkv_weight.shape[1]
    half = qkv_weight.shape[3]
    cols = half * cores // parts
    local_heads = cols // HEAD_DIM
    quarter = glu_weight.shape[3] // parts
    per_core = parts // cores
    home = part // per_core == core
    offset = (part % per_core) * cols

    def swap(x):
        return lax.ppermute(x, "heads", [(j, cores - 1 - j) for j in range(cores)])

    def hop(x, k):
        return lax.ppermute(x, "ctx", [(j, j ^ k) for j in range(parts)])

    def gather(x):
        return [x] + [hop(x, k) for k in range(1, parts)]

    def scatter(blocks):
        total = blocks[0]
        for k in range(1, parts):
            total = total + hop(blocks[k].astype(jnp.bfloat16), k).astype(jnp.float32)
        return total

    def weave(x):
        blocks = jnp.stack(gather(x))
        return [
            lax.dynamic_index_in_dim(blocks, part ^ q, 0, keepdims=False) for q in range(parts)
        ]

    query_key = lax.dynamic_slice_in_dim(qkv_weight[:, :, :2, :], offset, cols, 3)
    value_w = lax.dynamic_slice_in_dim(qkv_weight[:, :, 2, :], offset, cols, 2)
    out_w = lax.dynamic_slice_in_dim(out_weight, offset, cols, 2)
    value_out = jnp.concatenate([value_w, out_w], axis=2)
    query_key = jnp.concatenate([query_key[:, :, 0], query_key[:, :, 1]], axis=2)
    attn_shard = jnp.where(home, query_key, swap(value_out))
    glu_part = lax.dynamic_slice_in_dim(glu_weight, part * quarter, quarter, 3)
    down_part = lax.dynamic_slice_in_dim(down_weight, part * quarter, quarter, 2)
    feed_shard = jnp.concatenate([glu_part[:, :, 0], glu_part[:, :, 1], down_part], axis=2)

    attn_full = []
    feed_full = []
    for l in range(layers):
        if l == 0:
            attn_own = lax.all_gather(attn_shard[l], "dp", axis=0, tiled=True)
            feed_own = lax.all_gather(feed_shard[l], "dp", axis=0, tiled=True)
        else:
            both = lax.all_gather(
                jnp.concatenate([attn_shard[l], feed_shard[l]], axis=1), "dp", axis=0, tiled=True
            )
            attn_own = both[:, : 2 * cols]
            feed_own = both[:, 2 * cols :]
        attn_other = swap(attn_own)
        query_key = jnp.where(home, attn_own, attn_other)
        value_out = jnp.where(home, attn_other, attn_own)
        attn_full.append(
            (jnp.concatenate([query_key, value_out[:, :cols]], axis=1), value_out[:, cols:])
        )
        feed_other = swap(feed_own)
        feed_full.append(
            [(w[:, : 2 * quarter], w[:, 2 * quarter :]) for w in (feed_own, feed_other)]
        )

    slot = group * slots + core
    slot_ids = jnp.arange(lengths.shape[0], dtype=jnp.int32)
    sequence = jnp.sum(jnp.where(slot_ids == slot, dealing, 0))
    length = jnp.sum(jnp.where(slot_ids == sequence, lengths, 0))
    info = jnp.stack([part, length]).astype(jnp.int32)
    slopes = lax.dynamic_slice_in_dim(
        jnp.array(alibi_slopes(HEADS), jnp.float32), part * local_heads, local_heads
    )
    row_pos = part * rows + jnp.arange(rows, dtype=jnp.int32)
    row_mask = (row_pos < length).astype(jnp.float32)[:, None]

    def span(x, b):
        return x[b * rows : (b + 1) * rows]

    residual = lax.dynamic_index_in_dim(tokens, core, 0, keepdims=False).astype(jnp.float32)
    saved = []
    tops = []
    for l in range(layers):
        vectors = biases[l]
        qkv_w, out_w = attn_full[l]
        low = gather(residual.astype(jnp.bfloat16))
        bias = jnp.concatenate(
            [
                lax.dynamic_slice_in_dim(vectors[0], part * cols, cols),
                jnp.zeros((cols,), jnp.float32),
                lax.dynamic_slice_in_dim(vectors[1], part * cols, cols),
            ]
        )
        qkv = jnp.concatenate([(dot(b, qkv_w) + bias).astype(jnp.bfloat16) for b in low])
        mixed, probs, top = attend(info, slopes, qkv, rows)
        tops.append(top[0, :local_heads])
        attention = scatter([contract_cols(span(mixed, b), out_w) for b in range(parts)])
        hidden, n_one, r_one = norm_forward(
            residual + attention + vectors[2], gains[l, 0], vectors[4]
        )
        hidden_low = gather(hidden.astype(jnp.bfloat16))
        gates = [[], []]
        acts = [[], []]
        sums = []
        for b in range(parts):
            total = None
            for side, (glu_w, down_w) in enumerate(feed_full[l]):
                packed = dot(hidden_low[b], glu_w)
                gate, up = packed[:, :quarter], packed[:, quarter:]
                act = (gate * cdf(gate) * up).astype(jnp.bfloat16)
                gates[side].append(packed)
                acts[side].append(act)
                term = contract_cols(act, down_w)
                total = term if total is None else total + term
            sums.append(total)
        feed_out = scatter(sums)
        result, n_two, r_two = norm_forward(
            hidden + feed_out + vectors[3], gains[l, 1], vectors[5]
        )
        saved.append((low, qkv, probs, mixed, n_one, r_one, hidden_low, gates, acts, n_two, r_two))
        residual = result

    outputs = (residual * row_mask).astype(jnp.bfloat16)
    grad = lax.dynamic_index_in_dim(cotangent, core, 0, keepdims=False).astype(jnp.float32)
    grad = grad * row_mask

    bias_rows = [None] * layers
    gain_rows = [None] * layers
    attn_parts = [None] * layers
    feed_parts = [None] * layers
    for l in reversed(range(layers)):
        low, qkv, probs, mixed, n_one, r_one, hidden_low, gates, acts, n_two, r_two = saved[l]
        qkv_w, out_w = attn_full[l]
        grad_second, gain_two, shift_two = norm_backward(grad, n_two, r_two, gains[l, 1])
        feed_low = grad_second.astype(jnp.bfloat16)
        feed_grad = gather(feed_low)
        packed_grads = [[], []]
        sums = []
        for b in range(parts):
            total = None
            for side, (glu_w, down_w) in enumerate(feed_full[l]):
                grad_act = dot(feed_grad[b], down_w)
                packed = gates[side][b]
                gate, up = packed[:, :quarter], packed[:, quarter:]
                phi = cdf(gate)
                slope = phi + gate * (jnp.exp(-0.5 * gate * gate) * (2.0 * math.pi) ** -0.5)
                packed_grad = jnp.concatenate(
                    [grad_act * up * slope, grad_act * (gate * phi)], axis=1
                ).astype(jnp.bfloat16)
                packed_grads[side].append(packed_grad)
                term = contract_cols(packed_grad, glu_w)
                total = term if total is None else total + term
            sums.append(total)
        grad_hidden = grad_second + scatter(sums)
        feed_all = jnp.concatenate(feed_grad)
        hidden_all = jnp.concatenate(hidden_low)
        terms = [
            jnp.concatenate(
                [
                    contract_rows(hidden_all, jnp.concatenate(packed_grads[side])),
                    contract_rows(feed_all, jnp.concatenate(acts[side])),
                ],
                axis=1,
            )
            for side in range(2)
        ]
        feed_total = terms[0] + swap(terms[1].astype(jnp.bfloat16)).astype(jnp.float32)
        feed_parts[l] = lax.psum_scatter(
            feed_total.astype(jnp.bfloat16), "dp", scatter_dimension=0, tiled=True
        )

        grad_first, gain_one, shift_one = norm_backward(grad_hidden, n_one, r_one, gains[l, 0])
        attn_low = grad_first.astype(jnp.bfloat16)
        attn_grad = gather(attn_low)
        attn_all = jnp.concatenate(attn_grad)
        grad_mixed = dot(attn_all, out_w).astype(jnp.bfloat16)
        grad_qkv = attend_back(qkv, probs, grad_mixed, rows)
        grad = grad_first + scatter(
            [contract_cols(span(grad_qkv, b), qkv_w) for b in range(parts)]
        )
        low_all = jnp.concatenate(low)
        qkv_term = contract_rows(low_all, grad_qkv)
        out_term = contract_rows(attn_all, mixed)
        qk_term = qkv_term[:, : 2 * cols]
        vo_term = jnp.concatenate([qkv_term[:, 2 * cols :], out_term], axis=1)
        keep = jnp.where(home, qk_term, vo_term)
        give = jnp.where(home, vo_term, qk_term).astype(jnp.bfloat16)
        attn_total = keep + swap(give).astype(jnp.float32)
        attn_parts[l] = lax.psum_scatter(
            attn_total.astype(jnp.bfloat16), "dp", scatter_dimension=0, tiled=True
        )
        column_sums = jnp.sum(grad_qkv.astype(jnp.float32), axis=0)
        empty = jnp.zeros((width,), jnp.float32)
        bias_rows[l] = jnp.stack(
            [
                lax.dynamic_update_slice_in_dim(empty, column_sums[:cols], part * cols, 0),
                lax.dynamic_update_slice_in_dim(empty, column_sums[2 * cols :], part * cols, 0),
                jnp.sum(attn_low.astype(jnp.float32), axis=0),
                jnp.sum(feed_low.astype(jnp.float32), axis=0),
                shift_one,
                shift_two,
            ]
        )
        gain_rows[l] = jnp.stack([gain_one, gain_two])

    def both_slots(x):
        other = swap(x)
        return jnp.where(core == 0, jnp.stack([x, other]), jnp.stack([other, x]))

    out_tokens = both_slots(outputs)
    grad_tokens = both_slots(grad)

    joint = ("ctx", "heads")

    def share(x, k):
        pairs = [
            (j * cores + j // per_core, (j ^ k) * cores + j // per_core) for j in range(parts)
        ]
        return lax.ppermute(x, joint, pairs)

    qkv_out, out_out, glu_out, down_out = [], [], [], []
    for l in range(layers):
        blocks = weave(feed_parts[l])
        glu_out.append(
            jnp.stack(
                [
                    jnp.concatenate([b[:, s * quarter : (s + 1) * quarter] for b in blocks], axis=1)
                    for s in range(2)
                ],
                axis=1,
            ).astype(jnp.float32)
        )
        down_out.append(
            jnp.concatenate([b[:, 2 * quarter :] for b in blocks], axis=1).astype(jnp.float32)
        )
        whole = jnp.concatenate([attn_parts[l], swap(attn_parts[l])], axis=1)
        shared = [share(whole, k) for k in range(1, parts)]
        same = jnp.where(home, whole, shared[1])
        cross = jnp.where(home, shared[0], shared[2])
        even = part % per_core == 0
        first = jnp.where(even, same, cross).reshape(local_rows, 4, cols)
        second = jnp.where(even, cross, same).reshape(local_rows, 4, cols)
        joined = jnp.concatenate([first, second], axis=2).astype(jnp.float32)
        qkv_out.append(joined[:, :3])
        out_out.append(joined[:, 3])
    grad_qkv = jnp.stack(qkv_out)

    small = jnp.concatenate([jnp.stack(bias_rows), jnp.stack(gain_rows)], axis=1)
    small = lax.psum(small, ("dp", "ctx", "heads"))
    small = lax.dynamic_slice_in_dim(small, group * local_rows, local_rows, 2)

    top = jnp.full((layers, HEADS), NEGATIVE, jnp.float32)
    top = lax.dynamic_update_slice_in_dim(top, jnp.stack(tops), part * local_heads, 1)
    top = lax.pmax(top, ("dp", "ctx", "heads"))
    factor = CLIP_LIMIT / jnp.maximum(top, CLIP_LIMIT)
    factor = lax.dynamic_slice_in_dim(factor, core * (HEADS // cores), HEADS // cores, 1)
    factor_cols = jnp.repeat(factor, HEAD_DIM, axis=1)
    clipped_qk = (
        qkv_weight[:, :, :2, :].astype(jnp.float32) - STEP_SIZE * grad_qkv[:, :, :2, :]
    ) * factor_cols[:, None, None, :]
    return (
        out_tokens,
        grad_tokens,
        grad_qkv,
        jnp.stack(out_out),
        jnp.stack(glu_out),
        jnp.stack(down_out),
        small[:, :6],
        small[:, 6:],
        clipped_qk,
    )


def solution(mesh):
    in_specs = (
        P("dp", "ctx", None),
        P("dp", "ctx", None),
        P(),
        P(),
        P(None, "dp", None, "heads"),
        P(None, "dp", "heads"),
        P(None, "dp", None, "heads"),
        P(None, "dp", "heads"),
        P(),
        P(),
    )
    out_specs = (
        P("dp", "ctx", None),
        P("dp", "ctx", None),
        P(None, "dp", None, "heads"),
        P(None, "dp", "heads"),
        P(None, "dp", None, "heads"),
        P(None, "dp", "heads"),
        P(None, None, "dp"),
        P(None, None, "dp"),
        P(None, "dp", None, "heads"),
    )
    return jax.shard_map(shards, mesh=mesh, in_specs=in_specs, out_specs=out_specs, check_vma=False)
```

```python
import functools
import math

import jax
import jax.numpy as jnp
from jax import lax
from jax.experimental import pallas as pl
from jax.experimental.pallas import tpu as pltpu
from jax.sharding import PartitionSpec as P

HEADS = 12
HEAD_DIM = 64


EPSILON = 1e-12
NEGATIVE = -1e30
CLIP_LIMIT = 4.0
STEP_SIZE = 0.0008
MIB = 1024 * 1024


def power_slopes(head_count):
    first_slope = 2.0 ** (-8.0 / head_count)
    return [first_slope ** (position + 1) for position in range(head_count)]


def alibi_slopes(head_count):
    closest = 2 ** int(math.floor(math.log2(head_count)))
    slopes = power_slopes(closest)
    slopes = slopes + power_slopes(2 * closest)[0::2][: head_count - closest]
    return slopes


def dot(a, b):
    return jnp.dot(a, b, preferred_element_type=jnp.float32)


def contract_rows(former, latter):
    return lax.dot_general(
        former, latter, (((0,), (0,)), ((), ())), preferred_element_type=jnp.float32
    )


def contract_cols(former, latter):
    return lax.dot_general(
        former, latter, (((1,), (1,)), ((), ())), preferred_element_type=jnp.float32
    )


def low(x):
    return x.astype(jnp.bfloat16)


def wide(x):
    return x.astype(jnp.float32)


def positions_of(shape, axis, rows, part):
    index = lax.broadcasted_iota(jnp.int32, shape, axis)
    shift = rows.bit_length() - 1
    return (((index >> shift) ^ part) << shift) | (index & (rows - 1))


def join(refs):
    return jnp.concatenate([r[...] for r in refs], axis=0)


def call(body, name, outs, *args, scratch=(), flops=0, exps=0, limit=16, alias=None):
    spaces = {"s": pltpu.SMEM, "h": pltpu.HBM, "d": pl.ANY, "v": pltpu.VMEM}
    args = [a if isinstance(a, tuple) else ("v", a) for a in args]
    outs = [o if len(o) == 3 else (*o, "v") for o in outs]
    values = [
        pltpu.with_memory_space_constraint(a[1], pltpu.HBM) if a[0] == "h" else a[1] for a in args
    ]
    shapes = tuple(
        pltpu.HBM(o[0], o[1]) if o[2] == "h" else jax.ShapeDtypeStruct(o[0], o[1]) for o in outs
    )
    moved = sum(v.size * v.dtype.itemsize for v in values)
    moved += sum(math.prod(o[0]) * jnp.dtype(o[1]).itemsize for o in outs)
    return pl.pallas_call(
        body,
        out_shape=shapes,
        in_specs=[pl.BlockSpec(memory_space=spaces[a[0]]) for a in args],
        out_specs=tuple(pl.BlockSpec(memory_space=spaces[o[2]]) for o in outs),
        scratch_shapes=list(scratch),
        input_output_aliases=alias or {},
        compiler_params=pltpu.CompilerParams(vmem_limit_bytes=limit * MIB),
        cost_estimate=pl.CostEstimate(flops=flops, bytes_accessed=moved, transcendentals=exps),
        name=name,
    )(*values)


def start(source, target, sem):
    copy = pltpu.make_async_copy(source, target, sem)
    copy.start()
    return copy


def bf16(*shape):
    return pltpu.VMEM(shape, jnp.bfloat16)


def f32(*shape):
    return pltpu.VMEM(shape, jnp.float32)


def sems(count):
    return pltpu.SemaphoreType.DMA((count,))


def pick(flag, one, two):
    chosen = jnp.full(one.shape, flag, jnp.int32) == 1
    return jnp.where(chosen, wide(one[...]), wide(two[...])).astype(jnp.bfloat16)


def attend_kernel(count, at, info, slope_ref, x0, x1, x2, x3, own, other, bias, *refs):
    xs_out, qkvm_out, probs_out, w_out, top_ref = refs[:5]
    sends = refs[5:9]
    xs, qkvm, probs_ref, w, own_ref, other_ref, sem = refs[9:]
    columns = slice(at, at + own_ref.shape[1])
    one = start(own.at[:, columns], own_ref, sem.at[10])
    two = start(other.at[:, columns], other_ref, sem.at[11])
    blocks = (x0, x1, x2, x3)
    rows = x0.shape[0]
    total = rows * len(blocks)
    cols = own_ref.shape[1] // 2
    part, length, home = info[0], info[1], info[2]
    for b, ref in enumerate(blocks):
        xs[b * rows : (b + 1) * rows, :] = ref[...]
    copies = [start(xs, xs_out, sem.at[0])]
    height = own_ref.shape[0] // count
    one.wait()
    two.wait()
    for k in range(count):
        span = slice(k * height, (k + 1) * height)
        place = pl.ds(pl.multiple_of((info[3] ^ k) * height, height), height)
        w[place, : 2 * cols] = pick(home, own_ref[span, :], other_ref[span, :])
        w[place, 2 * cols :] = pick(home, other_ref[span, :], own_ref[span, :])
    copies.append(start(w, w_out, sem.at[9]))
    x = xs[...]
    qkvm[:, : 3 * cols] = low(dot(x, w[:, : 3 * cols]) + bias[...])
    out_w = w[:, 3 * cols :]
    key_pos = positions_of((1, total), 1, rows, part)
    key_ok = key_pos < length
    heads = cols // HEAD_DIM
    tops = [jnp.full((1, 1), NEGATIVE, jnp.float32)] * heads
    for b in range(len(blocks)):
        span = slice(b * rows, (b + 1) * rows)
        pos = ((b ^ part) * rows) + lax.broadcasted_iota(jnp.int32, (rows, 1), 0)
        distance = jnp.abs(pos - key_pos).astype(jnp.float32)
        for h in range(heads):
            lo = h * HEAD_DIM
            key = qkvm[:, cols + lo : cols + lo + HEAD_DIM]
            value = qkvm[:, 2 * cols + lo : 2 * cols + lo + HEAD_DIM]
            query = qkvm[span, lo : lo + HEAD_DIM] * jnp.bfloat16(HEAD_DIM**-0.5)
            masked = jnp.where(key_ok, contract_cols(query, key), NEGATIVE)
            block_top = jnp.max(masked, axis=1, keepdims=True)
            block_top = jnp.where(pos < length, block_top, NEGATIVE)
            tops[h] = jnp.maximum(tops[h], jnp.max(block_top, axis=0, keepdims=True))
            scores = masked - slope_ref[h] * distance
            row_max = jnp.max(scores, axis=1, keepdims=True)
            exponent = jnp.exp(scores - row_max)
            totals = jnp.sum(exponent, axis=1, keepdims=True)
            probs = low(exponent * (1.0 / totals))
            probs_ref[h, span, :] = probs
            qkvm[span, 3 * cols + lo : 3 * cols + lo + HEAD_DIM] = low(dot(probs, value))
        copies.append(
            start(probs_ref.at[:, span, :], probs_out.at[:, span, :], sem.at[1 + 2 * b])
        )
        copies.append(start(qkvm.at[span, :], qkvm_out.at[span, :], sem.at[2 + 2 * b]))
        sends[b][...] = low(contract_cols(qkvm[span, 3 * cols :], out_w))
    lane = lax.broadcasted_iota(jnp.int32, (8, 128), 1)
    packed = jnp.full((8, 128), NEGATIVE, jnp.float32)
    for h, top in enumerate(tops):
        packed = jnp.where(lane == h, top, packed)
    top_ref[...] = packed
    for copy in copies:
        copy.wait()


def attend(info, slopes, blocks, own, other, at, bias, count):
    rows, width = blocks[0].shape
    total = rows * len(blocks)
    cols = bias.shape[1] // 3
    heads = cols // HEAD_DIM
    outs = [
        ((total, width), jnp.bfloat16, "h"),
        ((total, 4 * cols), jnp.bfloat16, "h"),
        ((heads, total, total), jnp.bfloat16, "h"),
        ((width, 4 * cols), jnp.bfloat16, "h"),
        ((8, 128), jnp.float32),
    ] + [((rows, width), jnp.bfloat16)] * len(blocks)
    return call(
        functools.partial(attend_kernel, count, at),
        "attend",
        outs,
        ("s", info),
        ("s", slopes),
        *blocks,
        ("h", own),
        ("h", other),
        bias,
        scratch=[
            bf16(total, width),
            bf16(total, 4 * cols),
            bf16(heads, total, total),
            bf16(width, 4 * cols),
            bf16(width, 2 * cols),
            bf16(width, 2 * cols),
            sems(4 + 2 * len(blocks)),
        ],
        flops=16 * heads * total * total * HEAD_DIM + 8 * total * width * cols,
        exps=heads * total * total,
    )


def attend_back_kernel(g0, g1, g2, g3, w_in, qkvm_in, probs_in, *refs):
    out_ref, sum_ref, *sends = refs[-13:-7]
    w, qkvm, probs_ref, gs_ref, gm_ref, sem, sem_w = refs[-7:]
    blocks = (g0, g1, g2, g3)
    rows = g0.shape[0]
    cols = w.shape[1] // 4
    heads = cols // HEAD_DIM
    scale = HEAD_DIM**-0.5
    weights = start(w_in, w, sem_w)
    first = start(qkvm_in, qkvm, sem.at[0])
    rest = [start(probs_in.at[h], probs_ref.at[h], sem.at[1 + h]) for h in range(heads)]
    g = join(blocks)
    weights.wait()
    gm_ref[...] = low(dot(g, w[:, 3 * cols :]))
    first.wait()
    for h in range(heads):
        lo = h * HEAD_DIM
        query = qkvm[:, lo : lo + HEAD_DIM]
        key = qkvm[:, cols + lo : cols + lo + HEAD_DIM]
        value = qkvm[:, 2 * cols + lo : 2 * cols + lo + HEAD_DIM]
        rest[h].wait()
        for b in range(len(blocks)):
            span = slice(b * rows, (b + 1) * rows)
            probs = wide(probs_ref[h, span, :])
            grad_probs = contract_cols(gm_ref[span, lo : lo + HEAD_DIM], value)
            inner = jnp.sum(grad_probs * probs, axis=1, keepdims=True)
            grad_scores = low(probs * (grad_probs - inner))
            gs_ref[span, :] = grad_scores
            out_ref[span, lo : lo + HEAD_DIM] = low(dot(grad_scores, key) * scale)
        out_ref[:, cols + lo : cols + lo + HEAD_DIM] = low(
            contract_rows(gs_ref[...], query) * scale
        )
        out_ref[:, 2 * cols + lo : 2 * cols + lo + HEAD_DIM] = low(
            contract_rows(probs_ref[h], gm_ref[:, lo : lo + HEAD_DIM])
        )
    for b in range(len(blocks)):
        span = slice(b * rows, (b + 1) * rows)
        sends[b][...] = low(contract_cols(out_ref[span, :], w[:, : 3 * cols]))
    sums = jnp.sum(wide(out_ref[...]), axis=0, keepdims=True)
    sum_ref[...] = jnp.broadcast_to(sums, sum_ref.shape)


def attend_back(blocks, w, qkvm, probs, after):
    rows, width = blocks[0].shape
    total = rows * len(blocks)
    cols = w.shape[1] // 4
    heads = cols // HEAD_DIM
    outs = [
        ((total, 3 * cols), jnp.bfloat16),
        ((8, 3 * cols), jnp.float32),
    ] + [((rows, width), jnp.bfloat16)] * len(blocks)
    return call(
        attend_back_kernel,
        "attend_back",
        outs,
        *blocks,
        ("h", w),
        ("h", qkvm),
        ("h", probs),
        *[("d", a) for a in after],
        scratch=[
            bf16(*w.shape),
            bf16(total, 4 * cols),
            bf16(heads, total, total),
            bf16(total, total),
            bf16(total, cols),
            sems(1 + heads),
            pltpu.SemaphoreType.DMA,
        ],
        flops=32 * heads * total * total * HEAD_DIM + 8 * total * width * cols,
    )


def attend_weights_kernel(info, g0, g1, g2, g3, dqkv, xs_in, qkvm_in, give, keep, xs, mixed, sem):
    cols = dqkv.shape[1] // 3
    extra = mixed.shape[1] - cols
    first = start(xs_in, xs, sem.at[0])
    second = start(qkvm_in.at[:, 3 * cols - extra :], mixed, sem.at[1])
    second.wait()
    out = contract_rows(join((g0, g1, g2, g3)), mixed[:, extra:])
    first.wait()
    query_key = contract_rows(xs[...], dqkv[:, : 2 * cols])
    value = contract_rows(xs[...], dqkv[:, 2 * cols :])
    value_out = jnp.concatenate([value, out], axis=1)
    is_home = jnp.full(query_key.shape, info[2], jnp.int32) == 1
    give[...] = low(jnp.where(is_home, value_out, query_key))
    keep[...] = low(jnp.where(is_home, query_key, value_out))


def attend_weights(info, g, dqkv, xs, qkvm):
    total, width = xs.shape
    cols = qkvm.shape[1] // 4
    out = ((width, 2 * cols), jnp.bfloat16)
    return call(
        attend_weights_kernel,
        "attend_weights",
        [out, out],
        ("s", info),
        *g,
        dqkv,
        ("h", xs),
        ("h", qkvm),
        scratch=[bf16(total, width), bf16(total, -(-cols // 128) * 128), sems(2)],
        flops=8 * total * width * cols,
    )


def spread_kernel(count, place, keep, came, *refs):
    extra, outs = refs[:-count], refs[-count:]
    height = keep.shape[0] // count
    for k, out in enumerate(outs):
        to = place[0] ^ k
        span = pl.ds(pl.multiple_of(to * height, height), height)
        out[:height, :] = low(wide(keep[span, :]) + wide(came[span, :]))
        if extra:
            small, sums = extra
            cols = sums.shape[1] // 3
            row = lax.broadcasted_iota(jnp.int32, (small.shape[1], cols), 0)
            mine = jnp.full(row.shape, to, jnp.int32) == place[1]
            query = jnp.where(mine & (row == 0), sums[0:1, :cols], 0.0)
            value = jnp.where(mine & (row == 1), sums[0:1, 2 * cols :], 0.0)
            out[height:, :cols] = low(small[to][:, :cols] + query + value)
            out[height:, cols:] = low(small[to][:, cols:])


def spread(place, keep, came, count, *extra):
    added = extra[0].shape[1] if extra else 0
    out = ((keep.shape[0] // count + added, keep.shape[1]), jnp.bfloat16)
    body = functools.partial(spread_kernel, count)
    return call(body, "spread", [out] * count, ("s", place), keep, came, *extra)


def total_kernel(*refs):
    refs[-1][...] = low(summed(refs[:-1]))


def total_of(blocks):
    return call(total_kernel, "total", [(blocks[0].shape, jnp.bfloat16)], *blocks)[0]


def fetch(weights, scratch, sem, order):
    unit = scratch[0].shape[1] // 3
    cut = (slice(0, 2 * unit), slice(2 * unit, 3 * unit))
    copies = {}
    for i, (side, which) in enumerate(order):
        span = cut[which]
        copies[side, which] = start(
            weights[side].at[:, span], scratch[side].at[:, span], sem.at[i]
        )
    return copies


def feed_kernel(x_ref, own, other, part_ref, saved_out, saved, own_ref, other_ref, sem):
    unit = own_ref.shape[1] // 3
    scratch = (own_ref, other_ref)
    copies = fetch((own, other), scratch, sem, ((0, 0), (1, 0), (0, 1), (1, 1)))
    x = x_ref[...]
    width = x.shape[1]
    first = start(x_ref, saved_out.at[:, :width], sem.at[4])
    for side, w in enumerate(scratch):
        lo = side * unit
        copies[side, 0].wait()
        packed = dot(x, w[:, : 2 * unit])
        gate, up = packed[:, :unit], packed[:, unit:]
        phi = 0.5 + 0.5 * lax.erf(gate * (0.5**0.5))
        bell = jnp.exp(gate * gate * -0.5) * (2.0 * math.pi) ** -0.5
        gelu = gate * phi
        saved[:, lo : lo + unit] = low(gelu * up)
        saved[:, 2 * unit + lo : 3 * unit + lo] = low(up * (phi + gate * bell))
        saved[:, 4 * unit + lo : 5 * unit + lo] = low(gelu)
    second = start(saved, saved_out.at[:, width:], sem.at[5])
    copies[0, 1].wait()
    copies[1, 1].wait()
    part_ref[...] = low(
        contract_cols(saved[:, :unit], own_ref[:, 2 * unit :])
        + contract_cols(saved[:, unit : 2 * unit], other_ref[:, 2 * unit :])
    )
    first.wait()
    second.wait()


def feed(x, own, other, unit):
    rows, width = x.shape
    outs = [
        ((rows, width), jnp.bfloat16),
        ((rows, width + 6 * unit), jnp.bfloat16, "h"),
    ]
    return call(
        feed_kernel,
        "feed",
        outs,
        x,
        ("h", own),
        ("h", other),
        scratch=[
            bf16(rows, 6 * unit),
            bf16(width, 3 * unit),
            bf16(width, 3 * unit),
            sems(6),
        ],
        flops=12 * rows * width * unit,
        exps=4 * rows * unit,
    )


def feed_back_kernel(
    g_ref, own, other, saved_in, part_ref, packed_ref, saved, own_ref, other_ref, sem
):
    scratch = (own_ref, other_ref)
    copies = fetch((own, other), scratch, sem, ((0, 1), (1, 1)))
    g = g_ref[...]
    width = g.shape[1]
    unit = own_ref.shape[1] // 3
    copy = start(saved_in.at[:, width + 2 * unit :], saved, sem.at[4])
    cut = slice(0, 2 * unit)
    for side, w in enumerate((own, other)):
        copies[side, 0] = start(w.at[:, cut], scratch[side].at[:, cut], sem.at[2 + side])
    grads = []
    for side, w in enumerate(scratch):
        copies[side, 1].wait()
        grads.append(dot(g, w[:, 2 * unit :]))
    copy.wait()
    total = None
    for side, w in enumerate(scratch):
        lo = side * unit
        at = 2 * side * unit
        packed_ref[:, at : at + unit] = low(grads[side] * wide(saved[:, lo : lo + unit]))
        packed_ref[:, at + unit : at + 2 * unit] = low(
            grads[side] * wide(saved[:, 2 * unit + lo : 3 * unit + lo])
        )
        copies[side, 0].wait()
        term = contract_cols(packed_ref[:, at : at + 2 * unit], w[:, : 2 * unit])
        total = term if total is None else total + term
    part_ref[...] = low(total)


def feed_back(g, own, other, saved, unit):
    rows, width = g.shape
    outs = [((rows, width), jnp.bfloat16), ((rows, 4 * unit), jnp.bfloat16)]
    return call(
        feed_back_kernel,
        "feed_back",
        outs,
        g,
        ("h", own),
        ("h", other),
        ("h", saved),
        scratch=[
            bf16(rows, 4 * unit),
            bf16(width, 3 * unit),
            bf16(width, 3 * unit),
            sems(5),
        ],
        flops=12 * rows * width * unit,
    )


def feed_weights_kernel(side, *refs):
    saved_in, g, packed = refs[:4], refs[4:8], refs[8:12]
    out, xs, act, sem = refs[-4:]
    rows, width = g[0].shape
    unit = act.shape[1]
    at = width + side * unit
    copies = []
    for b, ref in enumerate(saved_in):
        span = slice(b * rows, (b + 1) * rows)
        copies.append(start(ref.at[:, at : at + unit], act.at[span, :], sem.at[2 * b]))
        copies.append(start(ref.at[:, :width], xs.at[span, :], sem.at[2 * b + 1]))
    g_all = join(g)
    lo = 2 * side * unit
    packed_all = jnp.concatenate([p[:, lo : lo + 2 * unit] for p in packed], axis=0)
    for copy in copies[0::2]:
        copy.wait()
    out[:, 2 * unit :] = low(contract_rows(g_all, act[...]))
    for copy in copies[1::2]:
        copy.wait()
    out[:, : 2 * unit] = low(contract_rows(xs[...], packed_all))


def feed_weights(side, saved, g, packed):
    rows, width = g[0].shape
    unit = packed[0].shape[1] // 4
    return call(
        functools.partial(feed_weights_kernel, side),
        "feed_weights",
        [((width, 3 * unit), jnp.bfloat16)],
        *[("h", x) for x in saved],
        *g,
        *packed,
        scratch=[bf16(4 * rows, width), bf16(4 * rows, unit), sems(8)],
        flops=24 * rows * width * unit,
    )[0]


def small_kernel(place, *refs):
    *given, out = refs
    layers = len(given) // 4
    groups, count, both = out.shape
    cols = both // 2
    row = lax.broadcasted_iota(jnp.int32, (count, cols), 0)
    lane = lax.broadcasted_iota(jnp.int32, (count, cols), 1)
    heads = cols // HEAD_DIM
    high = jnp.zeros((count, cols), jnp.float32)
    for l in range(layers):
        top = given[4 * l + 3]
        for h in range(heads):
            at = (place[0] * layers + l) * heads + h
            high = jnp.where(lane == at, top[0:1, h : h + 1], high)
    whole = wide(low(high))
    tops = jnp.where(row == 0, whole, jnp.where(row == 1, high - whole, 0.0))
    for g in range(groups):
        span = slice(g * cols, (g + 1) * cols)
        mine = jnp.full((1, cols), place[1], jnp.int32) == g
        values = jnp.zeros((count, cols), jnp.float32)
        for l in range(layers):
            one, two, sums = given[4 * l : 4 * l + 3]
            rows = [
                one[2:3, span],
                two[2:3, span],
                one[1:2, span],
                two[1:2, span],
                one[0:1, span],
                two[0:1, span],
            ]
            if l > 0:
                query = jnp.where(mine, sums[0:1, :cols], 0.0)
                rows = [query, jnp.where(mine, sums[0:1, 2 * cols :], 0.0)] + rows
            for i, value in enumerate(reversed(rows)):
                values = jnp.where(row == 8 * l + 7 - i, value, values)
        out[g, :, :cols] = values
        out[g, :, cols:] = tops


def small_rows(place, groups, given, cols):
    shape = (groups, 2 * len(given), 2 * cols)
    return call(small_kernel, "small", [(shape, jnp.float32)], ("s", place), *given)[0]


def finish_feed_kernel(l, place, *refs):
    glu_out, down_out, token, glu, down, sem = refs[-6:]
    parts, _, unit = down.shape
    token[...] = jnp.zeros_like(token)
    near = refs[:parts] if len(refs[0].shape) == 2 else [refs[0].at[k] for k in range(parts)]
    copies = []
    for k, block in enumerate(near):
        span = pl.ds(pl.multiple_of((place[1] ^ k) * unit, 128), unit)
        glu[k, :, 0, :] = wide(block[:, :unit])
        glu[k, :, 1, :] = wide(block[:, unit : 2 * unit])
        copies.append(start(glu.at[k], glu_out.at[l, :, :, span], sem.at[2 * k]))
        down[k] = wide(block[:, 2 * unit :])
        copies.append(start(down.at[k], down_out.at[l, :, span], sem.at[2 * k + 1]))
    for copy in copies:
        copy.wait()


def finish_feed(l, layers, place, near, parts, before):
    rows, width = near[0].shape[-2:]
    unit = width // 3
    outs = [
        ((layers, rows, 2, unit * parts), jnp.float32, "h"),
        ((layers, rows, unit * parts), jnp.float32, "h"),
        ((8, 128), jnp.float32),
    ]
    given = [("s", place), *near]
    alias = {}
    if before is not None:
        alias = {len(given): 0, len(given) + 1: 1}
        given += [("h", x) for x in before]
    return call(
        functools.partial(finish_feed_kernel, l),
        "finish_feed",
        outs,
        *given,
        scratch=[
            pltpu.VMEM((parts, rows, 2, unit), jnp.float32),
            pltpu.VMEM((parts, rows, unit), jnp.float32),
            sems(2 * parts),
        ],
        alias=alias,
    )


def choose_kernel(flags, *refs):
    *blocks, out = refs
    parts = len(blocks)
    pair = parts // 2
    height, _ = blocks[0].shape
    count = (out.shape[0] - pair * height) // parts
    home = jnp.full(blocks[0].shape, flags[0], jnp.int32) == 1
    for i in range(pair):
        out[i * height : (i + 1) * height, :] = low(
            jnp.where(home, wide(blocks[pair + i][...]), wide(blocks[i][...]))
        )
    for k, block in enumerate(blocks):
        at = pair * height + k * count
        out[at : at + count, :] = block[height - count :, :]


def choose(flags, blocks, count):
    parts = len(blocks)
    height, width = blocks[0].shape
    shape = (parts // 2 * height + parts * count, width)
    return call(choose_kernel, "choose", [(shape, jnp.bfloat16)], ("s", flags), *blocks)[0]


def finish_attention_kernel(groups, count, flags, *refs):
    qkv_out, out_out, clip_out, small_out, weights, qkv, out, clip, sem = refs[-9:]
    *blocks, came, weight_in = refs[:-9]
    parts = len(blocks)
    pair = parts // 2
    height, _ = blocks[0].shape
    layers, _, rows, half = qkv.shape
    cols = half // 2
    heads = cols // HEAD_DIM
    fetched = [start(weight_in.at[l, :2], weights.at[l], sem.at[l]) for l in range(layers)]
    total, tops = None, []
    for k, block in enumerate(blocks):
        at = pair * height + k * count
        mine, theirs = wide(block[height - count :, :]), wide(came[at : at + count, :])
        both = mine[:, :cols] + theirs[:, :cols]
        total = both if total is None else total + both
        tops.append(
            jnp.maximum(
                mine[0:1, cols:] + mine[1:2, cols:], theirs[0:1, cols:] + theirs[1:2, cols:]
            )
        )
    small_out[...] = total
    home = jnp.full((rows, half), flags[0], jnp.int32) == 1
    even = jnp.full((rows, half), flags[1], jnp.int32) == 1
    home_row, even_row = home[0:1, :cols], even[0:1, :cols]
    pick_tops = [jnp.where(home_row, tops[i], tops[pair + i]) for i in range(pair)]
    first_top = jnp.where(even_row, pick_tops[0], pick_tops[1])
    second_top = jnp.where(even_row, pick_tops[1], pick_tops[0])
    lane = lax.broadcasted_iota(jnp.int32, (1, half), 1) // HEAD_DIM
    copies = []
    for l in range(layers):
        span = slice(l * rows, (l + 1) * rows)
        near = [wide(b[span, :]) for b in blocks]
        far = [wide(came[i * height + l * rows : i * height + (l + 1) * rows, :]) for i in range(pair)]
        near = [jnp.where(home, near[i], near[pair + i]) for i in range(pair)]
        query_key = [jnp.where(even, near[0], near[1]), jnp.where(even, near[1], near[0])]
        value_out = [jnp.where(even, far[0], far[1]), jnp.where(even, far[1], far[0])]
        for i in range(pair):
            place = slice(i * cols, (i + 1) * cols)
            qkv[l, 0, :, place] = query_key[i][:, :cols]
            qkv[l, 1, :, place] = query_key[i][:, cols:]
            qkv[l, 2, :, place] = value_out[i][:, :cols]
            out[l, :, place] = value_out[i][:, cols:]
        copies.append(start(qkv.at[l], qkv_out.at[l], sem.at[layers + 3 * l]))
        copies.append(start(out.at[l], out_out.at[l], sem.at[layers + 3 * l + 1]))
        top = jnp.zeros((1, half), jnp.float32)
        for i, row in enumerate((first_top, second_top)):
            for h in range(heads):
                best = None
                for g in range(groups):
                    at = (g * layers + l) * heads + h
                    value = row[:, at : at + 1]
                    best = value if best is None else jnp.maximum(best, value)
                top = jnp.where(lane == i * heads + h, best, top)
        factor = CLIP_LIMIT / jnp.maximum(top, CLIP_LIMIT)
        fetched[l].wait()
        for m in range(2):
            clip[l, :, m, :] = (wide(weights[l, m]) - STEP_SIZE * qkv[l, m]) * factor
        copies.append(start(clip.at[l], clip_out.at[l], sem.at[layers + 3 * l + 2]))
    for copy in copies:
        copy.wait()


def finish_attention(groups, count, flags, blocks, came, weight):
    layers, _, rows, half = weight.shape
    outs = [
        ((layers, 3, rows, half), jnp.float32, "h"),
        ((layers, rows, half), jnp.float32, "h"),
        ((layers, rows, 2, half), jnp.float32, "h"),
        ((count, half // 2), jnp.float32),
    ]
    return call(
        functools.partial(finish_attention_kernel, groups, count),
        "finish_attention",
        outs,
        ("s", flags),
        *blocks,
        came,
        ("h", weight),
        scratch=[
            pltpu.VMEM((layers, 2, rows, half), weight.dtype),
            f32(layers, 3, rows, half),
            f32(layers, rows, half),
            f32(layers, rows, 2, half),
            sems(4 * layers),
        ],
    )


def both_kernel(core, own, other, out):
    out[core[0]] = own[...]
    out[1 - core[0]] = other[...]


def both_slots(core, own, other):
    out = ((2, *own.shape), own.dtype)
    return call(both_kernel, "both", [out], ("s", core), own, other)[0]


def normalised(z):
    mean = jnp.mean(z, axis=1, keepdims=True)
    centred = z - mean
    r = lax.rsqrt(jnp.mean(centred * centred, axis=1, keepdims=True) + EPSILON)
    return centred * r, r


def affine(n, vec, gain, shift):
    return n * vec[gain : gain + 1, :] + vec[shift : shift + 1, :]


def summed(refs):
    total = wide(refs[0][...])
    for ref in refs[1:]:
        total = total + wide(ref[...])
    return total


def norm_input(before, bias, parts, prev_in, prev, sem, vec_in, vec):
    copy = start(prev_in, prev, sem.at[0])
    other = start(vec_in, vec, sem.at[2])
    z = summed(parts)
    other.wait()
    z = z + vec[bias : bias + 1, :]
    copy.wait()
    if before is None:
        return z + wide(prev[...])
    return z + affine(normalised(prev[...])[0], vec, *before)


def norm_kernel(
    before, rows_of, p0, p1, p2, p3, prev_in, vec_in, low_ref, z_out, prev, zs, vec, sem
):
    bias, gain, shift = rows_of
    z = norm_input(before, bias, (p0, p1, p2, p3), prev_in, prev, sem, vec_in, vec)
    zs[...] = z
    copy = start(zs, z_out, sem.at[1])
    low_ref[...] = low(affine(normalised(z)[0], vec, gain, shift))
    copy.wait()


def norm(before, rows_of, parts, prev, vec):
    shape = parts[0].shape
    outs = [(shape, jnp.bfloat16), (shape, jnp.float32, "h")]
    return call(
        functools.partial(norm_kernel, before, rows_of),
        "norm",
        outs,
        *parts,
        ("h", prev),
        ("h", vec),
        scratch=[pltpu.VMEM(shape, prev.dtype), f32(*shape), f32(*vec.shape), sems(3)],
        flops=prev.size,
    )


def norm_grad(grad, n, r, gain, dz_out, low_ref, stat_ref, dzs, sem):
    scaled = grad * gain
    one = jnp.mean(scaled, axis=1, keepdims=True)
    two = jnp.mean(scaled * n, axis=1, keepdims=True)
    dz = (scaled - one - n * two) * r
    dz_low = low(dz)
    dzs[...] = dz
    copy = start(dzs, dz_out, sem)
    low_ref[...] = dz_low
    stat_ref[0:1, :] = jnp.sum(grad * n, axis=0, keepdims=True)
    stat_ref[1:2, :] = jnp.sum(grad, axis=0, keepdims=True)
    stat_ref[2:3, :] = jnp.sum(wide(dz_low), axis=0, keepdims=True)
    stat_ref[3:, :] = jnp.zeros((stat_ref.shape[0] - 3, stat_ref.shape[1]), jnp.float32)
    copy.wait()


def norm_back_kernel(gain_row, p0, p1, p2, p3, skip_in, z_in, vec_in, *refs):
    outs, (skip, zs, dzs, vec, sem) = refs[-8:-5], refs[-5:]
    one = start(z_in, zs, sem.at[0])
    two = start(skip_in, skip, sem.at[1])
    three = start(vec_in, vec, sem.at[3])
    grad = summed((p0, p1, p2, p3))
    one.wait()
    n, r = normalised(zs[...])
    two.wait()
    three.wait()
    gain = vec[gain_row : gain_row + 1, :]
    norm_grad(grad + skip[...], n, r, gain, *outs, dzs, sem.at[2])


def grad_outs(shape):
    return [
        (shape, jnp.float32, "h"),
        (shape, jnp.bfloat16),
        ((8, shape[1]), jnp.float32),
    ]


def norm_back(gain_row, parts, skip, z, vec, after):
    shape = skip.shape
    return call(
        functools.partial(norm_back_kernel, gain_row),
        "norm_back",
        grad_outs(shape),
        *parts,
        ("h", skip),
        ("h", z),
        ("h", vec),
        *[("d", a) for a in after],
        scratch=[f32(*shape), f32(*shape), f32(*shape), f32(*vec.shape), sems(4)],
        flops=skip.size,
    )


def turn_kernel(before, rows_of, info, p0, p1, p2, p3, prev_in, vec_in, cot, out_ref, *refs):
    outs, (prev, dzs, vec, sem) = refs[:3], refs[3:]
    bias, gain, shift = rows_of
    z = norm_input(before, bias, (p0, p1, p2, p3), prev_in, prev, sem, vec_in, vec)
    n, r = normalised(z)
    rows = z.shape[0]
    ok = info[0] * rows + lax.broadcasted_iota(jnp.int32, (rows, 1), 0) < info[1]
    out_ref[...] = low(jnp.where(ok, affine(n, vec, gain, shift), 0.0))
    grad = jnp.where(ok, wide(cot[...]), 0.0)
    norm_grad(grad, n, r, vec[gain : gain + 1, :], *outs, dzs, sem.at[1])


def turn(before, rows_of, info, parts, prev, vec, cot):
    shape = prev.shape
    outs = [(shape, jnp.bfloat16)] + grad_outs(shape)
    return call(
        functools.partial(turn_kernel, before, rows_of),
        "turn",
        outs,
        ("s", info),
        *parts,
        ("h", prev),
        ("h", vec),
        cot,
        scratch=[f32(*shape), f32(*shape), f32(*vec.shape), sems(3)],
        flops=prev.size,
    )


def shards(
    tokens,
    cotangent,
    lengths,
    dealing,
    qkv_weight,
    out_weight,
    glu_weight,
    down_weight,
    biases,
    gains,
):
    slots, rows, width = tokens.shape
    layers = qkv_weight.shape[0]
    parts = lax.axis_size("ctx")
    cores = lax.axis_size("heads")
    groups = lax.axis_size("dp")
    part = lax.axis_index("ctx")
    core = lax.axis_index("heads")
    group = lax.axis_index("dp")
    local_rows = qkv_weight.shape[1]
    half = qkv_weight.shape[3]
    cols = half * cores // parts
    local_heads = cols // HEAD_DIM
    quarter = glu_weight.shape[3] // parts
    per_core = parts // cores
    home = part // per_core == core
    offset = (part % per_core) * cols

    def swap(x):
        return lax.ppermute(x, "heads", [(j, cores - 1 - j) for j in range(cores)])

    def hop(x, k):
        return lax.ppermute(x, "ctx", [(j, j ^ k) for j in range(parts)])

    def hops(blocks):
        return [blocks[0]] + [hop(blocks[k], k) for k in range(1, parts)]

    def own_first(work, blocks, extras):
        done = [work(blocks[0], extras[0])]
        for block, extra in zip(blocks[1:], extras[1:]):
            block, _ = lax.optimization_barrier((block, done[0][0]))
            done.append(work(block, extra))
        return zip(*done)

    def gather(x):
        return hops([x] * parts)

    def tie(x, *others):
        return lax.optimization_barrier((x, *others))[0]

    value_out = jnp.concatenate(
        [
            lax.dynamic_slice_in_dim(qkv_weight[:, :, 2, :], offset, cols, 2),
            lax.dynamic_slice_in_dim(out_weight, offset, cols, 2),
        ],
        axis=2,
    )
    query_key = jnp.concatenate(
        [
            lax.dynamic_slice_in_dim(qkv_weight[:, :, 0, :], offset, cols, 2),
            lax.dynamic_slice_in_dim(qkv_weight[:, :, 1, :], offset, cols, 2),
        ],
        axis=2,
    )
    attn_shard = jnp.where(home, query_key, swap(value_out))
    attn_first, attn_shard_later = attn_shard[0], [attn_shard[l] for l in range(1, layers)]
    glu_part = lax.dynamic_slice_in_dim(glu_weight, part * quarter, quarter, 3)
    down_part = lax.dynamic_slice_in_dim(down_weight, part * quarter, quarter, 2)

    def over_dp(x):
        return lax.all_gather(x, "dp", axis=0, tiled=True)

    direct = groups <= 4 and local_rows == cols
    place = jnp.stack([group, part]).astype(jnp.int32)

    def hop_dp(x, k):
        return lax.ppermute(x, "dp", [(j, j ^ k) for j in range(groups)])

    feed_full = [None] * layers
    attn_full = [None] * layers
    tokens_own = lax.dynamic_index_in_dim(tokens, core, 0, keepdims=False)
    feed_shard = [
        jnp.concatenate([glu_part[l, :, 0], glu_part[l, :, 1], down_part[l]], axis=1)
        for l in range(layers)
    ]
    early = over_dp(jnp.concatenate([feed_shard[0]] + attn_shard_later, axis=1))
    if direct:
        own = jnp.concatenate([attn_first] + [hop_dp(attn_first, k) for k in range(1, groups)])
    else:
        own = over_dp(attn_first)
    low_zero = gather(tokens_own)
    attn_full[0] = (own, swap(own), 0)
    late = [over_dp(lax.optimization_barrier((x, own))[0]) for x in feed_shard[1:]]

    slot = group * slots + core
    slot_ids = jnp.arange(lengths.shape[0], dtype=jnp.int32)
    sequence = jnp.sum(jnp.where(slot_ids == slot, dealing, 0))
    length = jnp.sum(jnp.where(slot_ids == sequence, lengths, 0))
    info = [
        jnp.stack([part, length, home, group if direct and l == 0 else jnp.int32(0)]).astype(
            jnp.int32
        )
        for l in range(layers)
    ]
    slopes = lax.dynamic_slice_in_dim(
        jnp.array(alibi_slopes(HEADS), jnp.float32), part * local_heads, local_heads
    )
    vec = jnp.concatenate([biases, gains], axis=1).reshape(layers * 8, width)
    qv = lax.dynamic_slice_in_dim(biases[:, :2], part * cols, cols, 2)
    qkv_bias = jnp.concatenate([qv[:, :1], jnp.zeros_like(qv[:, :1]), qv[:, 1:]], axis=2)

    prev, before = tokens_own, None
    low_own = tokens_own
    saved = []
    tops = []
    for l in range(layers):
        v = 8 * l
        x_low = low_zero if l == 0 else gather(low_own)
        xs, qkvm, probs, attn_w, top, *sends = attend(
            info[l],
            slopes,
            x_low,
            *attn_full[l],
            qkv_bias[l],
            groups if direct and l == 0 else 1,
        )
        tops.append(top)
        hidden_low, z_one = norm(before, (v + 2, v + 6, v + 4), hops(sends), prev, vec)
        feed_own = tie(early if l == 0 else late[l - 1], hidden_low if l == 0 else top)
        feed_full[l] = (feed_own, swap(feed_own))
        if l == 0:
            for n in range(1, layers):
                attn_full[n] = (*feed_full[0], 3 * quarter + 2 * cols * (n - 1))
        h_low = gather(hidden_low)
        sends, kept = own_first(lambda h, _: feed(h, *feed_full[l], quarter), h_low, h_low)
        arrived = hops(sends)
        rows_of = (v + 3, v + 7, v + 5)
        if l + 1 < layers:
            low_own, z_two = norm((v + 6, v + 4), rows_of, arrived, z_one, vec)
            prev, before = z_two, (v + 7, v + 5)
        else:
            cot = lax.dynamic_index_in_dim(cotangent, core, 0, keepdims=False)
            outputs, grad_two, low_two, stats_two = turn(
                (v + 6, v + 4), rows_of, info[l], arrived, z_one, vec, cot
            )
            z_two = None
        saved.append((xs, qkvm, probs, attn_w, z_one, kept, z_two))

    feed_parts = [None] * layers
    attn_parts = [None] * layers
    carried = None
    woven = [None] * layers
    def over_dp_sum(x):
        return lax.psum_scatter(x, "dp", scatter_dimension=0, tiled=True)

    stats = [[None] * 3 for _ in range(layers)]
    for l in reversed(range(layers)):
        v = 8 * l
        x_low, qkvm, probs, attn_w, z_one, kept, _ = saved[l]
        above = l + 1 < layers
        stats[l][1] = stats_two
        g_low = gather(low_two)
        sends, packed = own_first(
            lambda g, k: feed_back(g, *feed_full[l], k, quarter), g_low, kept
        )
        arrived = hops(sends)
        packed = list(packed)
        packed[0], arrived[3] = lax.optimization_barrier((packed[0], arrived[3]))
        give = feed_weights(1, kept, g_low, packed)
        packed[0], arrived[2], give = lax.optimization_barrier((packed[0], arrived[2], give))
        keep = feed_weights(0, kept, g_low, packed)
        total = wide(keep) + wide(swap(give))
        if above:
            total = jnp.concatenate([total, carried], axis=1)
        total = low(total)
        arrived[0] = tie(arrived[0], total)
        if above:
            arrived[0], feed_parts[l + 1] = lax.optimization_barrier(
                (arrived[0], feed_parts[l + 1])
            )
        grad_one, low_one, stats[l][0] = norm_back(v + 6, arrived, grad_two, z_one, vec, [])
        feed_parts[l] = over_dp_sum(total)
        if above:
            attn_parts[l + 1] = feed_parts[l][:, 3 * quarter :]
            feed_parts[l] = feed_parts[l][:, : 3 * quarter]
        a_low = gather(low_one)
        if above:
            near = tie(feed_parts[l + 1], *a_low)
            near = [near] + [hop(near, k) for k in (1, 2)]
        dqkv, sums, *sends = attend_back(a_low, attn_w, qkvm, probs, [])
        if above:
            tied = lax.optimization_barrier((*sends, *near))
            sends, woven[l + 1] = list(tied[:parts]), list(tied[parts:])
            woven[l + 1] += [hop(woven[l + 1][0], k) for k in range(3, parts)]
        stats[l][2] = sums
        arrived = hops(sends)
        give, keep = attend_weights(info[l], a_low, dqkv, x_low, qkvm)
        came = swap(give)
        if l > 0:
            arrived[0] = tie(arrived[0], keep)
            carried = wide(keep) + wide(came)
            grad_two, low_two, stats_two = norm_back(
                v - 8 + 7, arrived, grad_one, saved[l - 1][6], vec, []
            )

    count = layers * local_heads
    if direct:
        given = []
        for l in range(layers):
            given += [stats[l][0], stats[l][1], stats[l][2] if l else stats[l][0], tops[l]]
        small = small_rows(place, groups, given, cols)
        terms = list(spread(place, keep, came, groups, small, sums))
        terms[1:] = [hop_dp(terms[k], k) for k in range(1, groups)]
        last = total_of(terms)
        near = [x for l in range(1, layers) for x in woven[l]]
        tied = lax.optimization_barrier((*arrived, *near, *terms))
        arrived, near = list(tied[:parts]), list(tied[parts : parts + len(near)])
        last = tie(last, *arrived, *near)
        for l in range(1, layers):
            woven[l] = near[(l - 1) * parts : l * parts]
        grad = grad_one + sum(wide(a) for a in arrived)
    else:
        grad = grad_one + sum(wide(a) for a in arrived)
        empty = jnp.zeros((width,), jnp.float32)
        small = []
        for l in range(layers):
            one, two, sums = stats[l]
            small += [
                lax.dynamic_update_slice_in_dim(empty, sums[0, lo : lo + cols], part * cols, 0)
                for lo in (0, 2 * cols)
            ]
            small += [one[2], two[2], one[1], two[1], one[0], two[0]]
        small = jnp.stack(small).reshape(layers * 8, groups, local_rows).transpose(1, 0, 2)
        small = jnp.pad(small, ((0, 0), (0, 0), (0, cols - local_rows)))
        own_tops = jnp.stack([t[0, :local_heads] for t in tops]).reshape(-1)
        high = wide(low(own_tops))
        pair = jnp.stack([high, own_tops - high])
        slots_of = jnp.zeros((layers * 8, cols), jnp.float32)
        slots_of = lax.dynamic_update_slice(slots_of, pair, (0, group * count))
        slots_of = jnp.broadcast_to(slots_of[None], (groups,) + slots_of.shape)
        small = jnp.concatenate([small, slots_of], axis=2)
        total = wide(keep) + wide(came)
        payload = jnp.concatenate([total.reshape(groups, local_rows, 2 * cols), small], axis=1)
        last = lax.psum_scatter(low(payload), "dp", scatter_dimension=0, tiled=False)
    core_ref = core.astype(jnp.int32)[None]
    out_tokens = both_slots(core_ref, outputs, swap(outputs))
    grad_tokens = both_slots(core_ref, grad, swap(grad))
    result = None
    for l in reversed(range(1, layers)):
        *result, _ = finish_feed(l, layers, place, woven[l], parts, result)
    flags = jnp.stack([home, part % per_core == 0]).astype(jnp.int32)
    small_count = layers * 8
    stacked = [last[:local_rows]] + attn_parts[1:] + [last[local_rows:]]
    shared = gather(jnp.concatenate(stacked))
    near = gather(tie(feed_parts[0], shared[0]))
    tied = lax.optimization_barrier((*shared, *near))
    shared, near = list(tied[:parts]), list(tied[parts:])
    given = choose(flags, shared, small_count)
    arrived = swap(given)

    grad_qkv, grad_out, clipped_qk, small_sum = finish_attention(
        groups, small_count, flags, shared, arrived, qkv_weight.transpose(0, 2, 1, 3)
    )
    small_sum = small_sum[:, :local_rows].reshape(layers, 8, local_rows)
    grad_glu, grad_down, _ = finish_feed(0, layers, place, near, parts, result)
    return (
        out_tokens,
        grad_tokens,
        grad_qkv.transpose(0, 2, 1, 3),
        grad_out,
        grad_glu,
        grad_down,
        small_sum[:, :6],
        small_sum[:, 6:],
        clipped_qk,
    )


def solution(mesh):
    in_specs = (
        P("dp", "ctx", None),
        P("dp", "ctx", None),
        P(),
        P(),
        P(None, "dp", None, "heads"),
        P(None, "dp", "heads"),
        P(None, "dp", None, "heads"),
        P(None, "dp", "heads"),
        P(),
        P(),
    )
    out_specs = (
        P("dp", "ctx", None),
        P("dp", "ctx", None),
        P(None, "dp", None, "heads"),
        P(None, "dp", "heads"),
        P(None, "dp", None, "heads"),
        P(None, "dp", "heads"),
        P(None, None, "dp"),
        P(None, None, "dp"),
        P(None, "dp", None, "heads"),
    )
    return jax.shard_map(shards, mesh=mesh, in_specs=in_specs, out_specs=out_specs, check_vma=False)
```

```python
import functools
import math

import jax
import jax.numpy as jnp
from jax import lax
from jax.experimental import pallas as pl
from jax.experimental.pallas import tpu as pltpu
from jax.sharding import PartitionSpec as P

HEADS = 12
HEAD_DIM = 64


EPSILON = 1e-12
NEGATIVE = -1e30
CLIP_LIMIT = 4.0
STEP_SIZE = 0.0008
MIB = 1024 * 1024


def power_slopes(head_count):
    first_slope = 2.0 ** (-8.0 / head_count)
    return [first_slope ** (position + 1) for position in range(head_count)]


def alibi_slopes(head_count):
    closest = 2 ** int(math.floor(math.log2(head_count)))
    slopes = power_slopes(closest)
    slopes = slopes + power_slopes(2 * closest)[0::2][: head_count - closest]
    return slopes


def dot(a, b):
    return jnp.dot(a, b, preferred_element_type=jnp.float32)


def contract_rows(former, latter):
    return lax.dot_general(
        former, latter, (((0,), (0,)), ((), ())), preferred_element_type=jnp.float32
    )


def contract_cols(former, latter):
    return lax.dot_general(
        former, latter, (((1,), (1,)), ((), ())), preferred_element_type=jnp.float32
    )


def low(x):
    return x.astype(jnp.bfloat16)


def wide(x):
    return x.astype(jnp.float32)


def positions_of(shape, axis, rows, part):
    index = lax.broadcasted_iota(jnp.int32, shape, axis)
    shift = rows.bit_length() - 1
    return (((index >> shift) ^ part) << shift) | (index & (rows - 1))


def join(refs):
    return jnp.concatenate([r[...] for r in refs], axis=0)


def call(body, name, outs, *args, scratch=(), flops=0, exps=0, limit=16, alias=None):
    spaces = {"s": pltpu.SMEM, "h": pltpu.HBM, "d": pl.ANY, "v": pltpu.VMEM}
    args = [a if isinstance(a, tuple) else ("v", a) for a in args]
    outs = [o if len(o) == 3 else (*o, "v") for o in outs]
    values = [
        pltpu.with_memory_space_constraint(a[1], pltpu.HBM) if a[0] == "h" else a[1] for a in args
    ]
    shapes = tuple(
        pltpu.HBM(o[0], o[1]) if o[2] == "h" else jax.ShapeDtypeStruct(o[0], o[1]) for o in outs
    )
    moved = sum(v.size * v.dtype.itemsize for v in values)
    moved += sum(math.prod(o[0]) * jnp.dtype(o[1]).itemsize for o in outs)
    return pl.pallas_call(
        body,
        out_shape=shapes,
        in_specs=[pl.BlockSpec(memory_space=spaces[a[0]]) for a in args],
        out_specs=tuple(pl.BlockSpec(memory_space=spaces[o[2]]) for o in outs),
        scratch_shapes=list(scratch),
        input_output_aliases=alias or {},
        compiler_params=pltpu.CompilerParams(vmem_limit_bytes=limit * MIB),
        cost_estimate=pl.CostEstimate(flops=flops, bytes_accessed=moved, transcendentals=exps),
        name=name,
    )(*values)


def start(source, target, sem):
    copy = pltpu.make_async_copy(source, target, sem)
    copy.start()
    return copy


def bf16(*shape):
    return pltpu.VMEM(shape, jnp.bfloat16)


def f32(*shape):
    return pltpu.VMEM(shape, jnp.float32)


def sems(count):
    return pltpu.SemaphoreType.DMA((count,))


def pick(flag, one, two):
    chosen = jnp.full(one.shape, flag, jnp.int32) == 1
    return jnp.where(chosen, wide(one[...]), wide(two[...])).astype(jnp.bfloat16)


def stage_kernel(*refs):
    *refs, sem = refs
    count = len(refs) // 2
    copies = []
    for i, (source, target) in enumerate(zip(refs[:count], refs[count:])):
        if source.shape != target.shape:
            source = source.at[:, : target.shape[1]]
        copies.append(start(source, target, sem.at[i]))
    for copy in copies:
        copy.wait()


def stage(arrays, columns=None):
    outs = [
        ((a.shape[0], columns) if columns and a.shape[0] > columns // 2 else a.shape, a.dtype)
        for a in arrays
    ]
    return call(
        stage_kernel, "stage", outs, *[("h", a) for a in arrays], scratch=[sems(len(arrays))], limit=4
    )


def attend_kernel(count, at, info, slope_ref, x0, x1, x2, x3, own, other, bias, *refs):
    xs_out, qkvm_out, probs_out, w_out, top_ref = refs[:5]
    sends = refs[5:9]
    xs, qkvm, probs_ref, w, own_ref, other_ref, sem = refs[9:]
    columns = slice(at, at + own_ref.shape[1])
    one = start(own.at[:, columns], own_ref, sem.at[10])
    two = start(other.at[:, columns], other_ref, sem.at[11])
    blocks = (x0, x1, x2, x3)
    rows = x0.shape[0]
    total = rows * len(blocks)
    cols = own_ref.shape[1] // 2
    part, length, home = info[0], info[1], info[2]
    for b, ref in enumerate(blocks):
        xs[b * rows : (b + 1) * rows, :] = ref[...]
    copies = [start(xs, xs_out, sem.at[0])]
    height = own_ref.shape[0] // count
    one.wait()
    two.wait()
    for k in range(count):
        span = slice(k * height, (k + 1) * height)
        place = pl.ds(pl.multiple_of((info[3] ^ k) * height, height), height)
        w[place, : 2 * cols] = pick(home, own_ref[span, :], other_ref[span, :])
        w[place, 2 * cols :] = pick(home, other_ref[span, :], own_ref[span, :])
    copies.append(start(w, w_out, sem.at[9]))
    x = xs[...]
    qkvm[:, : 3 * cols] = low(dot(x, w[:, : 3 * cols]) + bias[...])
    out_w = w[:, 3 * cols :]
    key_pos = positions_of((1, total), 1, rows, part)
    key_ok = key_pos < length
    heads = cols // HEAD_DIM
    tops = [jnp.full((1, 1), NEGATIVE, jnp.float32)] * heads
    for b in range(len(blocks)):
        span = slice(b * rows, (b + 1) * rows)
        pos = ((b ^ part) * rows) + lax.broadcasted_iota(jnp.int32, (rows, 1), 0)
        distance = jnp.abs(pos - key_pos).astype(jnp.float32)
        for h in range(heads):
            lo = h * HEAD_DIM
            key = qkvm[:, cols + lo : cols + lo + HEAD_DIM]
            value = qkvm[:, 2 * cols + lo : 2 * cols + lo + HEAD_DIM]
            query = qkvm[span, lo : lo + HEAD_DIM] * jnp.bfloat16(HEAD_DIM**-0.5)
            masked = jnp.where(key_ok, contract_cols(query, key), NEGATIVE)
            block_top = jnp.max(masked, axis=1, keepdims=True)
            block_top = jnp.where(pos < length, block_top, NEGATIVE)
            tops[h] = jnp.maximum(tops[h], jnp.max(block_top, axis=0, keepdims=True))
            scores = masked - slope_ref[h] * distance
            row_max = jnp.max(scores, axis=1, keepdims=True)
            exponent = jnp.exp(scores - row_max)
            totals = jnp.sum(exponent, axis=1, keepdims=True)
            probs = low(exponent * (1.0 / totals))
            probs_ref[h, span, :] = probs
            qkvm[span, 3 * cols + lo : 3 * cols + lo + HEAD_DIM] = low(dot(probs, value))
        copies.append(
            start(probs_ref.at[:, span, :], probs_out.at[:, span, :], sem.at[1 + 2 * b])
        )
        copies.append(start(qkvm.at[span, :], qkvm_out.at[span, :], sem.at[2 + 2 * b]))
        sends[b][...] = low(contract_cols(qkvm[span, 3 * cols :], out_w))
    lane = lax.broadcasted_iota(jnp.int32, (8, 128), 1)
    packed = jnp.full((8, 128), NEGATIVE, jnp.float32)
    for h, top in enumerate(tops):
        packed = jnp.where(lane == h, top, packed)
    top_ref[...] = packed
    for copy in copies:
        copy.wait()


def attend(info, slopes, blocks, own, other, at, bias, count):
    rows, width = blocks[0].shape
    total = rows * len(blocks)
    cols = bias.shape[1] // 3
    heads = cols // HEAD_DIM
    outs = [
        ((total, width), jnp.bfloat16, "h"),
        ((total, 4 * cols), jnp.bfloat16, "h"),
        ((heads, total, total), jnp.bfloat16, "h"),
        ((width, 4 * cols), jnp.bfloat16, "h"),
        ((8, 128), jnp.float32),
    ] + [((rows, width), jnp.bfloat16)] * len(blocks)
    return call(
        functools.partial(attend_kernel, count, at),
        "attend",
        outs,
        ("s", info),
        ("s", slopes),
        *blocks,
        ("h", own),
        ("h", other),
        bias,
        scratch=[
            bf16(total, width),
            bf16(total, 4 * cols),
            bf16(heads, total, total),
            bf16(width, 4 * cols),
            bf16(width, 2 * cols),
            bf16(width, 2 * cols),
            sems(4 + 2 * len(blocks)),
        ],
        flops=16 * heads * total * total * HEAD_DIM + 8 * total * width * cols,
        exps=heads * total * total,
    )


def attend_back_kernel(g0, g1, g2, g3, w, qkvm, probs_ref, *refs):
    out_ref, sum_ref, *sends, gs_ref, gm_ref = refs
    blocks = (g0, g1, g2, g3)
    rows = g0.shape[0]
    cols = w.shape[1] // 4
    heads = cols // HEAD_DIM
    scale = HEAD_DIM**-0.5
    gm_ref[...] = low(dot(join(blocks), w[:, 3 * cols :]))
    for h in range(heads):
        lo = h * HEAD_DIM
        query = qkvm[:, lo : lo + HEAD_DIM]
        key = qkvm[:, cols + lo : cols + lo + HEAD_DIM]
        value = qkvm[:, 2 * cols + lo : 2 * cols + lo + HEAD_DIM]
        for b in range(len(blocks)):
            span = slice(b * rows, (b + 1) * rows)
            probs = wide(probs_ref[h, span, :])
            grad_probs = contract_cols(gm_ref[span, lo : lo + HEAD_DIM], value)
            inner = jnp.sum(grad_probs * probs, axis=1, keepdims=True)
            grad_scores = low(probs * (grad_probs - inner))
            gs_ref[span, :] = grad_scores
            out_ref[span, lo : lo + HEAD_DIM] = low(dot(grad_scores, key) * scale)
        out_ref[:, cols + lo : cols + lo + HEAD_DIM] = low(
            contract_rows(gs_ref[...], query) * scale
        )
        out_ref[:, 2 * cols + lo : 2 * cols + lo + HEAD_DIM] = low(
            contract_rows(probs_ref[h], gm_ref[:, lo : lo + HEAD_DIM])
        )
    for b in range(len(blocks)):
        span = slice(b * rows, (b + 1) * rows)
        sends[b][...] = low(contract_cols(out_ref[span, :], w[:, : 3 * cols]))
    sums = jnp.sum(wide(out_ref[...]), axis=0, keepdims=True)
    sum_ref[...] = jnp.broadcast_to(sums, sum_ref.shape)


def attend_back(blocks, w, qkvm, probs):
    rows, width = blocks[0].shape
    total = rows * len(blocks)
    cols = w.shape[1] // 4
    heads = cols // HEAD_DIM
    outs = [
        ((total, 3 * cols), jnp.bfloat16),
        ((8, 3 * cols), jnp.float32),
    ] + [((rows, width), jnp.bfloat16)] * len(blocks)
    return call(
        attend_back_kernel,
        "attend_back",
        outs,
        *blocks,
        w,
        qkvm,
        probs,
        scratch=[bf16(total, total), bf16(total, cols)],
        flops=32 * heads * total * total * HEAD_DIM + 8 * total * width * cols,
    )


def attend_weights_kernel(info, g0, g1, g2, g3, dqkv, xs, qkvm, give, keep):
    cols = dqkv.shape[1] // 3
    out = contract_rows(join((g0, g1, g2, g3)), qkvm[:, 3 * cols :])
    query_key = contract_rows(xs[...], dqkv[:, : 2 * cols])
    value = contract_rows(xs[...], dqkv[:, 2 * cols :])
    value_out = jnp.concatenate([value, out], axis=1)
    is_home = jnp.full(query_key.shape, info[2], jnp.int32) == 1
    give[...] = low(jnp.where(is_home, value_out, query_key))
    keep[...] = low(jnp.where(is_home, query_key, value_out))


def attend_weights(info, g, dqkv, xs, qkvm):
    total, width = xs.shape
    cols = qkvm.shape[1] // 4
    out = ((width, 2 * cols), jnp.bfloat16)
    return call(
        attend_weights_kernel,
        "attend_weights",
        [out, out],
        ("s", info),
        *g,
        dqkv,
        xs,
        qkvm,
        flops=8 * total * width * cols,
    )


def spread_kernel(count, place, keep, came, *refs):
    extra, outs = refs[:-count], refs[-count:]
    height = keep.shape[0] // count
    for k, out in enumerate(outs):
        to = place[0] ^ k
        span = pl.ds(pl.multiple_of(to * height, height), height)
        out[:height, :] = low(wide(keep[span, :]) + wide(came[span, :]))
        if extra:
            small, sums = extra
            cols = sums.shape[1] // 3
            row = lax.broadcasted_iota(jnp.int32, (small.shape[1], cols), 0)
            mine = jnp.full(row.shape, to, jnp.int32) == place[1]
            query = jnp.where(mine & (row == 0), sums[0:1, :cols], 0.0)
            value = jnp.where(mine & (row == 1), sums[0:1, 2 * cols :], 0.0)
            out[height:, :cols] = low(small[to][:, :cols] + query + value)
            out[height:, cols:] = low(small[to][:, cols:])


def spread(place, keep, came, count, *extra):
    added = extra[0].shape[1] if extra else 0
    out = ((keep.shape[0] // count + added, keep.shape[1]), jnp.bfloat16)
    body = functools.partial(spread_kernel, count)
    return call(body, "spread", [out] * count, ("s", place), keep, came, *extra)


def total_kernel(*refs):
    refs[-1][...] = low(summed(refs[:-1]))


def total_of(blocks):
    return call(total_kernel, "total", [(blocks[0].shape, jnp.bfloat16)], *blocks)[0]


def feed_kernel(x_ref, own, other, part_ref, saved_out, saved, sem):
    unit = own.shape[1] // 3
    x = x_ref[...]
    width = x.shape[1]
    first = start(x_ref, saved_out.at[:, :width], sem.at[0])
    for side, w in enumerate((own, other)):
        lo = side * unit
        packed = dot(x, w[:, : 2 * unit])
        gate, up = packed[:, :unit], packed[:, unit:]
        phi = 0.5 + 0.5 * lax.erf(gate * (0.5**0.5))
        bell = jnp.exp(gate * gate * -0.5) * (2.0 * math.pi) ** -0.5
        gelu = gate * phi
        saved[:, lo : lo + unit] = low(gelu * up)
        saved[:, 2 * unit + lo : 3 * unit + lo] = low(up * (phi + gate * bell))
        saved[:, 4 * unit + lo : 5 * unit + lo] = low(gelu)
    second = start(saved, saved_out.at[:, width:], sem.at[1])
    part_ref[...] = low(
        contract_cols(saved[:, :unit], own[:, 2 * unit :])
        + contract_cols(saved[:, unit : 2 * unit], other[:, 2 * unit :])
    )
    first.wait()
    second.wait()


def feed(x, own, other):
    rows, width = x.shape
    unit = own.shape[1] // 3
    outs = [
        ((rows, width), jnp.bfloat16),
        ((rows, width + 6 * unit), jnp.bfloat16, "h"),
    ]
    return call(
        feed_kernel,
        "feed",
        outs,
        x,
        own,
        other,
        scratch=[bf16(rows, 6 * unit), sems(2)],
        flops=12 * rows * width * unit,
        exps=4 * rows * unit,
        limit=8,
    )


def feed_back_kernel(g_ref, own, other, saved, part_ref, packed_ref):
    g = g_ref[...]
    unit = own.shape[1] // 3
    total = None
    for side, w in enumerate((own, other)):
        lo = g.shape[1] + (2 + side) * unit
        at = 2 * side * unit
        grad = dot(g, w[:, 2 * unit :])
        packed_ref[:, at : at + unit] = low(grad * wide(saved[:, lo : lo + unit]))
        packed_ref[:, at + unit : at + 2 * unit] = low(
            grad * wide(saved[:, 2 * unit + lo : 3 * unit + lo])
        )
        term = contract_cols(packed_ref[:, at : at + 2 * unit], w[:, : 2 * unit])
        total = term if total is None else total + term
    part_ref[...] = low(total)


def feed_back(g, own, other, saved):
    rows, width = g.shape
    unit = own.shape[1] // 3
    outs = [((rows, width), jnp.bfloat16), ((rows, 4 * unit), jnp.bfloat16)]
    return call(
        feed_back_kernel,
        "feed_back",
        outs,
        g,
        own,
        other,
        saved,
        flops=12 * rows * width * unit,
        limit=8,
    )


def feed_weights_kernel(side, *refs):
    saved, g, packed, out = refs[:4], refs[4:8], refs[8:12], refs[12]
    width = g[0].shape[1]
    unit = out.shape[1] // 3
    lo = 2 * side * unit
    at = width + side * unit
    act = jnp.concatenate([s[:, at : at + unit] for s in saved], axis=0)
    out[:, 2 * unit :] = low(contract_rows(join(g), act))
    x = jnp.concatenate([s[:, :width] for s in saved], axis=0)
    packed_all = jnp.concatenate([p[:, lo : lo + 2 * unit] for p in packed], axis=0)
    out[:, : 2 * unit] = low(contract_rows(x, packed_all))


def feed_weights(side, saved, g, packed):
    rows, width = g[0].shape
    unit = packed[0].shape[1] // 4
    return call(
        functools.partial(feed_weights_kernel, side),
        "feed_weights",
        [((width, 3 * unit), jnp.bfloat16)],
        *saved,
        *g,
        *packed,
        flops=24 * rows * width * unit,
    )[0]


def small_kernel(place, *refs):
    *given, out = refs
    layers = len(given) // 4
    groups, count, both = out.shape
    cols = both // 2
    row = lax.broadcasted_iota(jnp.int32, (count, cols), 0)
    lane = lax.broadcasted_iota(jnp.int32, (count, cols), 1)
    heads = cols // HEAD_DIM
    high = jnp.zeros((count, cols), jnp.float32)
    for l in range(layers):
        top = given[4 * l + 3]
        for h in range(heads):
            at = (place[0] * layers + l) * heads + h
            high = jnp.where(lane == at, top[0:1, h : h + 1], high)
    whole = wide(low(high))
    tops = jnp.where(row == 0, whole, jnp.where(row == 1, high - whole, 0.0))
    for g in range(groups):
        span = slice(g * cols, (g + 1) * cols)
        mine = jnp.full((1, cols), place[1], jnp.int32) == g
        values = jnp.zeros((count, cols), jnp.float32)
        for l in range(layers):
            one, two, sums = given[4 * l : 4 * l + 3]
            rows = [
                one[2:3, span],
                two[2:3, span],
                one[1:2, span],
                two[1:2, span],
                one[0:1, span],
                two[0:1, span],
            ]
            if l > 0:
                query = jnp.where(mine, sums[0:1, :cols], 0.0)
                rows = [query, jnp.where(mine, sums[0:1, 2 * cols :], 0.0)] + rows
            for i, value in enumerate(reversed(rows)):
                values = jnp.where(row == 8 * l + 7 - i, value, values)
        out[g, :, :cols] = values
        out[g, :, cols:] = tops


def small_rows(place, groups, given, cols):
    shape = (groups, 2 * len(given), 2 * cols)
    return call(small_kernel, "small", [(shape, jnp.float32)], ("s", place), *given)[0]


def finish_feed_kernel(l, place, *refs):
    glu_out, down_out, token, glu, down, sem = refs[-6:]
    parts, _, unit = down.shape
    token[...] = jnp.zeros_like(token)
    near = refs[:parts]
    copies = []
    for k, block in enumerate(near):
        span = pl.ds(pl.multiple_of((place[1] ^ k) * unit, 128), unit)
        glu[k, :, 0, :] = wide(block[:, :unit])
        glu[k, :, 1, :] = wide(block[:, unit : 2 * unit])
        copies.append(start(glu.at[k], glu_out.at[l, :, :, span], sem.at[2 * k]))
        down[k] = wide(block[:, 2 * unit : 3 * unit])
        copies.append(start(down.at[k], down_out.at[l, :, span], sem.at[2 * k + 1]))
    for copy in copies:
        copy.wait()


def finish_feed(l, layers, place, near, unit, before):
    rows, parts = near[0].shape[0], len(near)
    outs = [
        ((layers, rows, 2, unit * parts), jnp.float32, "h"),
        ((layers, rows, unit * parts), jnp.float32, "h"),
        ((8, 128), jnp.float32),
    ]
    given = [("s", place), *near]
    alias = {}
    if before is not None:
        alias = {len(given): 0, len(given) + 1: 1}
        given += [("h", x) for x in before]
    return call(
        functools.partial(finish_feed_kernel, l),
        "finish_feed",
        outs,
        *given,
        scratch=[
            pltpu.VMEM((parts, rows, 2, unit), jnp.float32),
            pltpu.VMEM((parts, rows, unit), jnp.float32),
            sems(2 * parts),
        ],
        alias=alias,
    )


def choose_kernel(parts, count, at, flags, *refs):
    *blocks, out = refs
    pair = parts // 2
    row = 0
    for i in range(0, len(blocks), parts):
        for k in range(pair):
            near, far = blocks[i + k], blocks[i + pair + k]
            columns = slice(at if i else 0, None)
            near, far = wide(near[:, columns]), wide(far[:, columns])
            home = jnp.full(near.shape, flags[0], jnp.int32) == 1
            out[row : row + near.shape[0], :] = low(jnp.where(home, far, near))
            row += near.shape[0]
    for block in blocks[:parts]:
        height, _ = block.shape
        out[row : row + count, :] = block[height - count :, :]
        row += count


def choose(flags, blocks, others, count, at):
    parts = len(blocks)
    rows = sum(b[0].shape[0] for b in [blocks] + others) * (parts // 2) + parts * count
    body = functools.partial(choose_kernel, parts, count, at)
    given = [x for b in [blocks] + others for x in b]
    out = ((rows, blocks[0].shape[1]), jnp.bfloat16)
    return call(body, "choose", [out], ("s", flags), *given)[0]


def finish_attention_kernel(groups, parts, count, from_col, flags, *refs):
    qkv_out, out_out, clip_out, small_out, weights, qkv, out, clip, sem = refs[-9:]
    *given, came, weight_in = refs[:-9]
    blocks = given[:parts]
    pair = parts // 2
    height, _ = blocks[0].shape
    layers, _, rows, half = qkv.shape
    cols = half // 2
    heads = cols // HEAD_DIM
    fetched = [start(weight_in.at[l, :2], weights.at[l], sem.at[l]) for l in range(layers)]
    total, tops = None, []
    for k, block in enumerate(blocks):
        at = came.shape[0] - (parts - k) * count
        mine, theirs = wide(block[height - count :, :]), wide(came[at : at + count, :])
        both = mine[:, :cols] + theirs[:, :cols]
        total = both if total is None else total + both
        tops.append(
            jnp.maximum(
                mine[0:1, cols:] + mine[1:2, cols:], theirs[0:1, cols:] + theirs[1:2, cols:]
            )
        )
    small_out[...] = total
    home = jnp.full((rows, half), flags[0], jnp.int32) == 1
    even = jnp.full((rows, half), flags[1], jnp.int32) == 1
    home_row, even_row = home[0:1, :cols], even[0:1, :cols]
    pick_tops = [jnp.where(home_row, tops[i], tops[pair + i]) for i in range(pair)]
    first_top = jnp.where(even_row, pick_tops[0], pick_tops[1])
    second_top = jnp.where(even_row, pick_tops[1], pick_tops[0])
    lane = lax.broadcasted_iota(jnp.int32, (1, half), 1) // HEAD_DIM
    copies = []
    for l in range(layers):
        columns = slice(from_col if l else 0, None)
        near = [wide(b[:rows, columns]) for b in given[l * parts : (l + 1) * parts]]
        at, step = (pair * (height + (l - 1) * rows), rows) if l else (0, height)
        far = [wide(came[at + i * step : at + i * step + rows, :]) for i in range(pair)]
        near = [jnp.where(home, near[i], near[pair + i]) for i in range(pair)]
        query_key = [jnp.where(even, near[0], near[1]), jnp.where(even, near[1], near[0])]
        value_out = [jnp.where(even, far[0], far[1]), jnp.where(even, far[1], far[0])]
        for i in range(pair):
            place = slice(i * cols, (i + 1) * cols)
            qkv[l, 0, :, place] = query_key[i][:, :cols]
            qkv[l, 1, :, place] = query_key[i][:, cols:]
            qkv[l, 2, :, place] = value_out[i][:, :cols]
            out[l, :, place] = value_out[i][:, cols:]
        copies.append(start(qkv.at[l], qkv_out.at[l], sem.at[layers + 3 * l]))
        copies.append(start(out.at[l], out_out.at[l], sem.at[layers + 3 * l + 1]))
        top = jnp.zeros((1, half), jnp.float32)
        for i, row in enumerate((first_top, second_top)):
            for h in range(heads):
                best = None
                for g in range(groups):
                    at = (g * layers + l) * heads + h
                    value = row[:, at : at + 1]
                    best = value if best is None else jnp.maximum(best, value)
                top = jnp.where(lane == i * heads + h, best, top)
        factor = CLIP_LIMIT / jnp.maximum(top, CLIP_LIMIT)
        fetched[l].wait()
        for m in range(2):
            clip[l, :, m, :] = (wide(weights[l, m]) - STEP_SIZE * qkv[l, m]) * factor
        copies.append(start(clip.at[l], clip_out.at[l], sem.at[layers + 3 * l + 2]))
    for copy in copies:
        copy.wait()


def finish_attention(groups, count, at, flags, blocks, others, came, weight):
    layers, _, rows, half = weight.shape
    outs = [
        ((layers, 3, rows, half), jnp.float32, "h"),
        ((layers, rows, half), jnp.float32, "h"),
        ((layers, rows, 2, half), jnp.float32, "h"),
        ((count, half // 2), jnp.float32),
    ]
    return call(
        functools.partial(finish_attention_kernel, groups, len(blocks), count, at),
        "finish_attention",
        outs,
        ("s", flags),
        *[x for b in [blocks] + others for x in b],
        came,
        ("h", weight),
        scratch=[
            pltpu.VMEM((layers, 2, rows, half), weight.dtype),
            f32(layers, 3, rows, half),
            f32(layers, rows, half),
            f32(layers, rows, 2, half),
            sems(4 * layers),
        ],
    )


def both_kernel(core, own, other, out):
    out[core[0]] = own[...]
    out[1 - core[0]] = other[...]


def both_slots(core, own, other):
    out = ((2, *own.shape), own.dtype)
    return call(both_kernel, "both", [out], ("s", core), own, other)[0]


def normalised(z):
    mean = jnp.mean(z, axis=1, keepdims=True)
    centred = z - mean
    r = lax.rsqrt(jnp.mean(centred * centred, axis=1, keepdims=True) + EPSILON)
    return centred * r, r


def affine(n, vec, gain, shift):
    return n * vec[gain : gain + 1, :] + vec[shift : shift + 1, :]


def summed(refs):
    total = wide(refs[0][...])
    for ref in refs[1:]:
        total = total + wide(ref[...])
    return total


def norm_input(before, bias, parts, prev, vec):
    z = summed(parts) + vec[bias : bias + 1, :]
    if before is None:
        return z + wide(prev[...])
    return z + affine(normalised(prev[...])[0], vec, *before)


def norm_kernel(before, rows_of, p0, p1, p2, p3, prev, vec, low_ref, z_out, zs, sem):
    bias, gain, shift = rows_of
    z = norm_input(before, bias, (p0, p1, p2, p3), prev, vec)
    zs[...] = z
    copy = start(zs, z_out, sem.at[0])
    low_ref[...] = low(affine(normalised(z)[0], vec, gain, shift))
    copy.wait()


def norm(before, rows_of, parts, prev, vec):
    shape = parts[0].shape
    outs = [(shape, jnp.bfloat16), (shape, jnp.float32, "h")]
    return call(
        functools.partial(norm_kernel, before, rows_of),
        "norm",
        outs,
        *parts,
        prev,
        vec,
        scratch=[f32(*shape), sems(1)],
        flops=prev.size,
    )


def norm_grad(grad, n, r, gain, dz_out, low_ref, stat_ref, dzs, sem):
    scaled = grad * gain
    one = jnp.mean(scaled, axis=1, keepdims=True)
    two = jnp.mean(scaled * n, axis=1, keepdims=True)
    dz = (scaled - one - n * two) * r
    dz_low = low(dz)
    dzs[...] = dz
    copy = start(dzs, dz_out, sem)
    low_ref[...] = dz_low
    stat_ref[0:1, :] = jnp.sum(grad * n, axis=0, keepdims=True)
    stat_ref[1:2, :] = jnp.sum(grad, axis=0, keepdims=True)
    stat_ref[2:3, :] = jnp.sum(wide(dz_low), axis=0, keepdims=True)
    stat_ref[3:, :] = jnp.zeros((stat_ref.shape[0] - 3, stat_ref.shape[1]), jnp.float32)
    copy.wait()


def norm_back_kernel(gain_row, p0, p1, p2, p3, skip, z, vec, *refs):
    *outs, dzs, sem = refs
    grad = summed((p0, p1, p2, p3)) + skip[...]
    n, r = normalised(z[...])
    norm_grad(grad, n, r, vec[gain_row : gain_row + 1, :], *outs, dzs, sem.at[0])


def grad_outs(shape):
    return [
        (shape, jnp.float32, "h"),
        (shape, jnp.bfloat16),
        ((8, shape[1]), jnp.float32),
    ]


def norm_back(gain_row, parts, skip, z, vec):
    shape = skip.shape
    return call(
        functools.partial(norm_back_kernel, gain_row),
        "norm_back",
        grad_outs(shape),
        *parts,
        skip,
        z,
        vec,
        scratch=[f32(*shape), sems(1)],
        flops=skip.size,
    )


def turn_kernel(before, rows_of, info, p0, p1, p2, p3, prev, vec, cot, out_ref, *refs):
    *outs, dzs, sem = refs
    bias, gain, shift = rows_of
    z = norm_input(before, bias, (p0, p1, p2, p3), prev, vec)
    n, r = normalised(z)
    rows = z.shape[0]
    ok = info[0] * rows + lax.broadcasted_iota(jnp.int32, (rows, 1), 0) < info[1]
    out_ref[...] = low(jnp.where(ok, affine(n, vec, gain, shift), 0.0))
    grad = jnp.where(ok, wide(cot[...]), 0.0)
    norm_grad(grad, n, r, vec[gain : gain + 1, :], *outs, dzs, sem.at[0])


def turn(before, rows_of, info, parts, prev, vec, cot):
    shape = prev.shape
    outs = [(shape, jnp.bfloat16)] + grad_outs(shape)
    return call(
        functools.partial(turn_kernel, before, rows_of),
        "turn",
        outs,
        ("s", info),
        *parts,
        prev,
        vec,
        cot,
        scratch=[f32(*shape), sems(1)],
        flops=prev.size,
    )


def shards(
    tokens,
    cotangent,
    lengths,
    dealing,
    qkv_weight,
    out_weight,
    glu_weight,
    down_weight,
    biases,
    gains,
):
    slots, rows, width = tokens.shape
    layers = qkv_weight.shape[0]
    parts = lax.axis_size("ctx")
    cores = lax.axis_size("heads")
    groups = lax.axis_size("dp")
    part = lax.axis_index("ctx")
    core = lax.axis_index("heads")
    group = lax.axis_index("dp")
    local_rows = qkv_weight.shape[1]
    half = qkv_weight.shape[3]
    cols = half * cores // parts
    local_heads = cols // HEAD_DIM
    quarter = glu_weight.shape[3] // parts
    per_core = parts // cores
    home = part // per_core == core
    offset = (part % per_core) * cols

    def swap(x):
        return lax.ppermute(x, "heads", [(j, cores - 1 - j) for j in range(cores)])

    def hop(x, k):
        return lax.ppermute(x, "ctx", [(j, j ^ k) for j in range(parts)])

    def hops(blocks):
        return [blocks[0]] + [hop(blocks[k], k) for k in range(1, parts)]

    def own_first(work, blocks, extras):
        done = [work(blocks[0], extras[0])]
        for block, extra in zip(blocks[1:], extras[1:]):
            block, _ = lax.optimization_barrier((block, done[-1][0]))
            done.append(work(block, extra))
        return zip(*done)

    def behind(blocks, staged):
        return [tie(blocks[0], staged[0])] + blocks[1:]

    def gather(x):
        return hops([x] * parts)

    def tie(x, *others):
        return lax.optimization_barrier((x, *others))[0]

    value_out = jnp.concatenate(
        [
            lax.dynamic_slice_in_dim(qkv_weight[:, :, 2, :], offset, cols, 2),
            lax.dynamic_slice_in_dim(out_weight, offset, cols, 2),
        ],
        axis=2,
    )
    query_key = jnp.concatenate(
        [
            lax.dynamic_slice_in_dim(qkv_weight[:, :, 0, :], offset, cols, 2),
            lax.dynamic_slice_in_dim(qkv_weight[:, :, 1, :], offset, cols, 2),
        ],
        axis=2,
    )
    attn_shard = jnp.where(home, query_key, swap(value_out))
    attn_first, attn_shard_later = attn_shard[0], [attn_shard[l] for l in range(1, layers)]
    glu_part = lax.dynamic_slice_in_dim(glu_weight, part * quarter, quarter, 3)
    down_part = lax.dynamic_slice_in_dim(down_weight, part * quarter, quarter, 2)

    def over_dp(x):
        return lax.all_gather(x, "dp", axis=0, tiled=True)

    direct = groups <= 4 and local_rows == cols
    place = jnp.stack([group, part]).astype(jnp.int32)

    def hop_dp(x, k):
        return lax.ppermute(x, "dp", [(j, j ^ k) for j in range(groups)])

    feed_full = [None] * layers
    attn_full = [None] * layers
    tokens_own = lax.dynamic_index_in_dim(tokens, core, 0, keepdims=False)
    feed_shard = [
        jnp.concatenate([glu_part[l, :, 0], glu_part[l, :, 1], down_part[l]], axis=1)
        for l in range(layers)
    ]
    early = over_dp(jnp.concatenate([feed_shard[0]] + attn_shard_later, axis=1))
    if direct:
        low_zero = gather(tokens_own)
        own = lax.all_gather(attn_first, "dp", axis=0, tiled=True)
    else:
        own = over_dp(attn_first)
        low_zero = gather(tokens_own)
    attn_full[0] = (own, swap(own), 0)
    late = [over_dp(lax.optimization_barrier((x, own))[0]) for x in feed_shard[1:]]

    slot = group * slots + core
    slot_ids = jnp.arange(lengths.shape[0], dtype=jnp.int32)
    sequence = jnp.sum(jnp.where(slot_ids == slot, dealing, 0))
    length = jnp.sum(jnp.where(slot_ids == sequence, lengths, 0))
    info = [
        jnp.stack([part, length, home, jnp.int32(0)]).astype(
            jnp.int32
        )
        for l in range(layers)
    ]
    slopes = lax.dynamic_slice_in_dim(
        jnp.array(alibi_slopes(HEADS), jnp.float32), part * local_heads, local_heads
    )
    vec = jnp.concatenate([biases, gains], axis=1).reshape(layers * 8, width)
    qv = lax.dynamic_slice_in_dim(biases[:, :2], part * cols, cols, 2)
    qkv_bias = jnp.concatenate([qv[:, :1], jnp.zeros_like(qv[:, :1]), qv[:, 1:]], axis=2)

    prev, before = tokens_own, None
    low_own = tokens_own
    saved = []
    tops = []
    for l in range(layers):
        v = 8 * l
        x_low = low_zero if l == 0 else gather(low_own)
        xs, qkvm, probs, attn_w, top, *sends = attend(
            info[l],
            slopes,
            x_low,
            *attn_full[l],
            qkv_bias[l],
            1,
        )
        tops.append(top)
        near = stage([tie(prev, sends[0]), vec])
        hidden_low, z_one = norm(before, (v + 2, v + 6, v + 4), behind(hops(sends), near), *near)
        feed_own = tie(early if l == 0 else late[l - 1], hidden_low if l == 0 else top)
        feed_full[l] = (feed_own, swap(feed_own))
        if l == 0:
            for n in range(1, layers):
                attn_full[n] = (*feed_full[0], 3 * quarter + 2 * cols * (n - 1))
        h_low = gather(hidden_low)
        near = stage([tie(w, hidden_low) for w in feed_full[l]], 3 * quarter)
        sends, kept = own_first(lambda h, _: feed(h, *near), h_low, h_low)
        arrived = hops(sends)
        rows_of = (v + 3, v + 7, v + 5)
        near = stage([tie(z_one, sends[0]), vec])
        arrived = behind(arrived, near)
        if l + 1 < layers:
            low_own, z_two = norm((v + 6, v + 4), rows_of, arrived, *near)
            prev, before = z_two, (v + 7, v + 5)
        else:
            cot = lax.dynamic_index_in_dim(cotangent, core, 0, keepdims=False)
            outputs, grad_two, low_two, stats_two = turn(
                (v + 6, v + 4), rows_of, info[l], arrived, *near, cot
            )
            z_two = None
        saved.append((xs, qkvm, probs, attn_w, z_one, kept, z_two))

    feed_parts = [None] * layers
    carried = None
    woven = [None] * layers

    def over_dp_sum(x):
        return lax.psum_scatter(x, "dp", scatter_dimension=0, tiled=True)

    stats = [[None] * 3 for _ in range(layers)]
    for l in reversed(range(layers)):
        v = 8 * l
        x_low, qkvm, probs, attn_w, z_one, kept, _ = saved[l]
        above = l + 1 < layers
        stats[l][1] = stats_two
        g_low = gather(low_two)
        *near, k0, k1, k2, k3 = stage(
            [tie(w, low_two) for w in (*feed_full[l], *kept)], 3 * quarter
        )
        kept = [k0, k1, k2, k3]
        sends, packed = own_first(lambda g, k: feed_back(g, *near, k), g_low, kept)
        arrived = hops(sends)
        packed = list(packed)
        packed[0], arrived[1] = lax.optimization_barrier((packed[0], arrived[1]))
        give = feed_weights(1, kept, g_low, packed)
        packed[0], arrived[2], give = lax.optimization_barrier((packed[0], arrived[2], give))
        keep = feed_weights(0, kept, g_low, packed)
        came = tie(swap(give), arrived[3])
        total = wide(keep) + wide(came)
        if above:
            total = jnp.concatenate([total, carried], axis=1)
        total = low(total)
        arrived[0] = tie(arrived[0], total)
        near = stage([tie(grad_two, sends[0]), z_one, vec])
        grad_one, low_one, stats[l][0] = norm_back(v + 6, behind(arrived, near), *near)
        feed_parts[l] = over_dp_sum(total)
        a_low = gather(low_one)
        attn_w, qkvm, probs, x_low = stage([tie(attn_w, low_one), qkvm, probs, x_low])
        dqkv, sums, *sends = attend_back(a_low, attn_w, qkvm, probs)
        if above:
            woven[l + 1] = gather(tie(feed_parts[l + 1], *a_low))
        stats[l][2] = sums
        arrived = hops(sends)
        give, keep = attend_weights(info[l], a_low, dqkv, x_low, qkvm)
        came = swap(give)
        if l > 0:
            arrived[0] = tie(arrived[0], keep)
            carried = wide(keep) + wide(came)
            near = stage([tie(grad_one, sends[0]), saved[l - 1][6], vec])
            grad_two, low_two, stats_two = norm_back(v - 8 + 7, behind(arrived, near), *near)

    count = layers * local_heads
    if direct:
        given = []
        for l in range(layers):
            given += [stats[l][0], stats[l][1], stats[l][2] if l else stats[l][0], tops[l]]
        small = small_rows(place, groups, given, cols)
        terms = list(spread(place, keep, came, groups, small, sums))
        terms[1:] = [hop_dp(terms[k], k) for k in range(1, groups)]
        last = total_of(terms)
        near = [x for l in range(1, layers) for x in woven[l]]
        tied = lax.optimization_barrier((*arrived, *near, *terms))
        arrived, near = list(tied[:parts]), list(tied[parts : parts + len(near)])
        last = tie(last, *arrived, *near)
        for l in range(1, layers):
            woven[l] = near[(l - 1) * parts : l * parts]
        grad = grad_one + sum(wide(a) for a in arrived)
    else:
        grad = grad_one + sum(wide(a) for a in arrived)
        empty = jnp.zeros((width,), jnp.float32)
        small = []
        for l in range(layers):
            one, two, sums = stats[l]
            small += [
                lax.dynamic_update_slice_in_dim(empty, sums[0, lo : lo + cols], part * cols, 0)
                for lo in (0, 2 * cols)
            ]
            small += [one[2], two[2], one[1], two[1], one[0], two[0]]
        small = jnp.stack(small).reshape(layers * 8, groups, local_rows).transpose(1, 0, 2)
        small = jnp.pad(small, ((0, 0), (0, 0), (0, cols - local_rows)))
        own_tops = jnp.stack([t[0, :local_heads] for t in tops]).reshape(-1)
        high = wide(low(own_tops))
        pair = jnp.stack([high, own_tops - high])
        slots_of = jnp.zeros((layers * 8, cols), jnp.float32)
        slots_of = lax.dynamic_update_slice(slots_of, pair, (0, group * count))
        slots_of = jnp.broadcast_to(slots_of[None], (groups,) + slots_of.shape)
        small = jnp.concatenate([small, slots_of], axis=2)
        total = wide(keep) + wide(came)
        payload = jnp.concatenate([total.reshape(groups, local_rows, 2 * cols), small], axis=1)
        last = lax.psum_scatter(low(payload), "dp", scatter_dimension=0, tiled=False)
    core_ref = core.astype(jnp.int32)[None]
    out_tokens = both_slots(core_ref, outputs, swap(outputs))
    grad_tokens = both_slots(core_ref, grad, swap(grad))
    shared = gather(last)
    near = gather(tie(feed_parts[0], last))
    result, tokens = None, []
    for l in reversed(range(1, layers)):
        *result, token = finish_feed(l, layers, place, woven[l], quarter, result)
        tokens.append(token)
    tied = lax.optimization_barrier((*shared, *near, out_tokens, grad_tokens, *tokens))
    shared, near = list(tied[:parts]), list(tied[parts : 2 * parts])
    out_tokens, grad_tokens = tied[2 * parts : 2 * parts + 2]
    woven[0] = near
    flags = jnp.stack([home, part % per_core == 0]).astype(jnp.int32)
    small_count = layers * 8
    others = woven[: layers - 1]
    arrived = swap(choose(flags, shared, others, small_count, 3 * quarter))

    grad_qkv, grad_out, clipped_qk, small_sum = finish_attention(
        groups,
        small_count,
        3 * quarter,
        flags,
        shared,
        others,
        arrived,
        qkv_weight.transpose(0, 2, 1, 3),
    )
    small_sum = small_sum[:, :local_rows].reshape(layers, 8, local_rows)
    grad_glu, grad_down, _ = finish_feed(0, layers, place, near, quarter, result)
    return (
        out_tokens,
        grad_tokens,
        grad_qkv.transpose(0, 2, 1, 3),
        grad_out,
        grad_glu,
        grad_down,
        small_sum[:, :6],
        small_sum[:, 6:],
        clipped_qk,
    )


def solution(mesh):
    in_specs = (
        P("dp", "ctx", None),
        P("dp", "ctx", None),
        P(),
        P(),
        P(None, "dp", None, "heads"),
        P(None, "dp", "heads"),
        P(None, "dp", None, "heads"),
        P(None, "dp", "heads"),
        P(),
        P(),
    )
    out_specs = (
        P("dp", "ctx", None),
        P("dp", "ctx", None),
        P(None, "dp", None, "heads"),
        P(None, "dp", "heads"),
        P(None, "dp", None, "heads"),
        P(None, "dp", "heads"),
        P(None, None, "dp"),
        P(None, None, "dp"),
        P(None, "dp", None, "heads"),
    )
    return jax.shard_map(shards, mesh=mesh, in_specs=in_specs, out_specs=out_specs, check_vma=False)
```

```python
import functools
import math

import jax
import jax.numpy as jnp
from jax import lax
from jax.experimental import pallas as pl
from jax.experimental.pallas import tpu as pltpu
from jax.sharding import PartitionSpec as P

HEADS = 12
HEAD_DIM = 64


EPSILON = 1e-12
NEGATIVE = -1e30
CLIP_LIMIT = 4.0
STEP_SIZE = 0.0008
MIB = 1024 * 1024


def power_slopes(head_count):
    first_slope = 2.0 ** (-8.0 / head_count)
    return [first_slope ** (position + 1) for position in range(head_count)]


def alibi_slopes(head_count):
    closest = 2 ** int(math.floor(math.log2(head_count)))
    slopes = power_slopes(closest)
    slopes = slopes + power_slopes(2 * closest)[0::2][: head_count - closest]
    return slopes


def dot(a, b):
    return jnp.dot(a, b, preferred_element_type=jnp.float32)


def contract_rows(former, latter):
    return lax.dot_general(
        former, latter, (((0,), (0,)), ((), ())), preferred_element_type=jnp.float32
    )


def contract_cols(former, latter):
    return lax.dot_general(
        former, latter, (((1,), (1,)), ((), ())), preferred_element_type=jnp.float32
    )


def low(x):
    return x.astype(jnp.bfloat16)


def wide(x):
    return x.astype(jnp.float32)


def positions_of(shape, axis, rows, part):
    index = lax.broadcasted_iota(jnp.int32, shape, axis)
    shift = rows.bit_length() - 1
    return (((index >> shift) ^ part) << shift) | (index & (rows - 1))


def join(refs):
    return jnp.concatenate([r[...] for r in refs], axis=0)


def call(body, name, outs, *args, scratch=(), flops=0, exps=0, limit=16, alias=None):
    spaces = {"s": pltpu.SMEM, "h": pltpu.HBM, "d": pl.ANY, "v": pltpu.VMEM}
    args = [a if isinstance(a, tuple) else ("v", a) for a in args]
    outs = [o if len(o) == 3 else (*o, "v") for o in outs]
    values = [
        pltpu.with_memory_space_constraint(a[1], pltpu.HBM) if a[0] == "h" else a[1] for a in args
    ]
    shapes = tuple(
        pltpu.HBM(o[0], o[1]) if o[2] == "h" else jax.ShapeDtypeStruct(o[0], o[1]) for o in outs
    )
    moved = sum(v.size * v.dtype.itemsize for v in values)
    moved += sum(math.prod(o[0]) * jnp.dtype(o[1]).itemsize for o in outs)
    return pl.pallas_call(
        body,
        out_shape=shapes,
        in_specs=[pl.BlockSpec(memory_space=spaces[a[0]]) for a in args],
        out_specs=tuple(pl.BlockSpec(memory_space=spaces[o[2]]) for o in outs),
        scratch_shapes=list(scratch),
        input_output_aliases=alias or {},
        compiler_params=pltpu.CompilerParams(vmem_limit_bytes=limit * MIB),
        cost_estimate=pl.CostEstimate(flops=flops, bytes_accessed=moved, transcendentals=exps),
        name=name,
    )(*values)


def start(source, target, sem):
    copy = pltpu.make_async_copy(source, target, sem)
    copy.start()
    return copy


def bf16(*shape):
    return pltpu.VMEM(shape, jnp.bfloat16)


def f32(*shape):
    return pltpu.VMEM(shape, jnp.float32)


def sems(count):
    return pltpu.SemaphoreType.DMA((count,))


def pick(flag, one, two):
    chosen = jnp.full(one.shape, flag, jnp.int32) == 1
    return jnp.where(chosen, wide(one[...]), wide(two[...])).astype(jnp.bfloat16)


def stage_kernel(*refs):
    *refs, sem = refs
    count = len(refs) // 2
    copies = []
    for i, (source, target) in enumerate(zip(refs[:count], refs[count:])):
        if source.shape != target.shape:
            source = source.at[:, : target.shape[1]]
        copies.append(start(source, target, sem.at[i]))
    for copy in copies:
        copy.wait()


def stage(arrays, columns=None):
    outs = [
        ((a.shape[0], columns) if columns and a.shape[0] > columns // 2 else a.shape, a.dtype)
        for a in arrays
    ]
    return call(
        stage_kernel, "stage", outs, *[("h", a) for a in arrays], scratch=[sems(len(arrays))], limit=4
    )


def attend_kernel(count, at, info, slope_ref, x0, x1, x2, x3, own, other, bias, *refs):
    xs_out, qkvm_out, probs_out, w_out, top_ref = refs[:5]
    sends = refs[5:9]
    xs, qkvm, probs_ref, w, own_ref, other_ref, sem = refs[9:]
    columns = slice(at, at + own_ref.shape[1])
    one = start(own.at[:, columns], own_ref, sem.at[10])
    two = start(other.at[:, columns], other_ref, sem.at[11])
    blocks = (x0, x1, x2, x3)
    rows = x0.shape[0]
    total = rows * len(blocks)
    cols = own_ref.shape[1] // 2
    part, length, home = info[0], info[1], info[2]
    for b, ref in enumerate(blocks):
        xs[b * rows : (b + 1) * rows, :] = ref[...]
    copies = [start(xs, xs_out, sem.at[0])]
    height = own_ref.shape[0] // count
    one.wait()
    two.wait()
    for k in range(count):
        span = slice(k * height, (k + 1) * height)
        place = pl.ds(pl.multiple_of((info[3] ^ k) * height, height), height)
        w[place, : 2 * cols] = pick(home, own_ref[span, :], other_ref[span, :])
        w[place, 2 * cols :] = pick(home, other_ref[span, :], own_ref[span, :])
    copies.append(start(w, w_out, sem.at[9]))
    x = xs[...]
    qkvm[:, : 3 * cols] = low(dot(x, w[:, : 3 * cols]) + bias[...])
    out_w = w[:, 3 * cols :]
    key_pos = positions_of((1, total), 1, rows, part)
    key_ok = key_pos < length
    heads = cols // HEAD_DIM
    tops = [jnp.full((1, 1), NEGATIVE, jnp.float32)] * heads
    for b in range(len(blocks)):
        span = slice(b * rows, (b + 1) * rows)
        pos = ((b ^ part) * rows) + lax.broadcasted_iota(jnp.int32, (rows, 1), 0)
        distance = jnp.abs(pos - key_pos).astype(jnp.float32)
        for h in range(heads):
            lo = h * HEAD_DIM
            key = qkvm[:, cols + lo : cols + lo + HEAD_DIM]
            value = qkvm[:, 2 * cols + lo : 2 * cols + lo + HEAD_DIM]
            query = qkvm[span, lo : lo + HEAD_DIM] * jnp.bfloat16(HEAD_DIM**-0.5)
            masked = jnp.where(key_ok, contract_cols(query, key), NEGATIVE)
            block_top = jnp.max(masked, axis=1, keepdims=True)
            block_top = jnp.where(pos < length, block_top, NEGATIVE)
            tops[h] = jnp.maximum(tops[h], jnp.max(block_top, axis=0, keepdims=True))
            scores = masked - slope_ref[h] * distance
            row_max = jnp.max(scores, axis=1, keepdims=True)
            exponent = jnp.exp(scores - row_max)
            totals = jnp.sum(exponent, axis=1, keepdims=True)
            probs = low(exponent * (1.0 / totals))
            probs_ref[h, span, :] = probs
            qkvm[span, 3 * cols + lo : 3 * cols + lo + HEAD_DIM] = low(dot(probs, value))
        copies.append(
            start(probs_ref.at[:, span, :], probs_out.at[:, span, :], sem.at[1 + 2 * b])
        )
        copies.append(start(qkvm.at[span, :], qkvm_out.at[span, :], sem.at[2 + 2 * b]))
        sends[b][...] = low(contract_cols(qkvm[span, 3 * cols :], out_w))
    lane = lax.broadcasted_iota(jnp.int32, (8, 128), 1)
    packed = jnp.full((8, 128), NEGATIVE, jnp.float32)
    for h, top in enumerate(tops):
        packed = jnp.where(lane == h, top, packed)
    top_ref[...] = packed
    for copy in copies:
        copy.wait()


def attend(info, slopes, blocks, own, other, at, bias, count):
    rows, width = blocks[0].shape
    total = rows * len(blocks)
    cols = bias.shape[1] // 3
    heads = cols // HEAD_DIM
    outs = [
        ((total, width), jnp.bfloat16, "h"),
        ((total, 4 * cols), jnp.bfloat16, "h"),
        ((heads, total, total), jnp.bfloat16, "h"),
        ((width, 4 * cols), jnp.bfloat16, "h"),
        ((8, 128), jnp.float32),
    ] + [((rows, width), jnp.bfloat16)] * len(blocks)
    return call(
        functools.partial(attend_kernel, count, at),
        "attend",
        outs,
        ("s", info),
        ("s", slopes),
        *blocks,
        ("h", own),
        ("h", other),
        bias,
        scratch=[
            bf16(total, width),
            bf16(total, 4 * cols),
            bf16(heads, total, total),
            bf16(width, 4 * cols),
            bf16(width, 2 * cols),
            bf16(width, 2 * cols),
            sems(4 + 2 * len(blocks)),
        ],
        flops=16 * heads * total * total * HEAD_DIM + 8 * total * width * cols,
        exps=heads * total * total,
    )


def attend_back_kernel(g0, g1, g2, g3, w, qkvm, probs_ref, *refs):
    out_ref, sum_ref, *sends, gs_ref, gm_ref = refs
    blocks = (g0, g1, g2, g3)
    rows = g0.shape[0]
    cols = w.shape[1] // 4
    heads = cols // HEAD_DIM
    scale = HEAD_DIM**-0.5
    gm_ref[...] = low(dot(join(blocks), w[:, 3 * cols :]))
    for h in range(heads):
        lo = h * HEAD_DIM
        query = qkvm[:, lo : lo + HEAD_DIM]
        key = qkvm[:, cols + lo : cols + lo + HEAD_DIM]
        value = qkvm[:, 2 * cols + lo : 2 * cols + lo + HEAD_DIM]
        for b in range(len(blocks)):
            span = slice(b * rows, (b + 1) * rows)
            probs = wide(probs_ref[h, span, :])
            grad_probs = contract_cols(gm_ref[span, lo : lo + HEAD_DIM], value)
            inner = jnp.sum(grad_probs * probs, axis=1, keepdims=True)
            grad_scores = low(probs * (grad_probs - inner))
            gs_ref[span, :] = grad_scores
            out_ref[span, lo : lo + HEAD_DIM] = low(dot(grad_scores, key) * scale)
        out_ref[:, cols + lo : cols + lo + HEAD_DIM] = low(
            contract_rows(gs_ref[...], query) * scale
        )
        out_ref[:, 2 * cols + lo : 2 * cols + lo + HEAD_DIM] = low(
            contract_rows(probs_ref[h], gm_ref[:, lo : lo + HEAD_DIM])
        )
    for b in range(len(blocks)):
        span = slice(b * rows, (b + 1) * rows)
        sends[b][...] = low(contract_cols(out_ref[span, :], w[:, : 3 * cols]))
    sums = jnp.sum(wide(out_ref[...]), axis=0, keepdims=True)
    sum_ref[...] = jnp.broadcast_to(sums, sum_ref.shape)


def attend_back(blocks, w, qkvm, probs):
    rows, width = blocks[0].shape
    total = rows * len(blocks)
    cols = w.shape[1] // 4
    heads = cols // HEAD_DIM
    outs = [
        ((total, 3 * cols), jnp.bfloat16),
        ((8, 3 * cols), jnp.float32),
    ] + [((rows, width), jnp.bfloat16)] * len(blocks)
    return call(
        attend_back_kernel,
        "attend_back",
        outs,
        *blocks,
        w,
        qkvm,
        probs,
        scratch=[bf16(total, total), bf16(total, cols)],
        flops=32 * heads * total * total * HEAD_DIM + 8 * total * width * cols,
    )


def attend_weights_kernel(info, g0, g1, g2, g3, dqkv, xs, qkvm, give, keep):
    cols = dqkv.shape[1] // 3
    out = contract_rows(join((g0, g1, g2, g3)), qkvm[:, 3 * cols :])
    query_key = contract_rows(xs[...], dqkv[:, : 2 * cols])
    value = contract_rows(xs[...], dqkv[:, 2 * cols :])
    value_out = jnp.concatenate([value, out], axis=1)
    is_home = jnp.full(query_key.shape, info[2], jnp.int32) == 1
    give[...] = low(jnp.where(is_home, value_out, query_key))
    keep[...] = low(jnp.where(is_home, query_key, value_out))


def attend_weights(info, g, dqkv, xs, qkvm):
    total, width = xs.shape
    cols = qkvm.shape[1] // 4
    out = ((width, 2 * cols), jnp.bfloat16)
    return call(
        attend_weights_kernel,
        "attend_weights",
        [out, out],
        ("s", info),
        *g,
        dqkv,
        xs,
        qkvm,
        flops=8 * total * width * cols,
    )


def spread_kernel(count, place, keep, came, *refs):
    extra, outs = refs[:-count], refs[-count:]
    height = keep.shape[0] // count
    for k, out in enumerate(outs):
        to = place[0] ^ k
        span = pl.ds(pl.multiple_of(to * height, height), height)
        out[:height, :] = low(wide(keep[span, :]) + wide(came[span, :]))
        if extra:
            small, sums = extra
            cols = sums.shape[1] // 3
            row = lax.broadcasted_iota(jnp.int32, (small.shape[1], cols), 0)
            mine = jnp.full(row.shape, to, jnp.int32) == place[1]
            query = jnp.where(mine & (row == 0), sums[0:1, :cols], 0.0)
            value = jnp.where(mine & (row == 1), sums[0:1, 2 * cols :], 0.0)
            out[height:, :cols] = low(small[to][:, :cols] + query + value)
            out[height:, cols:] = low(small[to][:, cols:])


def spread(place, keep, came, count, *extra):
    added = extra[0].shape[1] if extra else 0
    out = ((keep.shape[0] // count + added, keep.shape[1]), jnp.bfloat16)
    body = functools.partial(spread_kernel, count)
    return call(body, "spread", [out] * count, ("s", place), keep, came, *extra)


def total_kernel(count, *refs):
    refs[-1][...] = low(summed(refs[:count]))


def total_of(blocks, after):
    body = functools.partial(total_kernel, len(blocks))
    return call(body, "total", [(blocks[0].shape, jnp.bfloat16)], *blocks, *after)[0]


def feed_kernel(x_ref, own, other, part_ref, saved_out, saved, sem):
    unit = own.shape[1] // 3
    x = x_ref[...]
    width = x.shape[1]
    first = start(x_ref, saved_out.at[:, :width], sem.at[0])
    for side, w in enumerate((own, other)):
        lo = side * unit
        packed = dot(x, w[:, : 2 * unit])
        gate, up = packed[:, :unit], packed[:, unit:]
        phi = 0.5 + 0.5 * lax.erf(gate * (0.5**0.5))
        bell = jnp.exp(gate * gate * -0.5) * (2.0 * math.pi) ** -0.5
        gelu = gate * phi
        saved[:, lo : lo + unit] = low(gelu * up)
        saved[:, 2 * unit + lo : 3 * unit + lo] = low(up * (phi + gate * bell))
        saved[:, 4 * unit + lo : 5 * unit + lo] = low(gelu)
    second = start(saved, saved_out.at[:, width:], sem.at[1])
    part_ref[...] = low(
        contract_cols(saved[:, :unit], own[:, 2 * unit :])
        + contract_cols(saved[:, unit : 2 * unit], other[:, 2 * unit :])
    )
    first.wait()
    second.wait()


def feed(x, own, other):
    rows, width = x.shape
    unit = own.shape[1] // 3
    outs = [
        ((rows, width), jnp.bfloat16),
        ((rows, width + 6 * unit), jnp.bfloat16, "h"),
    ]
    return call(
        feed_kernel,
        "feed",
        outs,
        x,
        own,
        other,
        scratch=[bf16(rows, 6 * unit), sems(2)],
        flops=12 * rows * width * unit,
        exps=4 * rows * unit,
        limit=8,
    )


def feed_back_kernel(g_ref, own, other, saved, part_ref, packed_ref):
    g = g_ref[...]
    unit = own.shape[1] // 3
    total = None
    for side, w in enumerate((own, other)):
        lo = g.shape[1] + (2 + side) * unit
        at = 2 * side * unit
        grad = dot(g, w[:, 2 * unit :])
        packed_ref[:, at : at + unit] = low(grad * wide(saved[:, lo : lo + unit]))
        packed_ref[:, at + unit : at + 2 * unit] = low(
            grad * wide(saved[:, 2 * unit + lo : 3 * unit + lo])
        )
        term = contract_cols(packed_ref[:, at : at + 2 * unit], w[:, : 2 * unit])
        total = term if total is None else total + term
    part_ref[...] = low(total)


def feed_back(g, own, other, saved):
    rows, width = g.shape
    unit = own.shape[1] // 3
    outs = [((rows, width), jnp.bfloat16), ((rows, 4 * unit), jnp.bfloat16)]
    return call(
        feed_back_kernel,
        "feed_back",
        outs,
        g,
        own,
        other,
        saved,
        flops=12 * rows * width * unit,
        limit=8,
    )


def feed_weights_kernel(side, *refs):
    saved, g, packed, out = refs[:4], refs[4:8], refs[8:12], refs[12]
    width = g[0].shape[1]
    unit = out.shape[1] // 3
    lo = 2 * side * unit
    at = width + side * unit
    act = jnp.concatenate([s[:, at : at + unit] for s in saved], axis=0)
    out[:, 2 * unit :] = low(contract_rows(join(g), act))
    x = jnp.concatenate([s[:, :width] for s in saved], axis=0)
    packed_all = jnp.concatenate([p[:, lo : lo + 2 * unit] for p in packed], axis=0)
    out[:, : 2 * unit] = low(contract_rows(x, packed_all))


def feed_weights(side, saved, g, packed):
    rows, width = g[0].shape
    unit = packed[0].shape[1] // 4
    return call(
        functools.partial(feed_weights_kernel, side),
        "feed_weights",
        [((width, 3 * unit), jnp.bfloat16)],
        *saved,
        *g,
        *packed,
        flops=24 * rows * width * unit,
    )[0]


def small_kernel(place, *refs):
    *given, out = refs
    layers = len(given) // 4
    groups, count, both = out.shape
    cols = both // 2
    row = lax.broadcasted_iota(jnp.int32, (count, cols), 0)
    lane = lax.broadcasted_iota(jnp.int32, (count, cols), 1)
    heads = cols // HEAD_DIM
    high = jnp.zeros((count, cols), jnp.float32)
    for l in range(layers):
        top = given[4 * l + 3]
        for h in range(heads):
            at = (place[0] * layers + l) * heads + h
            high = jnp.where(lane == at, top[0:1, h : h + 1], high)
    whole = wide(low(high))
    tops = jnp.where(row == 0, whole, jnp.where(row == 1, high - whole, 0.0))
    for g in range(groups):
        span = slice(g * cols, (g + 1) * cols)
        mine = jnp.full((1, cols), place[1], jnp.int32) == g
        values = jnp.zeros((count, cols), jnp.float32)
        for l in range(layers):
            one, two, sums = given[4 * l : 4 * l + 3]
            rows = [
                one[2:3, span],
                two[2:3, span],
                one[1:2, span],
                two[1:2, span],
                one[0:1, span],
                two[0:1, span],
            ]
            if l > 0:
                query = jnp.where(mine, sums[0:1, :cols], 0.0)
                rows = [query, jnp.where(mine, sums[0:1, 2 * cols :], 0.0)] + rows
            for i, value in enumerate(reversed(rows)):
                values = jnp.where(row == 8 * l + 7 - i, value, values)
        out[g, :, :cols] = values
        out[g, :, cols:] = tops


def small_rows(place, groups, given, cols):
    shape = (groups, 2 * len(given), 2 * cols)
    return call(small_kernel, "small", [(shape, jnp.float32)], ("s", place), *given)[0]


def finish_feed_kernel(l, place, *refs):
    glu_out, down_out, token, glu, down, sem = refs[-6:]
    parts, _, unit = down.shape
    token[...] = jnp.zeros_like(token)
    near = refs[:parts]
    copies = []
    for k, block in enumerate(near):
        span = pl.ds(pl.multiple_of((place[1] ^ k) * unit, 128), unit)
        glu[k, :, 0, :] = wide(block[:, :unit])
        glu[k, :, 1, :] = wide(block[:, unit : 2 * unit])
        copies.append(start(glu.at[k], glu_out.at[l, :, :, span], sem.at[2 * k]))
        down[k] = wide(block[:, 2 * unit : 3 * unit])
        copies.append(start(down.at[k], down_out.at[l, :, span], sem.at[2 * k + 1]))
    for copy in copies:
        copy.wait()


def finish_feed(l, layers, place, near, unit, before):
    rows, parts = near[0].shape[0], len(near)
    outs = [
        ((layers, rows, 2, unit * parts), jnp.float32, "h"),
        ((layers, rows, unit * parts), jnp.float32, "h"),
        ((8, 128), jnp.float32),
    ]
    given = [("s", place), *near]
    alias = {}
    if before is not None:
        alias = {len(given): 0, len(given) + 1: 1}
        given += [("h", x) for x in before]
    return call(
        functools.partial(finish_feed_kernel, l),
        "finish_feed",
        outs,
        *given,
        scratch=[
            pltpu.VMEM((parts, rows, 2, unit), jnp.float32),
            pltpu.VMEM((parts, rows, unit), jnp.float32),
            sems(2 * parts),
        ],
        alias=alias,
    )


def choose_kernel(parts, count, at, flags, *refs):
    *blocks, out = refs
    pair = parts // 2
    row = 0
    for i in range(0, len(blocks), parts):
        for k in range(pair):
            near, far = blocks[i + k], blocks[i + pair + k]
            columns = slice(at if i else 0, None)
            near, far = wide(near[:, columns]), wide(far[:, columns])
            home = jnp.full(near.shape, flags[0], jnp.int32) == 1
            out[row : row + near.shape[0], :] = low(jnp.where(home, far, near))
            row += near.shape[0]
    for block in blocks[:parts]:
        height, _ = block.shape
        out[row : row + count, :] = block[height - count :, :]
        row += count


def choose(flags, blocks, others, count, at):
    parts = len(blocks)
    rows = sum(b[0].shape[0] for b in [blocks] + others) * (parts // 2) + parts * count
    body = functools.partial(choose_kernel, parts, count, at)
    given = [x for b in [blocks] + others for x in b]
    out = ((rows, blocks[0].shape[1]), jnp.bfloat16)
    return call(body, "choose", [out], ("s", flags), *given)[0]


def finish_attention_kernel(groups, parts, count, from_col, flags, *refs):
    qkv_out, out_out, clip_out, small_out, weights, qkv, out, clip, sem = refs[-9:]
    *given, came, weight_in = refs[:-9]
    blocks = given[:parts]
    pair = parts // 2
    height, _ = blocks[0].shape
    layers, _, rows, half = qkv.shape
    cols = half // 2
    heads = cols // HEAD_DIM
    fetched = [start(weight_in.at[l, :2], weights.at[l], sem.at[l]) for l in range(layers)]
    total, tops = None, []
    for k, block in enumerate(blocks):
        at = came.shape[0] - (parts - k) * count
        mine, theirs = wide(block[height - count :, :]), wide(came[at : at + count, :])
        both = mine[:, :cols] + theirs[:, :cols]
        total = both if total is None else total + both
        tops.append(
            jnp.maximum(
                mine[0:1, cols:] + mine[1:2, cols:], theirs[0:1, cols:] + theirs[1:2, cols:]
            )
        )
    small_out[...] = total
    home = jnp.full((rows, half), flags[0], jnp.int32) == 1
    even = jnp.full((rows, half), flags[1], jnp.int32) == 1
    home_row, even_row = home[0:1, :cols], even[0:1, :cols]
    pick_tops = [jnp.where(home_row, tops[i], tops[pair + i]) for i in range(pair)]
    first_top = jnp.where(even_row, pick_tops[0], pick_tops[1])
    second_top = jnp.where(even_row, pick_tops[1], pick_tops[0])
    lane = lax.broadcasted_iota(jnp.int32, (1, half), 1) // HEAD_DIM
    copies = []
    for l in range(layers):
        columns = slice(from_col if l else 0, None)
        near = [wide(b[:rows, columns]) for b in given[l * parts : (l + 1) * parts]]
        at, step = (pair * (height + (l - 1) * rows), rows) if l else (0, height)
        far = [wide(came[at + i * step : at + i * step + rows, :]) for i in range(pair)]
        near = [jnp.where(home, near[i], near[pair + i]) for i in range(pair)]
        query_key = [jnp.where(even, near[0], near[1]), jnp.where(even, near[1], near[0])]
        value_out = [jnp.where(even, far[0], far[1]), jnp.where(even, far[1], far[0])]
        for i in range(pair):
            place = slice(i * cols, (i + 1) * cols)
            qkv[l, 0, :, place] = query_key[i][:, :cols]
            qkv[l, 1, :, place] = query_key[i][:, cols:]
            qkv[l, 2, :, place] = value_out[i][:, :cols]
            out[l, :, place] = value_out[i][:, cols:]
        copies.append(start(qkv.at[l], qkv_out.at[l], sem.at[layers + 3 * l]))
        copies.append(start(out.at[l], out_out.at[l], sem.at[layers + 3 * l + 1]))
        top = jnp.zeros((1, half), jnp.float32)
        for i, row in enumerate((first_top, second_top)):
            for h in range(heads):
                best = None
                for g in range(groups):
                    at = (g * layers + l) * heads + h
                    value = row[:, at : at + 1]
                    best = value if best is None else jnp.maximum(best, value)
                top = jnp.where(lane == i * heads + h, best, top)
        factor = CLIP_LIMIT / jnp.maximum(top, CLIP_LIMIT)
        fetched[l].wait()
        for m in range(2):
            clip[l, :, m, :] = (wide(weights[l, m]) - STEP_SIZE * qkv[l, m]) * factor
        copies.append(start(clip.at[l], clip_out.at[l], sem.at[layers + 3 * l + 2]))
    for copy in copies:
        copy.wait()


def finish_attention(groups, count, at, flags, blocks, others, came, weight):
    layers, _, rows, half = weight.shape
    outs = [
        ((layers, 3, rows, half), jnp.float32, "h"),
        ((layers, rows, half), jnp.float32, "h"),
        ((layers, rows, 2, half), jnp.float32, "h"),
        ((count, half // 2), jnp.float32),
    ]
    return call(
        functools.partial(finish_attention_kernel, groups, len(blocks), count, at),
        "finish_attention",
        outs,
        ("s", flags),
        *[x for b in [blocks] + others for x in b],
        came,
        ("h", weight),
        scratch=[
            pltpu.VMEM((layers, 2, rows, half), weight.dtype),
            f32(layers, 3, rows, half),
            f32(layers, rows, half),
            f32(layers, rows, 2, half),
            sems(4 * layers),
        ],
    )


def both_kernel(core, own, other, out):
    out[core[0]] = own[...]
    out[1 - core[0]] = other[...]


def both_slots(core, own, other):
    out = ((2, *own.shape), own.dtype)
    return call(both_kernel, "both", [out], ("s", core), own, other)[0]


def normalised(z):
    mean = jnp.mean(z, axis=1, keepdims=True)
    centred = z - mean
    r = lax.rsqrt(jnp.mean(centred * centred, axis=1, keepdims=True) + EPSILON)
    return centred * r, r


def affine(n, vec, gain, shift):
    return n * vec[gain : gain + 1, :] + vec[shift : shift + 1, :]


def summed(refs):
    total = wide(refs[0][...])
    for ref in refs[1:]:
        total = total + wide(ref[...])
    return total


def norm_input(before, bias, parts, prev, vec):
    z = summed(parts) + vec[bias : bias + 1, :]
    if before is None:
        return z + wide(prev[...])
    return z + affine(normalised(prev[...])[0], vec, *before)


def norm_kernel(before, rows_of, p0, p1, p2, p3, prev, vec, low_ref, z_out, zs, sem):
    bias, gain, shift = rows_of
    z = norm_input(before, bias, (p0, p1, p2, p3), prev, vec)
    zs[...] = z
    copy = start(zs, z_out, sem.at[0])
    low_ref[...] = low(affine(normalised(z)[0], vec, gain, shift))
    copy.wait()


def norm(before, rows_of, parts, prev, vec):
    shape = parts[0].shape
    outs = [(shape, jnp.bfloat16), (shape, jnp.float32, "h")]
    return call(
        functools.partial(norm_kernel, before, rows_of),
        "norm",
        outs,
        *parts,
        prev,
        vec,
        scratch=[f32(*shape), sems(1)],
        flops=prev.size,
    )


def norm_grad(grad, n, r, gain, dz_out, low_ref, stat_ref, dzs, sem):
    scaled = grad * gain
    one = jnp.mean(scaled, axis=1, keepdims=True)
    two = jnp.mean(scaled * n, axis=1, keepdims=True)
    dz = (scaled - one - n * two) * r
    dz_low = low(dz)
    dzs[...] = dz
    copy = start(dzs, dz_out, sem)
    low_ref[...] = dz_low
    stat_ref[0:1, :] = jnp.sum(grad * n, axis=0, keepdims=True)
    stat_ref[1:2, :] = jnp.sum(grad, axis=0, keepdims=True)
    stat_ref[2:3, :] = jnp.sum(wide(dz_low), axis=0, keepdims=True)
    stat_ref[3:, :] = jnp.zeros((stat_ref.shape[0] - 3, stat_ref.shape[1]), jnp.float32)
    copy.wait()


def norm_back_kernel(gain_row, p0, p1, p2, p3, skip, z, vec, *refs):
    *outs, dzs, sem = refs
    grad = summed((p0, p1, p2, p3)) + skip[...]
    n, r = normalised(z[...])
    norm_grad(grad, n, r, vec[gain_row : gain_row + 1, :], *outs, dzs, sem.at[0])


def grad_outs(shape):
    return [
        (shape, jnp.float32, "h"),
        (shape, jnp.bfloat16),
        ((8, shape[1]), jnp.float32),
    ]


def norm_back(gain_row, parts, skip, z, vec):
    shape = skip.shape
    return call(
        functools.partial(norm_back_kernel, gain_row),
        "norm_back",
        grad_outs(shape),
        *parts,
        skip,
        z,
        vec,
        scratch=[f32(*shape), sems(1)],
        flops=skip.size,
    )


def turn_kernel(before, rows_of, info, p0, p1, p2, p3, prev, vec, cot, out_ref, *refs):
    *outs, dzs, sem = refs
    bias, gain, shift = rows_of
    z = norm_input(before, bias, (p0, p1, p2, p3), prev, vec)
    n, r = normalised(z)
    rows = z.shape[0]
    ok = info[0] * rows + lax.broadcasted_iota(jnp.int32, (rows, 1), 0) < info[1]
    out_ref[...] = low(jnp.where(ok, affine(n, vec, gain, shift), 0.0))
    grad = jnp.where(ok, wide(cot[...]), 0.0)
    norm_grad(grad, n, r, vec[gain : gain + 1, :], *outs, dzs, sem.at[0])


def turn(before, rows_of, info, parts, prev, vec, cot):
    shape = prev.shape
    outs = [(shape, jnp.bfloat16)] + grad_outs(shape)
    return call(
        functools.partial(turn_kernel, before, rows_of),
        "turn",
        outs,
        ("s", info),
        *parts,
        prev,
        vec,
        cot,
        scratch=[f32(*shape), sems(1)],
        flops=prev.size,
    )


def shards(
    tokens,
    cotangent,
    lengths,
    dealing,
    qkv_weight,
    out_weight,
    glu_weight,
    down_weight,
    biases,
    gains,
):
    slots, rows, width = tokens.shape
    layers = qkv_weight.shape[0]
    parts = lax.axis_size("ctx")
    cores = lax.axis_size("heads")
    groups = lax.axis_size("dp")
    part = lax.axis_index("ctx")
    core = lax.axis_index("heads")
    group = lax.axis_index("dp")
    local_rows = qkv_weight.shape[1]
    half = qkv_weight.shape[3]
    cols = half * cores // parts
    local_heads = cols // HEAD_DIM
    quarter = glu_weight.shape[3] // parts
    per_core = parts // cores
    home = part // per_core == core
    offset = (part % per_core) * cols

    def swap(x):
        return lax.ppermute(x, "heads", [(j, cores - 1 - j) for j in range(cores)])

    def hop(x, k):
        return lax.ppermute(x, "ctx", [(j, j ^ k) for j in range(parts)])

    def hops(blocks):
        return [blocks[0]] + [hop(blocks[k], k) for k in range(1, parts)]

    def own_first(work, blocks, extras):
        done = [work(blocks[0], extras[0])]
        for block, extra in zip(blocks[1:], extras[1:]):
            block, _ = lax.optimization_barrier((block, done[-1][0]))
            done.append(work(block, extra))
        return zip(*done)

    def behind(blocks, staged):
        return [tie(blocks[0], staged[0])] + blocks[1:]

    def gather(x):
        return hops([x] * parts)

    def tie(x, *others):
        return lax.optimization_barrier((x, *others))[0]

    value_out = jnp.concatenate(
        [
            lax.dynamic_slice_in_dim(qkv_weight[:, :, 2, :], offset, cols, 2),
            lax.dynamic_slice_in_dim(out_weight, offset, cols, 2),
        ],
        axis=2,
    )
    query_key = jnp.concatenate(
        [
            lax.dynamic_slice_in_dim(qkv_weight[:, :, 0, :], offset, cols, 2),
            lax.dynamic_slice_in_dim(qkv_weight[:, :, 1, :], offset, cols, 2),
        ],
        axis=2,
    )
    attn_shard = jnp.where(home, query_key, swap(value_out))
    attn_first, attn_shard_later = attn_shard[0], [attn_shard[l] for l in range(1, layers)]
    glu_part = lax.dynamic_slice_in_dim(glu_weight, part * quarter, quarter, 3)
    down_part = lax.dynamic_slice_in_dim(down_weight, part * quarter, quarter, 2)

    def over_dp(x):
        return lax.all_gather(x, "dp", axis=0, tiled=True)

    direct = groups <= 4 and local_rows == cols
    place = jnp.stack([group, part]).astype(jnp.int32)

    def hop_dp(x, k):
        return lax.ppermute(x, "dp", [(j, j ^ k) for j in range(groups)])

    feed_full = [None] * layers
    attn_full = [None] * layers
    tokens_own = lax.dynamic_index_in_dim(tokens, core, 0, keepdims=False)
    feed_shard = [
        jnp.concatenate([glu_part[l, :, 0], glu_part[l, :, 1], down_part[l]], axis=1)
        for l in range(layers)
    ]
    early = over_dp(jnp.concatenate([feed_shard[0]] + attn_shard_later, axis=1))
    if direct:
        low_zero = gather(tokens_own)
        own = lax.all_gather(attn_first, "dp", axis=0, tiled=True)
    else:
        own = over_dp(attn_first)
        low_zero = gather(tokens_own)
    attn_full[0] = (own, swap(own), 0)
    late = [over_dp(lax.optimization_barrier((x, own))[0]) for x in feed_shard[1:]]

    slot = group * slots + core
    slot_ids = jnp.arange(lengths.shape[0], dtype=jnp.int32)
    sequence = jnp.sum(jnp.where(slot_ids == slot, dealing, 0))
    length = jnp.sum(jnp.where(slot_ids == sequence, lengths, 0))
    info = [
        jnp.stack([part, length, home, jnp.int32(0)]).astype(
            jnp.int32
        )
        for l in range(layers)
    ]
    slopes = lax.dynamic_slice_in_dim(
        jnp.array(alibi_slopes(HEADS), jnp.float32), part * local_heads, local_heads
    )
    vec = jnp.concatenate([biases, gains], axis=1).reshape(layers * 8, width)
    qv = lax.dynamic_slice_in_dim(biases[:, :2], part * cols, cols, 2)
    qkv_bias = jnp.concatenate([qv[:, :1], jnp.zeros_like(qv[:, :1]), qv[:, 1:]], axis=2)

    prev, before = tokens_own, None
    low_own = tokens_own
    saved = []
    tops = []
    for l in range(layers):
        v = 8 * l
        x_low = low_zero if l == 0 else gather(low_own)
        xs, qkvm, probs, attn_w, top, *sends = attend(
            info[l],
            slopes,
            x_low,
            *attn_full[l],
            qkv_bias[l],
            1,
        )
        tops.append(top)
        near = stage([tie(prev, sends[0]), vec])
        hidden_low, z_one = norm(before, (v + 2, v + 6, v + 4), behind(hops(sends), near), *near)
        feed_own = tie(early if l == 0 else late[l - 1], hidden_low if l == 0 else top)
        feed_full[l] = (feed_own, swap(feed_own))
        if l == 0:
            for n in range(1, layers):
                attn_full[n] = (*feed_full[0], 3 * quarter + 2 * cols * (n - 1))
        h_low = gather(hidden_low)
        near = stage([tie(w, hidden_low) for w in feed_full[l]], 3 * quarter)
        sends, kept = own_first(lambda h, _: feed(h, *near), h_low, h_low)
        arrived = hops(sends)
        rows_of = (v + 3, v + 7, v + 5)
        near = stage([tie(z_one, sends[0]), vec])
        arrived = behind(arrived, near)
        if l + 1 < layers:
            low_own, z_two = norm((v + 6, v + 4), rows_of, arrived, *near)
            prev, before = z_two, (v + 7, v + 5)
        else:
            cot = lax.dynamic_index_in_dim(cotangent, core, 0, keepdims=False)
            outputs, grad_two, low_two, stats_two = turn(
                (v + 6, v + 4), rows_of, info[l], arrived, *near, cot
            )
            z_two = None
        saved.append((xs, qkvm, probs, attn_w, z_one, kept, z_two))

    feed_parts = [None] * layers
    carried = None
    woven = [None] * layers

    def over_dp_sum(x):
        return lax.psum_scatter(x, "dp", scatter_dimension=0, tiled=True)

    stats = [[None] * 3 for _ in range(layers)]
    for l in reversed(range(layers)):
        v = 8 * l
        x_low, qkvm, probs, attn_w, z_one, kept, _ = saved[l]
        above = l + 1 < layers
        stats[l][1] = stats_two
        g_low = gather(low_two)
        *near, k0, k1, k2, k3 = stage(
            [tie(w, low_two) for w in (*feed_full[l], *kept)], 3 * quarter
        )
        kept = [k0, k1, k2, k3]
        sends, packed = own_first(lambda g, k: feed_back(g, *near, k), g_low, kept)
        arrived = hops(sends)
        packed = list(packed)
        packed[0], arrived[1] = lax.optimization_barrier((packed[0], arrived[1]))
        give = feed_weights(1, kept, g_low, packed)
        packed[0], arrived[2], give = lax.optimization_barrier((packed[0], arrived[2], give))
        keep = feed_weights(0, kept, g_low, packed)
        came = tie(swap(give), arrived[3])
        total = wide(keep) + wide(came)
        if above:
            total = jnp.concatenate([total, carried], axis=1)
        total = low(total)
        arrived[0] = tie(arrived[0], total)
        near = stage([tie(grad_two, sends[0]), z_one, vec])
        grad_one, low_one, stats[l][0] = norm_back(v + 6, behind(arrived, near), *near)
        feed_parts[l] = over_dp_sum(total)
        a_low = gather(low_one)
        attn_w, qkvm, probs, x_low = stage([tie(attn_w, low_one), qkvm, probs, x_low])
        dqkv, sums, *sends = attend_back(a_low, attn_w, qkvm, probs)
        if above:
            woven[l + 1] = gather(tie(feed_parts[l + 1], *a_low))
        stats[l][2] = sums
        arrived = hops(sends)
        give, keep = attend_weights(info[l], a_low, dqkv, x_low, qkvm)
        came = swap(give)
        if l > 0:
            arrived[0] = tie(arrived[0], keep)
            carried = wide(keep) + wide(came)
            near = stage([tie(grad_one, sends[0]), saved[l - 1][6], vec])
            grad_two, low_two, stats_two = norm_back(v - 8 + 7, behind(arrived, near), *near)

    count = layers * local_heads
    if direct:
        given = []
        for l in range(layers):
            given += [stats[l][0], stats[l][1], stats[l][2] if l else stats[l][0], tops[l]]
        small = small_rows(place, groups, given, cols)
        terms = list(spread(place, keep, came, groups, small, sums))
        terms[1:] = [hop_dp(terms[k], k) for k in range(1, groups)]
        grad = grad_one + sum(wide(a) for a in arrived)
    else:
        grad = grad_one + sum(wide(a) for a in arrived)
        empty = jnp.zeros((width,), jnp.float32)
        small = []
        for l in range(layers):
            one, two, sums = stats[l]
            small += [
                lax.dynamic_update_slice_in_dim(empty, sums[0, lo : lo + cols], part * cols, 0)
                for lo in (0, 2 * cols)
            ]
            small += [one[2], two[2], one[1], two[1], one[0], two[0]]
        small = jnp.stack(small).reshape(layers * 8, groups, local_rows).transpose(1, 0, 2)
        small = jnp.pad(small, ((0, 0), (0, 0), (0, cols - local_rows)))
        own_tops = jnp.stack([t[0, :local_heads] for t in tops]).reshape(-1)
        high = wide(low(own_tops))
        pair = jnp.stack([high, own_tops - high])
        slots_of = jnp.zeros((layers * 8, cols), jnp.float32)
        slots_of = lax.dynamic_update_slice(slots_of, pair, (0, group * count))
        slots_of = jnp.broadcast_to(slots_of[None], (groups,) + slots_of.shape)
        small = jnp.concatenate([small, slots_of], axis=2)
        total = wide(keep) + wide(came)
        payload = jnp.concatenate([total.reshape(groups, local_rows, 2 * cols), small], axis=1)
        last = lax.psum_scatter(low(payload), "dp", scatter_dimension=0, tiled=False)
    core_ref = core.astype(jnp.int32)[None]
    out_tokens = both_slots(core_ref, outputs, swap(outputs))
    grad_tokens = both_slots(core_ref, grad, swap(grad))
    result, tokens = None, []
    for l in reversed(range(1, layers)):
        *result, token = finish_feed(l, layers, place, woven[l], quarter, result)
        tokens.append(token)
    near = [feed_parts[0]] + [hop(feed_parts[0], k) for k in (1, 2)]
    if direct:
        tied = lax.optimization_barrier((*terms, grad_tokens, out_tokens, *near))
        grad_tokens, out_tokens, *near = tied[groups:]
        last = total_of(tied[:groups], tokens)
    shared = gather(last)
    rest, last = lax.optimization_barrier((near[0], last))
    near += [hop(rest, k) for k in range(len(near), parts)]
    shared = [last] + shared[1:]
    tied = lax.optimization_barrier((*shared, *near))
    shared, near = list(tied[:parts]), list(tied[parts:])
    woven[0] = near
    flags = jnp.stack([home, part % per_core == 0]).astype(jnp.int32)
    small_count = layers * 8
    others = woven[: layers - 1]
    arrived = swap(choose(flags, shared, others, small_count, 3 * quarter))

    grad_qkv, grad_out, clipped_qk, small_sum = finish_attention(
        groups,
        small_count,
        3 * quarter,
        flags,
        shared,
        others,
        arrived,
        qkv_weight.transpose(0, 2, 1, 3),
    )
    small_sum = small_sum[:, :local_rows].reshape(layers, 8, local_rows)
    grad_glu, grad_down, _ = finish_feed(0, layers, place, near, quarter, result)
    return (
        out_tokens,
        grad_tokens,
        grad_qkv.transpose(0, 2, 1, 3),
        grad_out,
        grad_glu,
        grad_down,
        small_sum[:, :6],
        small_sum[:, 6:],
        clipped_qk,
    )


def solution(mesh):
    in_specs = (
        P("dp", "ctx", None),
        P("dp", "ctx", None),
        P(),
        P(),
        P(None, "dp", None, "heads"),
        P(None, "dp", "heads"),
        P(None, "dp", None, "heads"),
        P(None, "dp", "heads"),
        P(),
        P(),
    )
    out_specs = (
        P("dp", "ctx", None),
        P("dp", "ctx", None),
        P(None, "dp", None, "heads"),
        P(None, "dp", "heads"),
        P(None, "dp", None, "heads"),
        P(None, "dp", "heads"),
        P(None, None, "dp"),
        P(None, None, "dp"),
        P(None, "dp", None, "heads"),
    )
    return jax.shard_map(shards, mesh=mesh, in_specs=in_specs, out_specs=out_specs, check_vma=False)
```

```python
import functools
import math

import jax
import jax.numpy as jnp
from jax import lax
from jax.experimental import pallas as pl
from jax.experimental.pallas import tpu as pltpu
from jax.sharding import PartitionSpec as P

HEADS = 12
HEAD_DIM = 64


EPSILON = 1e-12
NEGATIVE = -1e30
CLIP_LIMIT = 4.0
STEP_SIZE = 0.0008
MIB = 1024 * 1024


def power_slopes(head_count):
    first_slope = 2.0 ** (-8.0 / head_count)
    return [first_slope ** (position + 1) for position in range(head_count)]


def alibi_slopes(head_count):
    closest = 2 ** int(math.floor(math.log2(head_count)))
    slopes = power_slopes(closest)
    slopes = slopes + power_slopes(2 * closest)[0::2][: head_count - closest]
    return slopes


def dot(a, b):
    return jnp.dot(a, b, preferred_element_type=jnp.float32)


def contract_rows(former, latter):
    return lax.dot_general(
        former, latter, (((0,), (0,)), ((), ())), preferred_element_type=jnp.float32
    )


def contract_cols(former, latter):
    return lax.dot_general(
        former, latter, (((1,), (1,)), ((), ())), preferred_element_type=jnp.float32
    )


def low(x):
    return x.astype(jnp.bfloat16)


def wide(x):
    return x.astype(jnp.float32)


def positions_of(shape, axis, rows, part):
    index = lax.broadcasted_iota(jnp.int32, shape, axis)
    shift = rows.bit_length() - 1
    return (((index >> shift) ^ part) << shift) | (index & (rows - 1))


def join(refs):
    return jnp.concatenate([r[...] for r in refs], axis=0)


def call(body, name, outs, *args, scratch=(), flops=0, exps=0, limit=16, alias=None):
    spaces = {"s": pltpu.SMEM, "h": pltpu.HBM, "d": pl.ANY, "v": pltpu.VMEM}
    args = [a if isinstance(a, tuple) else ("v", a) for a in args]
    outs = [o if len(o) == 3 else (*o, "v") for o in outs]
    values = [
        pltpu.with_memory_space_constraint(a[1], pltpu.HBM) if a[0] == "h" else a[1] for a in args
    ]
    shapes = tuple(
        pltpu.HBM(o[0], o[1]) if o[2] == "h" else jax.ShapeDtypeStruct(o[0], o[1]) for o in outs
    )
    moved = sum(v.size * v.dtype.itemsize for v in values)
    moved += sum(math.prod(o[0]) * jnp.dtype(o[1]).itemsize for o in outs)
    return pl.pallas_call(
        body,
        out_shape=shapes,
        in_specs=[pl.BlockSpec(memory_space=spaces[a[0]]) for a in args],
        out_specs=tuple(pl.BlockSpec(memory_space=spaces[o[2]]) for o in outs),
        scratch_shapes=list(scratch),
        input_output_aliases=alias or {},
        compiler_params=pltpu.CompilerParams(vmem_limit_bytes=limit * MIB),
        cost_estimate=pl.CostEstimate(flops=flops, bytes_accessed=moved, transcendentals=exps),
        name=name,
    )(*values)


def start(source, target, sem):
    copy = pltpu.make_async_copy(source, target, sem)
    copy.start()
    return copy


def bf16(*shape):
    return pltpu.VMEM(shape, jnp.bfloat16)


def f32(*shape):
    return pltpu.VMEM(shape, jnp.float32)


def sems(count):
    return pltpu.SemaphoreType.DMA((count,))


def pick(flag, one, two):
    chosen = jnp.full(one.shape, flag, jnp.int32) == 1
    return jnp.where(chosen, wide(one[...]), wide(two[...])).astype(jnp.bfloat16)


def stage_kernel(*refs):
    *refs, sem = refs
    count = len(refs) // 2
    copies = []
    for i, (source, target) in enumerate(zip(refs[:count], refs[count:])):
        if source.shape != target.shape:
            source = source.at[:, : target.shape[1]]
        copies.append(start(source, target, sem.at[i]))
    for copy in copies:
        copy.wait()


def stage(arrays, columns=None):
    outs = [
        ((a.shape[0], columns) if columns and a.shape[0] > columns // 2 else a.shape, a.dtype)
        for a in arrays
    ]
    return call(
        stage_kernel, "stage", outs, *[("h", a) for a in arrays], scratch=[sems(len(arrays))], limit=4
    )


def arrange_kernel(at, info, own, other, w, sem):
    half = w.shape[1] // 2
    columns = slice(at, at + half)

    def bring(first, second):
        one = start(first.at[:, columns], w.at[:, :half], sem.at[0])
        two = start(second.at[:, columns], w.at[:, half:], sem.at[1])
        one.wait()
        two.wait()

    @pl.when(info[2] == 1)
    def _():
        bring(own, other)

    @pl.when(info[2] == 0)
    def _():
        bring(other, own)


def arrange(info, own, other, at, cols):
    return call(
        functools.partial(arrange_kernel, at),
        "arrange",
        [((own.shape[0], 4 * cols), jnp.bfloat16)],
        ("s", info),
        ("h", own),
        ("h", other),
        scratch=[sems(2)],
        limit=4,
    )[0]


def attend_kernel(info, slope_ref, x0, x1, x2, x3, w, bias, *refs):
    xs_out, qkvm_out, probs_out, top_ref = refs[:4]
    sends = refs[4:8]
    xs, qkvm, probs_ref, sem = refs[8:]
    blocks = (x0, x1, x2, x3)
    rows = x0.shape[0]
    total = rows * len(blocks)
    cols = w.shape[1] // 4
    part, length = info[0], info[1]
    for b, ref in enumerate(blocks):
        xs[b * rows : (b + 1) * rows, :] = ref[...]
    copies = [start(xs, xs_out, sem.at[0])]
    x = xs[...]
    qkvm[:, : 3 * cols] = low(dot(x, w[:, : 3 * cols]) + bias[...])
    out_w = w[:, 3 * cols :]
    key_pos = positions_of((1, total), 1, rows, part)
    key_ok = key_pos < length
    heads = cols // HEAD_DIM
    tops = [jnp.full((1, total), NEGATIVE, jnp.float32)] * heads
    for b in range(len(blocks)):
        span = slice(b * rows, (b + 1) * rows)
        pos = ((b ^ part) * rows) + lax.broadcasted_iota(jnp.int32, (rows, 1), 0)
        distance = jnp.abs(pos - key_pos).astype(jnp.float32)
        for h in range(heads):
            lo = h * HEAD_DIM
            key = qkvm[:, cols + lo : cols + lo + HEAD_DIM]
            value = qkvm[:, 2 * cols + lo : 2 * cols + lo + HEAD_DIM]
            query = qkvm[span, lo : lo + HEAD_DIM] * jnp.bfloat16(HEAD_DIM**-0.5)
            masked = jnp.where(key_ok, contract_cols(query, key), NEGATIVE)
            valid = jnp.where(pos < length, masked, NEGATIVE)
            tops[h] = jnp.maximum(tops[h], jnp.max(valid, axis=0, keepdims=True))
            scores = masked - slope_ref[h] * distance
            row_max = jnp.max(scores, axis=1, keepdims=True)
            exponent = jnp.exp(scores - row_max)
            totals = jnp.sum(exponent, axis=1, keepdims=True)
            probs = low(exponent * (1.0 / totals))
            probs_ref[h, span, :] = probs
            qkvm[span, 3 * cols + lo : 3 * cols + lo + HEAD_DIM] = low(dot(probs, value))
        copies.append(
            start(probs_ref.at[:, span, :], probs_out.at[:, span, :], sem.at[1 + 2 * b])
        )
        copies.append(start(qkvm.at[span, :], qkvm_out.at[span, :], sem.at[2 + 2 * b]))
        sends[b][...] = low(contract_cols(qkvm[span, 3 * cols :], out_w))
    lane = lax.broadcasted_iota(jnp.int32, (8, 128), 1)
    packed = jnp.full((8, 128), NEGATIVE, jnp.float32)
    for h, top in enumerate(tops):
        packed = jnp.where(lane == h, jnp.max(top, axis=1, keepdims=True), packed)
    top_ref[...] = packed
    for copy in copies:
        copy.wait()


def attend(info, slopes, blocks, w, bias):
    rows, width = blocks[0].shape
    total = rows * len(blocks)
    cols = bias.shape[1] // 3
    heads = cols // HEAD_DIM
    outs = [
        ((total, width), jnp.bfloat16, "h"),
        ((total, 4 * cols), jnp.bfloat16, "h"),
        ((heads, total, total), jnp.bfloat16, "h"),
        ((8, 128), jnp.float32),
    ] + [((rows, width), jnp.bfloat16)] * len(blocks)
    return call(
        attend_kernel,
        "attend",
        outs,
        ("s", info),
        ("s", slopes),
        *blocks,
        w,
        bias,
        scratch=[
            bf16(total, width),
            bf16(total, 4 * cols),
            bf16(heads, total, total),
            sems(1 + 2 * len(blocks)),
        ],
        flops=16 * heads * total * total * HEAD_DIM + 8 * total * width * cols,
        exps=heads * total * total,
    )


def attend_back_kernel(g0, g1, g2, g3, w, qkvm, probs_ref, *refs):
    out_ref, sum_ref, *sends, gs_ref, gm_ref = refs
    blocks = (g0, g1, g2, g3)
    rows = g0.shape[0]
    cols = w.shape[1] // 4
    heads = cols // HEAD_DIM
    scale = HEAD_DIM**-0.5
    gm_ref[...] = low(dot(join(blocks), w[:, 3 * cols :]))
    for h in range(heads):
        lo = h * HEAD_DIM
        query = qkvm[:, lo : lo + HEAD_DIM]
        key = qkvm[:, cols + lo : cols + lo + HEAD_DIM]
        value = qkvm[:, 2 * cols + lo : 2 * cols + lo + HEAD_DIM]
        for b in range(len(blocks)):
            span = slice(b * rows, (b + 1) * rows)
            probs = wide(probs_ref[h, span, :])
            grad_probs = contract_cols(gm_ref[span, lo : lo + HEAD_DIM], value)
            mixed = qkvm[span, 3 * cols + lo : 3 * cols + lo + HEAD_DIM]
            inner = wide(gm_ref[span, lo : lo + HEAD_DIM]) * wide(mixed)
            inner = jnp.sum(inner, axis=1, keepdims=True)
            grad_scores = low(probs * (grad_probs - inner))
            gs_ref[span, :] = grad_scores
            out_ref[span, lo : lo + HEAD_DIM] = low(dot(grad_scores, key) * scale)
        out_ref[:, cols + lo : cols + lo + HEAD_DIM] = low(
            contract_rows(gs_ref[...], query) * scale
        )
        out_ref[:, 2 * cols + lo : 2 * cols + lo + HEAD_DIM] = low(
            contract_rows(probs_ref[h], gm_ref[:, lo : lo + HEAD_DIM])
        )
    for b in range(len(blocks)):
        span = slice(b * rows, (b + 1) * rows)
        sends[b][...] = low(contract_cols(out_ref[span, :], w[:, : 3 * cols]))
    sums = jnp.sum(wide(out_ref[...]), axis=0, keepdims=True)
    sum_ref[...] = jnp.broadcast_to(sums, sum_ref.shape)


def attend_back(blocks, w, qkvm, probs):
    rows, width = blocks[0].shape
    total = rows * len(blocks)
    cols = w.shape[1] // 4
    heads = cols // HEAD_DIM
    outs = [
        ((total, 3 * cols), jnp.bfloat16),
        ((8, 3 * cols), jnp.float32),
    ] + [((rows, width), jnp.bfloat16)] * len(blocks)
    return call(
        attend_back_kernel,
        "attend_back",
        outs,
        *blocks,
        w,
        qkvm,
        probs,
        scratch=[bf16(total, total), bf16(total, cols)],
        flops=32 * heads * total * total * HEAD_DIM + 8 * total * width * cols,
    )


def attend_weights_kernel(info, g0, g1, g2, g3, dqkv, xs, qkvm, give, keep):
    cols = dqkv.shape[1] // 3
    out = contract_rows(join((g0, g1, g2, g3)), qkvm[:, 3 * cols :])
    query_key = contract_rows(xs[...], dqkv[:, : 2 * cols])
    value = contract_rows(xs[...], dqkv[:, 2 * cols :])
    value_out = jnp.concatenate([value, out], axis=1)
    is_home = jnp.full(query_key.shape, info[2], jnp.int32) == 1
    give[...] = low(jnp.where(is_home, value_out, query_key))
    keep[...] = low(jnp.where(is_home, query_key, value_out))


def attend_weights(info, g, dqkv, xs, qkvm):
    total, width = xs.shape
    cols = qkvm.shape[1] // 4
    out = ((width, 2 * cols), jnp.bfloat16)
    return call(
        attend_weights_kernel,
        "attend_weights",
        [out, out],
        ("s", info),
        *g,
        dqkv,
        xs,
        qkvm,
        flops=8 * total * width * cols,
    )


def spread_kernel(count, place, keep, came, *refs):
    extra, outs = refs[:-count], refs[-count:]
    height = keep.shape[0] // count
    for k, out in enumerate(outs):
        to = place[0] ^ k
        span = pl.ds(pl.multiple_of(to * height, height), height)
        out[:height, :] = low(wide(keep[span, :]) + wide(came[span, :]))
        if extra:
            small, sums = extra
            cols = sums.shape[1] // 3
            row = lax.broadcasted_iota(jnp.int32, (small.shape[1], cols), 0)
            mine = jnp.full(row.shape, to, jnp.int32) == place[1]
            query = jnp.where(mine & (row == 0), sums[0:1, :cols], 0.0)
            value = jnp.where(mine & (row == 1), sums[0:1, 2 * cols :], 0.0)
            out[height:, :cols] = low(small[to][:, :cols] + query + value)
            out[height:, cols:] = low(small[to][:, cols:])


def spread(place, keep, came, count, *extra):
    added = extra[0].shape[1] if extra else 0
    out = ((keep.shape[0] // count + added, keep.shape[1]), jnp.bfloat16)
    body = functools.partial(spread_kernel, count)
    return call(body, "spread", [out] * count, ("s", place), keep, came, *extra)


def total_kernel(count, *refs):
    refs[-1][...] = low(summed(refs[:count]))


def total_of(blocks, after):
    body = functools.partial(total_kernel, len(blocks))
    return call(body, "total", [(blocks[0].shape, jnp.bfloat16)], *blocks, *after)[0]


def feed_kernel(x_ref, own, other, part_ref, saved_out, saved, sem):
    unit = own.shape[1] // 3
    x = x_ref[...]
    width = x.shape[1]
    first = start(x_ref, saved_out.at[:, :width], sem.at[0])
    for side, w in enumerate((own, other)):
        lo = side * unit
        packed = dot(x, w[:, : 2 * unit])
        gate, up = packed[:, :unit], packed[:, unit:]
        phi = 0.5 + 0.5 * lax.erf(gate * (0.5**0.5))
        bell = jnp.exp(gate * gate * -0.5) * (2.0 * math.pi) ** -0.5
        gelu = gate * phi
        saved[:, lo : lo + unit] = low(gelu * up)
        saved[:, 2 * unit + lo : 3 * unit + lo] = low(up * (phi + gate * bell))
        saved[:, 4 * unit + lo : 5 * unit + lo] = low(gelu)
    second = start(saved, saved_out.at[:, width:], sem.at[1])
    part_ref[...] = low(
        contract_cols(saved[:, :unit], own[:, 2 * unit :])
        + contract_cols(saved[:, unit : 2 * unit], other[:, 2 * unit :])
    )
    first.wait()
    second.wait()


def feed(x, own, other):
    rows, width = x.shape
    unit = own.shape[1] // 3
    outs = [
        ((rows, width), jnp.bfloat16),
        ((rows, width + 6 * unit), jnp.bfloat16, "h"),
    ]
    return call(
        feed_kernel,
        "feed",
        outs,
        x,
        own,
        other,
        scratch=[bf16(rows, 6 * unit), sems(2)],
        flops=12 * rows * width * unit,
        exps=4 * rows * unit,
        limit=8,
    )


def feed_back_kernel(g_ref, own, other, saved, part_ref, packed_ref):
    g = g_ref[...]
    unit = own.shape[1] // 3
    total = None
    for side, w in enumerate((own, other)):
        lo = g.shape[1] + (2 + side) * unit
        at = 2 * side * unit
        grad = dot(g, w[:, 2 * unit :])
        packed_ref[:, at : at + unit] = low(grad * wide(saved[:, lo : lo + unit]))
        packed_ref[:, at + unit : at + 2 * unit] = low(
            grad * wide(saved[:, 2 * unit + lo : 3 * unit + lo])
        )
        term = contract_cols(packed_ref[:, at : at + 2 * unit], w[:, : 2 * unit])
        total = term if total is None else total + term
    part_ref[...] = low(total)


def feed_back(g, own, other, saved):
    rows, width = g.shape
    unit = own.shape[1] // 3
    outs = [((rows, width), jnp.bfloat16), ((rows, 4 * unit), jnp.bfloat16)]
    return call(
        feed_back_kernel,
        "feed_back",
        outs,
        g,
        own,
        other,
        saved,
        flops=12 * rows * width * unit,
        limit=8,
    )


def feed_weights_kernel(side, *refs):
    saved, g, packed, out = refs[:4], refs[4:8], refs[8:12], refs[12]
    width = g[0].shape[1]
    unit = out.shape[1] // 3
    lo = 2 * side * unit
    at = width + side * unit
    act = jnp.concatenate([s[:, at : at + unit] for s in saved], axis=0)
    out[:, 2 * unit :] = low(contract_rows(join(g), act))
    x = jnp.concatenate([s[:, :width] for s in saved], axis=0)
    packed_all = jnp.concatenate([p[:, lo : lo + 2 * unit] for p in packed], axis=0)
    out[:, : 2 * unit] = low(contract_rows(x, packed_all))


def feed_weights(side, saved, g, packed):
    rows, width = g[0].shape
    unit = packed[0].shape[1] // 4
    return call(
        functools.partial(feed_weights_kernel, side),
        "feed_weights",
        [((width, 3 * unit), jnp.bfloat16)],
        *saved,
        *g,
        *packed,
        flops=24 * rows * width * unit,
    )[0]


def small_kernel(place, *refs):
    *given, out = refs
    layers = len(given) // 4
    groups, count, both = out.shape
    cols = both // 2
    row = lax.broadcasted_iota(jnp.int32, (count, cols), 0)
    lane = lax.broadcasted_iota(jnp.int32, (count, cols), 1)
    heads = cols // HEAD_DIM
    high = jnp.zeros((count, cols), jnp.float32)
    for l in range(layers):
        top = given[4 * l + 3]
        for h in range(heads):
            at = (place[0] * layers + l) * heads + h
            high = jnp.where(lane == at, top[0:1, h : h + 1], high)
    whole = wide(low(high))
    tops = jnp.where(row == 0, whole, jnp.where(row == 1, high - whole, 0.0))
    for g in range(groups):
        span = slice(g * cols, (g + 1) * cols)
        mine = jnp.full((1, cols), place[1], jnp.int32) == g
        values = jnp.zeros((count, cols), jnp.float32)
        for l in range(layers):
            one, two, sums = given[4 * l : 4 * l + 3]
            rows = [
                one[2:3, span],
                two[2:3, span],
                one[1:2, span],
                two[1:2, span],
                one[0:1, span],
                two[0:1, span],
            ]
            if l > 0:
                query = jnp.where(mine, sums[0:1, :cols], 0.0)
                rows = [query, jnp.where(mine, sums[0:1, 2 * cols :], 0.0)] + rows
            for i, value in enumerate(reversed(rows)):
                values = jnp.where(row == 8 * l + 7 - i, value, values)
        out[g, :, :cols] = values
        out[g, :, cols:] = tops


def small_rows(place, groups, given, cols):
    shape = (groups, 2 * len(given), 2 * cols)
    return call(small_kernel, "small", [(shape, jnp.float32)], ("s", place), *given)[0]


def finish_feed_kernel(l, place, *refs):
    glu_out, down_out, token, glu, down, sem = refs[-6:]
    parts, _, unit = down.shape
    token[...] = jnp.zeros_like(token)
    near = refs[:parts]
    copies = []
    for k, block in enumerate(near):
        span = pl.ds(pl.multiple_of((place[1] ^ k) * unit, 128), unit)
        glu[k, :, 0, :] = wide(block[:, :unit])
        glu[k, :, 1, :] = wide(block[:, unit : 2 * unit])
        copies.append(start(glu.at[k], glu_out.at[l, :, :, span], sem.at[2 * k]))
        down[k] = wide(block[:, 2 * unit : 3 * unit])
        copies.append(start(down.at[k], down_out.at[l, :, span], sem.at[2 * k + 1]))
    for copy in copies:
        copy.wait()


def finish_feed(l, layers, place, near, unit, before):
    rows, parts = near[0].shape[0], len(near)
    outs = [
        ((layers, rows, 2, unit * parts), jnp.float32, "h"),
        ((layers, rows, unit * parts), jnp.float32, "h"),
        ((8, 128), jnp.float32),
    ]
    given = [("s", place), *near]
    alias = {}
    if before is not None:
        alias = {len(given): 0, len(given) + 1: 1}
        given += [("h", x) for x in before]
    return call(
        functools.partial(finish_feed_kernel, l),
        "finish_feed",
        outs,
        *given,
        scratch=[
            pltpu.VMEM((parts, rows, 2, unit), jnp.float32),
            pltpu.VMEM((parts, rows, unit), jnp.float32),
            sems(2 * parts),
        ],
        alias=alias,
    )


def choose_kernel(parts, count, at, flags, *refs):
    *blocks, out = refs
    pair = parts // 2
    row = 0
    for i in range(0, len(blocks), parts):
        for k in range(pair):
            near, far = blocks[i + k], blocks[i + pair + k]
            columns = slice(at if i else 0, None)
            near, far = wide(near[:, columns]), wide(far[:, columns])
            home = jnp.full(near.shape, flags[0], jnp.int32) == 1
            out[row : row + near.shape[0], :] = low(jnp.where(home, far, near))
            row += near.shape[0]
    for block in blocks[:parts]:
        height, _ = block.shape
        out[row : row + count, :] = block[height - count :, :]
        row += count


def choose(flags, blocks, others, count, at):
    parts = len(blocks)
    rows = sum(b[0].shape[0] for b in [blocks] + others) * (parts // 2) + parts * count
    body = functools.partial(choose_kernel, parts, count, at)
    given = [x for b in [blocks] + others for x in b]
    out = ((rows, blocks[0].shape[1]), jnp.bfloat16)
    return call(body, "choose", [out], ("s", flags), *given)[0]


def finish_attention_kernel(groups, parts, count, from_col, flags, *refs):
    qkv_out, out_out, clip_out, bias_out, gain_out, weights, qkv, out, clip, sem = refs[-10:]
    *given, came, weight_in = refs[:-10]
    blocks = given[:parts]
    pair = parts // 2
    height, _ = blocks[0].shape
    layers, _, rows, half = qkv.shape
    cols = half // 2
    heads = cols // HEAD_DIM
    fetched = [start(weight_in.at[l, :2], weights.at[l], sem.at[l]) for l in range(layers)]
    total, tops = None, []
    for k, block in enumerate(blocks):
        at = came.shape[0] - (parts - k) * count
        mine, theirs = wide(block[height - count :, :]), wide(came[at : at + count, :])
        both = mine[:, :cols] + theirs[:, :cols]
        total = both if total is None else total + both
        tops.append(
            jnp.maximum(
                mine[0:1, cols:] + mine[1:2, cols:], theirs[0:1, cols:] + theirs[1:2, cols:]
            )
        )
    for l in range(layers):
        for i in range(bias_out.shape[0]):
            bias_out[i, l : l + 1, :] = total[8 * l + i : 8 * l + i + 1, : bias_out.shape[2]]
        gains = bias_out.shape[0] + 8 * l
        gain_out[l] = total[gains : 8 * (l + 1), : gain_out.shape[2]]
    home = jnp.full((rows, half), flags[0], jnp.int32) == 1
    even = jnp.full((rows, half), flags[1], jnp.int32) == 1
    home_row, even_row = home[0:1, :cols], even[0:1, :cols]
    pick_tops = [jnp.where(home_row, tops[i], tops[pair + i]) for i in range(pair)]
    first_top = jnp.where(even_row, pick_tops[0], pick_tops[1])
    second_top = jnp.where(even_row, pick_tops[1], pick_tops[0])
    lane = lax.broadcasted_iota(jnp.int32, (1, half), 1) // HEAD_DIM
    copies = []
    for l in range(layers):
        columns = slice(from_col if l else 0, None)
        near = [wide(b[:rows, columns]) for b in given[l * parts : (l + 1) * parts]]
        at, step = (pair * (height + (l - 1) * rows), rows) if l else (0, height)
        far = [wide(came[at + i * step : at + i * step + rows, :]) for i in range(pair)]
        near = [jnp.where(home, near[i], near[pair + i]) for i in range(pair)]
        query_key = [jnp.where(even, near[0], near[1]), jnp.where(even, near[1], near[0])]
        value_out = [jnp.where(even, far[0], far[1]), jnp.where(even, far[1], far[0])]
        for i in range(pair):
            place = slice(i * cols, (i + 1) * cols)
            qkv[l, 0, :, place] = query_key[i][:, :cols]
            qkv[l, 1, :, place] = query_key[i][:, cols:]
            qkv[l, 2, :, place] = value_out[i][:, :cols]
            out[l, :, place] = value_out[i][:, cols:]
        copies.append(start(qkv.at[l], qkv_out.at[l], sem.at[layers + 3 * l]))
        copies.append(start(out.at[l], out_out.at[l], sem.at[layers + 3 * l + 1]))
        top = jnp.zeros((1, half), jnp.float32)
        for i, row in enumerate((first_top, second_top)):
            for h in range(heads):
                best = None
                for g in range(groups):
                    at = (g * layers + l) * heads + h
                    value = row[:, at : at + 1]
                    best = value if best is None else jnp.maximum(best, value)
                top = jnp.where(lane == i * heads + h, best, top)
        factor = CLIP_LIMIT / jnp.maximum(top, CLIP_LIMIT)
        fetched[l].wait()
        for m in range(2):
            clip[l, :, m, :] = (wide(weights[l, m]) - STEP_SIZE * qkv[l, m]) * factor
        copies.append(start(clip.at[l], clip_out.at[l], sem.at[layers + 3 * l + 2]))
    for copy in copies:
        copy.wait()


def finish_attention(groups, count, at, flags, blocks, others, came, weight):
    layers, _, rows, half = weight.shape
    outs = [
        ((layers, 3, rows, half), jnp.float32, "h"),
        ((layers, rows, half), jnp.float32, "h"),
        ((layers, rows, 2, half), jnp.float32, "h"),
        ((6, layers, rows), jnp.float32),
        ((layers, 2, rows), jnp.float32),
    ]
    return call(
        functools.partial(finish_attention_kernel, groups, len(blocks), count, at),
        "finish_attention",
        outs,
        ("s", flags),
        *[x for b in [blocks] + others for x in b],
        came,
        ("h", weight),
        scratch=[
            pltpu.VMEM((layers, 2, rows, half), weight.dtype),
            f32(layers, 3, rows, half),
            f32(layers, rows, half),
            f32(layers, rows, 2, half),
            sems(4 * layers),
        ],
    )


def both_kernel(core, own, other, out):
    out[core[0]] = own[...]
    out[1 - core[0]] = other[...]


def both_slots(core, own, other):
    out = ((2, *own.shape), own.dtype)
    return call(both_kernel, "both", [out], ("s", core), own, other)[0]


def normalised(z):
    mean = jnp.mean(z, axis=1, keepdims=True)
    centred = z - mean
    r = lax.rsqrt(jnp.mean(centred * centred, axis=1, keepdims=True) + EPSILON)
    return centred * r, r


def affine(n, vec, gain, shift):
    return n * vec[gain : gain + 1, :] + vec[shift : shift + 1, :]


def summed(refs):
    total = wide(refs[0][...])
    for ref in refs[1:]:
        total = total + wide(ref[...])
    return total


def norm_input(before, bias, parts, prev, vec):
    z = summed(parts) + vec[bias : bias + 1, :]
    if before is None:
        return z + wide(prev[...])
    return z + affine(normalised(prev[...])[0], vec, *before)


def norm_kernel(before, rows_of, p0, p1, p2, p3, prev, vec, low_ref, z_out, zs, sem):
    bias, gain, shift = rows_of
    z = norm_input(before, bias, (p0, p1, p2, p3), prev, vec)
    zs[...] = z
    copy = start(zs, z_out, sem.at[0])
    low_ref[...] = low(affine(normalised(z)[0], vec, gain, shift))
    copy.wait()


def norm(before, rows_of, parts, prev, vec):
    shape = parts[0].shape
    outs = [(shape, jnp.bfloat16), (shape, jnp.float32, "h")]
    return call(
        functools.partial(norm_kernel, before, rows_of),
        "norm",
        outs,
        *parts,
        prev,
        vec,
        scratch=[f32(*shape), sems(1)],
        flops=prev.size,
    )


def norm_grad(grad, n, r, gain, dz_out, low_ref, stat_ref, dzs, sem):
    scaled = grad * gain
    one = jnp.mean(scaled, axis=1, keepdims=True)
    two = jnp.mean(scaled * n, axis=1, keepdims=True)
    dz = (scaled - one - n * two) * r
    dz_low = low(dz)
    dzs[...] = dz
    copy = start(dzs, dz_out, sem)
    low_ref[...] = dz_low
    stat_ref[0:1, :] = jnp.sum(grad * n, axis=0, keepdims=True)
    stat_ref[1:2, :] = jnp.sum(grad, axis=0, keepdims=True)
    stat_ref[2:3, :] = jnp.sum(wide(dz_low), axis=0, keepdims=True)
    stat_ref[3:, :] = jnp.zeros((stat_ref.shape[0] - 3, stat_ref.shape[1]), jnp.float32)
    copy.wait()


def norm_back_kernel(gain_row, p0, p1, p2, p3, skip, z, vec, *refs):
    *outs, dzs, sem = refs
    grad = summed((p0, p1, p2, p3)) + skip[...]
    n, r = normalised(z[...])
    norm_grad(grad, n, r, vec[gain_row : gain_row + 1, :], *outs, dzs, sem.at[0])


def grad_outs(shape):
    return [
        (shape, jnp.float32, "h"),
        (shape, jnp.bfloat16),
        ((8, shape[1]), jnp.float32),
    ]


def norm_back(gain_row, parts, skip, z, vec):
    shape = skip.shape
    return call(
        functools.partial(norm_back_kernel, gain_row),
        "norm_back",
        grad_outs(shape),
        *parts,
        skip,
        z,
        vec,
        scratch=[f32(*shape), sems(1)],
        flops=skip.size,
    )


def turn_kernel(before, rows_of, info, p0, p1, p2, p3, prev, vec, cot, out_ref, *refs):
    *outs, dzs, sem = refs
    bias, gain, shift = rows_of
    z = norm_input(before, bias, (p0, p1, p2, p3), prev, vec)
    n, r = normalised(z)
    rows = z.shape[0]
    ok = info[0] * rows + lax.broadcasted_iota(jnp.int32, (rows, 1), 0) < info[1]
    out_ref[...] = low(jnp.where(ok, affine(n, vec, gain, shift), 0.0))
    grad = jnp.where(ok, wide(cot[...]), 0.0)
    norm_grad(grad, n, r, vec[gain : gain + 1, :], *outs, dzs, sem.at[0])


def turn(before, rows_of, info, parts, prev, vec, cot):
    shape = prev.shape
    outs = [(shape, jnp.bfloat16)] + grad_outs(shape)
    return call(
        functools.partial(turn_kernel, before, rows_of),
        "turn",
        outs,
        ("s", info),
        *parts,
        prev,
        vec,
        cot,
        scratch=[f32(*shape), sems(1)],
        flops=prev.size,
    )


def shards(
    tokens,
    cotangent,
    lengths,
    dealing,
    qkv_weight,
    out_weight,
    glu_weight,
    down_weight,
    biases,
    gains,
):
    slots, rows, width = tokens.shape
    layers = qkv_weight.shape[0]
    parts = lax.axis_size("ctx")
    cores = lax.axis_size("heads")
    groups = lax.axis_size("dp")
    part = lax.axis_index("ctx")
    core = lax.axis_index("heads")
    group = lax.axis_index("dp")
    local_rows = qkv_weight.shape[1]
    half = qkv_weight.shape[3]
    cols = half * cores // parts
    local_heads = cols // HEAD_DIM
    quarter = glu_weight.shape[3] // parts
    per_core = parts // cores
    home = part // per_core == core
    offset = (part % per_core) * cols

    def swap(x):
        return lax.ppermute(x, "heads", [(j, cores - 1 - j) for j in range(cores)])

    def hop(x, k):
        return lax.ppermute(x, "ctx", [(j, j ^ k) for j in range(parts)])

    def hops(blocks):
        return [blocks[0]] + [hop(blocks[k], k) for k in range(1, parts)]

    def own_first(work, blocks, extras):
        done = [work(blocks[0], extras[0])]
        for block, extra in zip(blocks[1:], extras[1:]):
            block, _ = lax.optimization_barrier((block, done[-1][0]))
            done.append(work(block, extra))
        return zip(*done)

    def behind(blocks, staged):
        return [tie(blocks[0], staged[0])] + blocks[1:]

    def gather(x):
        return hops([x] * parts)

    def tie(x, *others):
        return lax.optimization_barrier((x, *others))[0]

    value_out = jnp.concatenate(
        [
            lax.dynamic_slice_in_dim(qkv_weight[:, :, 2, :], offset, cols, 2),
            lax.dynamic_slice_in_dim(out_weight, offset, cols, 2),
        ],
        axis=2,
    )
    query_key = jnp.concatenate(
        [
            lax.dynamic_slice_in_dim(qkv_weight[:, :, 0, :], offset, cols, 2),
            lax.dynamic_slice_in_dim(qkv_weight[:, :, 1, :], offset, cols, 2),
        ],
        axis=2,
    )
    attn_shard = jnp.where(home, query_key, swap(value_out))
    attn_first, attn_shard_later = attn_shard[0], [attn_shard[l] for l in range(1, layers)]
    glu_part = lax.dynamic_slice_in_dim(glu_weight, part * quarter, quarter, 3)
    down_part = lax.dynamic_slice_in_dim(down_weight, part * quarter, quarter, 2)

    def over_dp(x):
        return lax.all_gather(x, "dp", axis=0, tiled=True)

    direct = groups <= 4 and local_rows == cols
    place = jnp.stack([group, part]).astype(jnp.int32)

    def hop_dp(x, k):
        return lax.ppermute(x, "dp", [(j, j ^ k) for j in range(groups)])

    feed_full = [None] * layers
    attn_full = [None] * layers
    tokens_own = lax.dynamic_index_in_dim(tokens, core, 0, keepdims=False)
    feed_shard = [
        jnp.concatenate([glu_part[l, :, 0], glu_part[l, :, 1], down_part[l]], axis=1)
        for l in range(layers)
    ]
    early = over_dp(jnp.concatenate([feed_shard[0]] + attn_shard_later, axis=1))
    if direct:
        low_zero = gather(tokens_own)
        own = lax.all_gather(attn_first, "dp", axis=0, tiled=True)
    else:
        own = over_dp(attn_first)
        low_zero = gather(tokens_own)
    attn_full[0] = (own, swap(own), 0)
    late = [over_dp(lax.optimization_barrier((x, own))[0]) for x in feed_shard[1:]]

    slot = group * slots + core
    slot_ids = jnp.arange(lengths.shape[0], dtype=jnp.int32)
    sequence = jnp.sum(jnp.where(slot_ids == slot, dealing, 0))
    length = jnp.sum(jnp.where(slot_ids == sequence, lengths, 0))
    info = [
        jnp.stack([part, length, home, jnp.int32(0)]).astype(
            jnp.int32
        )
        for l in range(layers)
    ]
    slopes = lax.dynamic_slice_in_dim(
        jnp.array(alibi_slopes(HEADS), jnp.float32), part * local_heads, local_heads
    )
    vec = jnp.concatenate([biases, gains], axis=1).reshape(layers * 8, width)
    qv = lax.dynamic_slice_in_dim(biases[:, :2], part * cols, cols, 2)
    qkv_bias = jnp.concatenate([qv[:, :1], jnp.zeros_like(qv[:, :1]), qv[:, 1:]], axis=2)

    prev, before = tokens_own, None
    low_own = tokens_own
    saved = []
    tops = []
    for l in range(layers):
        v = 8 * l
        own, other, at = attn_full[l]
        if l > 0:
            own, other, low_own = lax.optimization_barrier((own, other, low_own))
        x_low = low_zero if l == 0 else gather(low_own)
        attn_now = arrange(info[l], own, other, at, cols)
        xs, qkvm, probs, top, *sends = attend(info[l], slopes, x_low, attn_now, qkv_bias[l])
        tops.append(top)
        near = stage([tie(prev, sends[0]), vec])
        hidden_low, z_one = norm(before, (v + 2, v + 6, v + 4), behind(hops(sends), near), *near)
        feed_own = tie(early if l == 0 else late[l - 1], hidden_low if l == 0 else top)
        feed_full[l] = (feed_own, swap(feed_own))
        if l == 0:
            for n in range(1, layers):
                attn_full[n] = (*feed_full[0], 3 * quarter + 2 * cols * (n - 1))
        h_low = gather(hidden_low)
        near = stage([tie(w, hidden_low) for w in feed_full[l]], 3 * quarter)
        sends, kept = own_first(lambda h, _: feed(h, *near), h_low, h_low)
        arrived = hops(sends)
        rows_of = (v + 3, v + 7, v + 5)
        near = stage([tie(z_one, sends[0]), vec])
        arrived = behind(arrived, near)
        if l + 1 < layers:
            low_own, z_two = norm((v + 6, v + 4), rows_of, arrived, *near)
            prev, before = z_two, (v + 7, v + 5)
        else:
            cot = lax.dynamic_index_in_dim(cotangent, core, 0, keepdims=False)
            outputs, grad_two, low_two, stats_two = turn(
                (v + 6, v + 4), rows_of, info[l], arrived, *near, cot
            )
            z_two = None
        saved.append((xs, qkvm, probs, (own, other, at), z_one, kept, z_two))

    feed_parts = [None] * layers
    carried = None
    woven = [None] * layers

    def over_dp_sum(x):
        return lax.psum_scatter(x, "dp", scatter_dimension=0, tiled=True)

    stats = [[None] * 3 for _ in range(layers)]
    for l in reversed(range(layers)):
        v = 8 * l
        x_low, qkvm, probs, attn_w, z_one, kept, _ = saved[l]
        above = l + 1 < layers
        stats[l][1] = stats_two
        g_low = gather(low_two)
        *near, k0, k1, k2, k3 = stage(
            [tie(w, low_two) for w in (*feed_full[l], *kept)], 3 * quarter
        )
        kept = [k0, k1, k2, k3]
        sends, packed = own_first(lambda g, k: feed_back(g, *near, k), g_low, kept)
        arrived = hops(sends)
        packed = list(packed)
        packed[0], arrived[1] = lax.optimization_barrier((packed[0], arrived[1]))
        give = feed_weights(1, kept, g_low, packed)
        packed[0], arrived[2], give = lax.optimization_barrier((packed[0], arrived[2], give))
        keep = feed_weights(0, kept, g_low, packed)
        came = tie(swap(give), arrived[3])
        total = wide(keep) + wide(came)
        if above:
            total = jnp.concatenate([total, carried], axis=1)
        total = low(total)
        arrived[0] = tie(arrived[0], total)
        near = stage([tie(grad_two, sends[0]), z_one, vec])
        grad_one, low_one, stats[l][0] = norm_back(v + 6, behind(arrived, near), *near)
        feed_parts[l] = over_dp_sum(total)
        a_low = gather(low_one)
        qkvm, probs, x_low = stage([tie(qkvm, low_one), probs, x_low])
        attn_w = arrange(info[l], tie(attn_w[0], low_one), *attn_w[1:], cols)
        dqkv, sums, *sends = attend_back(a_low, attn_w, qkvm, probs)
        if above:
            woven[l + 1] = gather(tie(feed_parts[l + 1], *a_low))
        stats[l][2] = sums
        arrived = hops(sends)
        give, keep = attend_weights(info[l], a_low, dqkv, x_low, qkvm)
        came = swap(give)
        if l > 0:
            arrived[0] = tie(arrived[0], keep)
            carried = wide(keep) + wide(came)
            near = stage([tie(grad_one, sends[0]), saved[l - 1][6], vec])
            grad_two, low_two, stats_two = norm_back(v - 8 + 7, behind(arrived, near), *near)

    count = layers * local_heads
    if direct:
        given = []
        for l in range(layers):
            given += [stats[l][0], stats[l][1], stats[l][2] if l else stats[l][0], tops[l]]
        small = small_rows(place, groups, given, cols)
        terms = list(spread(place, keep, came, groups, small, sums))
        terms[1:] = [hop_dp(terms[k], k) for k in range(1, groups)]
        grad = grad_one + sum(wide(a) for a in arrived)
    else:
        grad = grad_one + sum(wide(a) for a in arrived)
        empty = jnp.zeros((width,), jnp.float32)
        small = []
        for l in range(layers):
            one, two, sums = stats[l]
            small += [
                lax.dynamic_update_slice_in_dim(empty, sums[0, lo : lo + cols], part * cols, 0)
                for lo in (0, 2 * cols)
            ]
            small += [one[2], two[2], one[1], two[1], one[0], two[0]]
        small = jnp.stack(small).reshape(layers * 8, groups, local_rows).transpose(1, 0, 2)
        small = jnp.pad(small, ((0, 0), (0, 0), (0, cols - local_rows)))
        own_tops = jnp.stack([t[0, :local_heads] for t in tops]).reshape(-1)
        high = wide(low(own_tops))
        pair = jnp.stack([high, own_tops - high])
        slots_of = jnp.zeros((layers * 8, cols), jnp.float32)
        slots_of = lax.dynamic_update_slice(slots_of, pair, (0, group * count))
        slots_of = jnp.broadcast_to(slots_of[None], (groups,) + slots_of.shape)
        small = jnp.concatenate([small, slots_of], axis=2)
        total = wide(keep) + wide(came)
        payload = jnp.concatenate([total.reshape(groups, local_rows, 2 * cols), small], axis=1)
        last = lax.psum_scatter(low(payload), "dp", scatter_dimension=0, tiled=False)
    core_ref = core.astype(jnp.int32)[None]
    out_tokens = both_slots(core_ref, outputs, swap(outputs))
    grad_tokens = both_slots(core_ref, grad, swap(grad))
    result, tokens = None, []
    for l in reversed(range(1, layers)):
        *result, token = finish_feed(l, layers, place, woven[l], quarter, result)
        tokens.append(token)
    near = [feed_parts[0]] + [hop(feed_parts[0], k) for k in (1, 2)]
    if direct:
        tied = lax.optimization_barrier((*terms, grad_tokens, out_tokens, *near))
        grad_tokens, out_tokens, *near = tied[groups:]
        last = total_of(tied[:groups], tokens)
    shared = gather(last)
    rest, last = lax.optimization_barrier((near[0], last))
    near += [hop(rest, k) for k in range(len(near), parts)]
    shared = [last] + shared[1:]
    tied = lax.optimization_barrier((*shared, *near))
    shared, near = list(tied[:parts]), list(tied[parts:])
    woven[0] = near
    flags = jnp.stack([home, part % per_core == 0]).astype(jnp.int32)
    small_count = layers * 8
    others = woven[: layers - 1]
    arrived = swap(choose(flags, shared, others, small_count, 3 * quarter))

    grad_qkv, grad_out, clipped_qk, grad_biases, grad_gains = finish_attention(
        groups,
        small_count,
        3 * quarter,
        flags,
        shared,
        others,
        arrived,
        qkv_weight.transpose(0, 2, 1, 3),
    )
    grad_glu, grad_down, _ = finish_feed(0, layers, place, near, quarter, result)
    return (
        out_tokens,
        grad_tokens,
        grad_qkv.transpose(0, 2, 1, 3),
        grad_out,
        grad_glu,
        grad_down,
        grad_biases.transpose(1, 0, 2),
        grad_gains,
        clipped_qk,
    )


def solution(mesh):
    in_specs = (
        P("dp", "ctx", None),
        P("dp", "ctx", None),
        P(),
        P(),
        P(None, "dp", None, "heads"),
        P(None, "dp", "heads"),
        P(None, "dp", None, "heads"),
        P(None, "dp", "heads"),
        P(),
        P(),
    )
    out_specs = (
        P("dp", "ctx", None),
        P("dp", "ctx", None),
        P(None, "dp", None, "heads"),
        P(None, "dp", "heads"),
        P(None, "dp", None, "heads"),
        P(None, "dp", "heads"),
        P(None, None, "dp"),
        P(None, None, "dp"),
        P(None, "dp", None, "heads"),
    )
    return jax.shard_map(shards, mesh=mesh, in_specs=in_specs, out_specs=out_specs, check_vma=False)
```

```python
import functools
import math

import jax
import jax.numpy as jnp
from jax import lax
from jax.experimental import pallas as pl
from jax.experimental.pallas import tpu as pltpu
from jax.sharding import PartitionSpec as P

HEADS = 12
HEAD_DIM = 64


EPSILON = 1e-12
NEGATIVE = -1e30
CLIP_LIMIT = 4.0
STEP_SIZE = 0.0008
MIB = 1024 * 1024


def power_slopes(head_count):
    first_slope = 2.0 ** (-8.0 / head_count)
    return [first_slope ** (position + 1) for position in range(head_count)]


def alibi_slopes(head_count):
    closest = 2 ** int(math.floor(math.log2(head_count)))
    slopes = power_slopes(closest)
    slopes = slopes + power_slopes(2 * closest)[0::2][: head_count - closest]
    return slopes


def dot(a, b):
    return jnp.dot(a, b, preferred_element_type=jnp.float32)


def contract_rows(former, latter):
    return lax.dot_general(
        former, latter, (((0,), (0,)), ((), ())), preferred_element_type=jnp.float32
    )


def contract_cols(former, latter):
    return lax.dot_general(
        former, latter, (((1,), (1,)), ((), ())), preferred_element_type=jnp.float32
    )


def low(x):
    return x.astype(jnp.bfloat16)


def wide(x):
    return x.astype(jnp.float32)


def positions_of(shape, axis, rows, part):
    index = lax.broadcasted_iota(jnp.int32, shape, axis)
    shift = rows.bit_length() - 1
    return (((index >> shift) ^ part) << shift) | (index & (rows - 1))


def join(refs):
    return jnp.concatenate([r[...] for r in refs], axis=0)


def call(body, name, outs, *args, scratch=(), flops=0, exps=0, limit=16, alias=None):
    spaces = {"s": pltpu.SMEM, "h": pltpu.HBM, "d": pl.ANY, "v": pltpu.VMEM}
    args = [a if isinstance(a, tuple) else ("v", a) for a in args]
    outs = [o if len(o) == 3 else (*o, "v") for o in outs]
    values = [
        pltpu.with_memory_space_constraint(a[1], pltpu.HBM) if a[0] == "h" else a[1] for a in args
    ]
    shapes = tuple(
        pltpu.HBM(o[0], o[1]) if o[2] == "h" else jax.ShapeDtypeStruct(o[0], o[1]) for o in outs
    )
    moved = sum(v.size * v.dtype.itemsize for v in values)
    moved += sum(math.prod(o[0]) * jnp.dtype(o[1]).itemsize for o in outs)
    return pl.pallas_call(
        body,
        out_shape=shapes,
        in_specs=[pl.BlockSpec(memory_space=spaces[a[0]]) for a in args],
        out_specs=tuple(pl.BlockSpec(memory_space=spaces[o[2]]) for o in outs),
        scratch_shapes=list(scratch),
        input_output_aliases=alias or {},
        compiler_params=pltpu.CompilerParams(vmem_limit_bytes=limit * MIB),
        cost_estimate=pl.CostEstimate(flops=flops, bytes_accessed=moved, transcendentals=exps),
        name=name,
    )(*values)


def start(source, target, sem):
    copy = pltpu.make_async_copy(source, target, sem)
    copy.start()
    return copy


def bf16(*shape):
    return pltpu.VMEM(shape, jnp.bfloat16)


def f32(*shape):
    return pltpu.VMEM(shape, jnp.float32)


def sems(count):
    return pltpu.SemaphoreType.DMA((count,))


def pick(flag, one, two):
    chosen = jnp.full(one.shape, flag, jnp.int32) == 1
    return jnp.where(chosen, wide(one[...]), wide(two[...])).astype(jnp.bfloat16)


def stage_kernel(*refs):
    *refs, sem = refs
    count = len(refs) // 2
    copies = []
    for i, (source, target) in enumerate(zip(refs[:count], refs[count:])):
        if source.shape != target.shape:
            source = source.at[:, : target.shape[1]]
        copies.append(start(source, target, sem.at[i]))
    for copy in copies:
        copy.wait()


def stage(arrays, columns=None):
    outs = [
        ((a.shape[0], columns) if columns and a.shape[0] > columns // 2 else a.shape, a.dtype)
        for a in arrays
    ]
    return call(
        stage_kernel, "stage", outs, *[("h", a) for a in arrays], scratch=[sems(len(arrays))], limit=4
    )


def arrange_kernel(at, info, own, other, w, sem):
    half = w.shape[1] // 2
    columns = slice(at, at + half)

    def bring(first, second):
        one = start(first.at[:, columns], w.at[:, :half], sem.at[0])
        two = start(second.at[:, columns], w.at[:, half:], sem.at[1])
        one.wait()
        two.wait()

    @pl.when(info[2] == 1)
    def _():
        bring(own, other)

    @pl.when(info[2] == 0)
    def _():
        bring(other, own)


def arrange(info, own, other, at, cols):
    return call(
        functools.partial(arrange_kernel, at),
        "arrange",
        [((own.shape[0], 4 * cols), jnp.bfloat16)],
        ("s", info),
        ("h", own),
        ("h", other),
        scratch=[sems(2)],
        limit=4,
    )[0]


def attend_kernel(info, slope_ref, x0, x1, x2, x3, w, bias, *refs):
    xs_out, qkvm_out, probs_out, top_ref = refs[:4]
    sends = refs[4:8]
    xs, qkvm, probs_ref, sem = refs[8:]
    blocks = (x0, x1, x2, x3)
    rows = x0.shape[0]
    total = rows * len(blocks)
    cols = w.shape[1] // 4
    part, length = info[0], info[1]
    for b, ref in enumerate(blocks):
        xs[b * rows : (b + 1) * rows, :] = ref[...]
    copies = [start(xs, xs_out, sem.at[0])]
    x = xs[...]
    qkvm[:, : 3 * cols] = low(dot(x, w[:, : 3 * cols]) + bias[...])
    out_w = w[:, 3 * cols :]
    key_pos = positions_of((1, total), 1, rows, part)
    key_ok = key_pos < length
    heads = cols // HEAD_DIM
    tops = [jnp.full((1, total), NEGATIVE, jnp.float32)] * heads
    for b in range(len(blocks)):
        span = slice(b * rows, (b + 1) * rows)
        pos = ((b ^ part) * rows) + lax.broadcasted_iota(jnp.int32, (rows, 1), 0)
        distance = jnp.abs(pos - key_pos).astype(jnp.float32)
        for h in range(heads):
            lo = h * HEAD_DIM
            key = qkvm[:, cols + lo : cols + lo + HEAD_DIM]
            value = qkvm[:, 2 * cols + lo : 2 * cols + lo + HEAD_DIM]
            query = qkvm[span, lo : lo + HEAD_DIM] * jnp.bfloat16(HEAD_DIM**-0.5)
            masked = jnp.where(key_ok, contract_cols(query, key), NEGATIVE)
            valid = jnp.where(pos < length, masked, NEGATIVE)
            tops[h] = jnp.maximum(tops[h], jnp.max(valid, axis=0, keepdims=True))
            scores = masked - slope_ref[h] * distance
            row_max = jnp.max(scores, axis=1, keepdims=True)
            exponent = jnp.exp(scores - row_max)
            totals = jnp.sum(exponent, axis=1, keepdims=True)
            probs = low(exponent * (1.0 / totals))
            probs_ref[h, span, :] = probs
            qkvm[span, 3 * cols + lo : 3 * cols + lo + HEAD_DIM] = low(dot(probs, value))
        copies.append(
            start(probs_ref.at[:, span, :], probs_out.at[:, span, :], sem.at[1 + 2 * b])
        )
        copies.append(start(qkvm.at[span, :], qkvm_out.at[span, :], sem.at[2 + 2 * b]))
        sends[b][...] = low(contract_cols(qkvm[span, 3 * cols :], out_w))
    lane = lax.broadcasted_iota(jnp.int32, (8, 128), 1)
    packed = jnp.full((8, 128), NEGATIVE, jnp.float32)
    for h, top in enumerate(tops):
        packed = jnp.where(lane == h, jnp.max(top, axis=1, keepdims=True), packed)
    top_ref[...] = packed
    for copy in copies:
        copy.wait()


def attend(info, slopes, blocks, w, bias):
    rows, width = blocks[0].shape
    total = rows * len(blocks)
    cols = bias.shape[1] // 3
    heads = cols // HEAD_DIM
    outs = [
        ((total, width), jnp.bfloat16, "h"),
        ((total, 4 * cols), jnp.bfloat16, "h"),
        ((heads, total, total), jnp.bfloat16, "h"),
        ((8, 128), jnp.float32),
    ] + [((rows, width), jnp.bfloat16)] * len(blocks)
    return call(
        attend_kernel,
        "attend",
        outs,
        ("s", info),
        ("s", slopes),
        *blocks,
        w,
        bias,
        scratch=[
            bf16(total, width),
            bf16(total, 4 * cols),
            bf16(heads, total, total),
            sems(1 + 2 * len(blocks)),
        ],
        flops=16 * heads * total * total * HEAD_DIM + 8 * total * width * cols,
        exps=heads * total * total,
    )


def attend_back_kernel(g0, g1, g2, g3, w, qkvm, probs_ref, *refs):
    *along, out_ref, sum_ref, s0, s1, s2, s3, gs_ref, gm_ref = refs[:-1] if len(refs) > 8 else refs
    sends, copies, below = (s0, s1, s2, s3), [], 0
    if along:
        height, unit, sem = along[0].shape[0], s1.shape[1], refs[-1]
        below = along[0].shape[1] // unit * height
        for k, send in enumerate(sends[1:]):
            for j in range(below // height):
                source = along[0].at[:, j * unit : (j + 1) * unit]
                target = send.at[j * height : (j + 1) * height, :]
                copies.append(start(source, target, sem.at[3 * k + j]))
    blocks = (g0, g1, g2, g3)
    rows = g0.shape[0]
    cols = w.shape[1] // 4
    heads = cols // HEAD_DIM
    scale = HEAD_DIM**-0.5
    gm_ref[...] = low(dot(join(blocks), w[:, 3 * cols :]))
    for h in range(heads):
        lo = h * HEAD_DIM
        query = qkvm[:, lo : lo + HEAD_DIM]
        key = qkvm[:, cols + lo : cols + lo + HEAD_DIM]
        value = qkvm[:, 2 * cols + lo : 2 * cols + lo + HEAD_DIM]
        for b in range(len(blocks)):
            span = slice(b * rows, (b + 1) * rows)
            probs = wide(probs_ref[h, span, :])
            grad_probs = contract_cols(gm_ref[span, lo : lo + HEAD_DIM], value)
            mixed = qkvm[span, 3 * cols + lo : 3 * cols + lo + HEAD_DIM]
            inner = wide(gm_ref[span, lo : lo + HEAD_DIM]) * wide(mixed)
            inner = jnp.sum(inner, axis=1, keepdims=True)
            grad_scores = low(probs * (grad_probs - inner))
            gs_ref[span, :] = grad_scores
            out_ref[span, lo : lo + HEAD_DIM] = low(dot(grad_scores, key) * scale)
        out_ref[:, cols + lo : cols + lo + HEAD_DIM] = low(
            contract_rows(gs_ref[...], query) * scale
        )
        out_ref[:, 2 * cols + lo : 2 * cols + lo + HEAD_DIM] = low(
            contract_rows(probs_ref[h], gm_ref[:, lo : lo + HEAD_DIM])
        )
    for b in range(len(blocks)):
        span = slice(b * rows, (b + 1) * rows)
        send = low(contract_cols(out_ref[span, :], w[:, : 3 * cols]))
        if b and copies:
            for j in range(send.shape[1] // unit):
                place = slice(below + j * rows, below + (j + 1) * rows)
                sends[b][place, :] = send[:, j * unit : (j + 1) * unit]
        else:
            sends[b][...] = send
    sums = jnp.sum(wide(out_ref[...]), axis=0, keepdims=True)
    sum_ref[...] = jnp.broadcast_to(sums, sum_ref.shape)
    for copy in copies:
        copy.wait()


def attend_back(blocks, w, qkvm, probs, along=None):
    rows, width = blocks[0].shape
    total = rows * len(blocks)
    cols = w.shape[1] // 4
    heads = cols // HEAD_DIM
    outs = [
        ((total, 3 * cols), jnp.bfloat16),
        ((8, 3 * cols), jnp.float32),
    ] + [((rows, width), jnp.bfloat16)] * len(blocks)
    if along is not None:
        unit = along.shape[1] // 3
        packed = (3 * along.shape[0] + width // unit * rows, unit)
        outs[3:] = [(packed, jnp.bfloat16)] * (len(blocks) - 1)
    return call(
        attend_back_kernel,
        "attend_back",
        outs,
        *blocks,
        w,
        qkvm,
        probs,
        *([] if along is None else [("h", along)]),
        scratch=[bf16(total, total), bf16(total, cols)] + ([] if along is None else [sems(9)]),
        flops=32 * heads * total * total * HEAD_DIM + 8 * total * width * cols,
    )


def attend_weights_kernel(info, g0, g1, g2, g3, dqkv, xs, qkvm, give, keep):
    cols = dqkv.shape[1] // 3
    out = contract_rows(join((g0, g1, g2, g3)), qkvm[:, 3 * cols :])
    query_key = contract_rows(xs[...], dqkv[:, : 2 * cols])
    value = contract_rows(xs[...], dqkv[:, 2 * cols :])
    value_out = jnp.concatenate([value, out], axis=1)
    is_home = jnp.full(query_key.shape, info[2], jnp.int32) == 1
    give[...] = low(jnp.where(is_home, value_out, query_key))
    keep[...] = low(jnp.where(is_home, query_key, value_out))


def attend_weights(info, g, dqkv, xs, qkvm):
    total, width = xs.shape
    cols = qkvm.shape[1] // 4
    out = ((width, 2 * cols), jnp.bfloat16)
    return call(
        attend_weights_kernel,
        "attend_weights",
        [out, out],
        ("s", info),
        *g,
        dqkv,
        xs,
        qkvm,
        flops=8 * total * width * cols,
    )


def spread_kernel(count, place, keep, came, *refs):
    extra, outs = refs[:-1], [refs[-1].at[k] for k in range(count)]
    height = keep.shape[0] // count
    for to, out in enumerate(outs):
        span = slice(to * height, (to + 1) * height)
        out[:height, :] = low(wide(keep[span, :]) + wide(came[span, :]))
        if extra:
            small, sums = extra
            cols = sums.shape[1] // 3
            row = lax.broadcasted_iota(jnp.int32, (small.shape[1], cols), 0)
            mine = jnp.full(row.shape, place[1], jnp.int32) == to
            query = jnp.where(mine & (row == 0), sums[0:1, :cols], 0.0)
            value = jnp.where(mine & (row == 1), sums[0:1, 2 * cols :], 0.0)
            out[height:, :cols] = low(small[to][:, :cols] + query + value)
            out[height:, cols:] = low(small[to][:, cols:])


def spread(place, keep, came, count, *extra):
    added = extra[0].shape[1] if extra else 0
    out = ((count, keep.shape[0] // count + added, keep.shape[1]), jnp.bfloat16)
    body = functools.partial(spread_kernel, count)
    return call(body, "spread", [out], ("s", place), keep, came, *extra)[0]


def feed_kernel(x_ref, own, other, part_ref, saved_out, saved, sem):
    unit = own.shape[1] // 3
    x = x_ref[...]
    width = x.shape[1]
    first = start(x_ref, saved_out.at[:, :width], sem.at[0])
    for side, w in enumerate((own, other)):
        lo = side * unit
        packed = dot(x, w[:, : 2 * unit])
        gate, up = packed[:, :unit], packed[:, unit:]
        phi = 0.5 + 0.5 * lax.erf(gate * (0.5**0.5))
        bell = jnp.exp(gate * gate * -0.5) * (2.0 * math.pi) ** -0.5
        gelu = gate * phi
        saved[:, lo : lo + unit] = low(gelu * up)
        saved[:, 2 * unit + lo : 3 * unit + lo] = low(up * (phi + gate * bell))
        saved[:, 4 * unit + lo : 5 * unit + lo] = low(gelu)
    second = start(saved, saved_out.at[:, width:], sem.at[1])
    part_ref[...] = low(
        contract_cols(saved[:, :unit], own[:, 2 * unit :])
        + contract_cols(saved[:, unit : 2 * unit], other[:, 2 * unit :])
    )
    first.wait()
    second.wait()


def feed(x, own, other):
    rows, width = x.shape
    unit = own.shape[1] // 3
    outs = [
        ((rows, width), jnp.bfloat16),
        ((rows, width + 6 * unit), jnp.bfloat16, "h"),
    ]
    return call(
        feed_kernel,
        "feed",
        outs,
        x,
        own,
        other,
        scratch=[bf16(rows, 6 * unit), sems(2)],
        flops=12 * rows * width * unit,
        exps=4 * rows * unit,
        limit=8,
    )


def feed_back_kernel(g_ref, own, other, saved, part_ref, packed_ref):
    g = g_ref[...]
    unit = own.shape[1] // 3
    total = None
    for side, w in enumerate((own, other)):
        lo = g.shape[1] + (2 + side) * unit
        at = 2 * side * unit
        grad = dot(g, w[:, 2 * unit :])
        packed_ref[:, at : at + unit] = low(grad * wide(saved[:, lo : lo + unit]))
        packed_ref[:, at + unit : at + 2 * unit] = low(
            grad * wide(saved[:, 2 * unit + lo : 3 * unit + lo])
        )
        term = contract_cols(packed_ref[:, at : at + 2 * unit], w[:, : 2 * unit])
        total = term if total is None else total + term
    part_ref[...] = low(total)


def feed_back(g, own, other, saved):
    rows, width = g.shape
    unit = own.shape[1] // 3
    outs = [((rows, width), jnp.bfloat16), ((rows, 4 * unit), jnp.bfloat16)]
    return call(
        feed_back_kernel,
        "feed_back",
        outs,
        g,
        own,
        other,
        saved,
        flops=12 * rows * width * unit,
        limit=8,
    )


def feed_weights_kernel(side, *refs):
    saved, g, packed, out = refs[:4], refs[4:8], refs[8:12], refs[12]
    width = g[0].shape[1]
    unit = out.shape[1] // 3
    lo = 2 * side * unit
    at = width + side * unit
    act = jnp.concatenate([s[:, at : at + unit] for s in saved], axis=0)
    out[:, 2 * unit :] = low(contract_rows(join(g), act))
    x = jnp.concatenate([s[:, :width] for s in saved], axis=0)
    packed_all = jnp.concatenate([p[:, lo : lo + 2 * unit] for p in packed], axis=0)
    out[:, : 2 * unit] = low(contract_rows(x, packed_all))


def feed_weights(side, saved, g, packed):
    rows, width = g[0].shape
    unit = packed[0].shape[1] // 4
    return call(
        functools.partial(feed_weights_kernel, side),
        "feed_weights",
        [((width, 3 * unit), jnp.bfloat16)],
        *saved,
        *g,
        *packed,
        flops=24 * rows * width * unit,
    )[0]


def small_kernel(place, *refs):
    *given, out = refs
    layers = len(given) // 4
    groups, count, both = out.shape
    cols = both // 2
    row = lax.broadcasted_iota(jnp.int32, (count, cols), 0)
    lane = lax.broadcasted_iota(jnp.int32, (count, cols), 1)
    heads = cols // HEAD_DIM
    high = jnp.zeros((count, cols), jnp.float32)
    for l in range(layers):
        top = given[4 * l + 3]
        for h in range(heads):
            at = (place[0] * layers + l) * heads + h
            high = jnp.where(lane == at, top[0:1, h : h + 1], high)
    whole = wide(low(high))
    tops = jnp.where(row == 0, whole, jnp.where(row == 1, high - whole, 0.0))
    for g in range(groups):
        span = slice(g * cols, (g + 1) * cols)
        mine = jnp.full((1, cols), place[1], jnp.int32) == g
        values = jnp.zeros((count, cols), jnp.float32)
        for l in range(layers):
            one, two, sums = given[4 * l : 4 * l + 3]
            rows = [
                one[2:3, span],
                two[2:3, span],
                one[1:2, span],
                two[1:2, span],
                one[0:1, span],
                two[0:1, span],
            ]
            if l > 0:
                query = jnp.where(mine, sums[0:1, :cols], 0.0)
                rows = [query, jnp.where(mine, sums[0:1, 2 * cols :], 0.0)] + rows
            for i, value in enumerate(reversed(rows)):
                values = jnp.where(row == 8 * l + 7 - i, value, values)
        out[g, :, :cols] = values
        out[g, :, cols:] = tops


def small_rows(place, groups, given, cols):
    shape = (groups, 2 * len(given), 2 * cols)
    return call(small_kernel, "small", [(shape, jnp.float32)], ("s", place), *given)[0]


def finish_feed_kernel(l, place, *refs):
    glu_out, down_out, token, glu, down, sem = refs[-6:]
    parts, _, unit = down.shape
    token[...] = jnp.zeros_like(token)
    near = refs[:parts]
    copies = []
    for k, block in enumerate(near):
        span = pl.ds(pl.multiple_of((place[1] ^ k) * unit, 128), unit)
        rows = down.shape[1]
        if block.shape[1] == unit:
            cut = [block[j * rows : (j + 1) * rows, :] for j in range(3)]
        else:
            cut = [block[:, j * unit : (j + 1) * unit] for j in range(3)]
        glu[k, :, 0, :] = wide(cut[0])
        glu[k, :, 1, :] = wide(cut[1])
        copies.append(start(glu.at[k], glu_out.at[l, :, :, span], sem.at[2 * k]))
        down[k] = wide(cut[2])
        copies.append(start(down.at[k], down_out.at[l, :, span], sem.at[2 * k + 1]))
    for copy in copies:
        copy.wait()


def finish_feed(l, layers, place, near, unit, before):
    rows, parts = near[0].shape[0], len(near)
    outs = [
        ((layers, rows, 2, unit * parts), jnp.float32, "h"),
        ((layers, rows, unit * parts), jnp.float32, "h"),
        ((8, 128), jnp.float32),
    ]
    given = [("s", place), *near]
    alias = {}
    if before is not None:
        alias = {len(given): 0, len(given) + 1: 1}
        given += [("h", x) for x in before]
    return call(
        functools.partial(finish_feed_kernel, l),
        "finish_feed",
        outs,
        *given,
        scratch=[
            pltpu.VMEM((parts, rows, 2, unit), jnp.float32),
            pltpu.VMEM((parts, rows, unit), jnp.float32),
            sems(2 * parts),
        ],
        alias=alias,
    )


def choose_kernel(parts, count, at, total, flags, *refs):
    blocks, out = refs[:total], refs[-1]
    pair = parts // 2
    row = 0
    for i in range(0, len(blocks), parts):
        for k in range(pair):
            near, far = blocks[i + k], blocks[i + pair + k]
            columns = slice(at if i else 0, None)
            near, far = wide(near[:, columns]), wide(far[:, columns])
            home = jnp.full(near.shape, flags[0], jnp.int32) == 1
            out[row : row + near.shape[0], :] = low(jnp.where(home, far, near))
            row += near.shape[0]
    for block in blocks[:parts]:
        height, _ = block.shape
        out[row : row + count, :] = block[height - count :, :]
        row += count


def choose(flags, blocks, others, count, at, after):
    parts = len(blocks)
    rows = sum(b[0].shape[0] for b in [blocks] + others) * (parts // 2) + parts * count
    given = [x for b in [blocks] + others for x in b]
    body = functools.partial(choose_kernel, parts, count, at, len(given))
    out = ((rows, blocks[0].shape[1]), jnp.bfloat16)
    return call(body, "choose", [out], ("s", flags), *given, *after)[0]


def finish_attention_kernel(groups, parts, count, from_col, flags, *refs):
    qkv_out, out_out, clip_out, bias_out, gain_out, weights, qkv, out, clip, sem = refs[-10:]
    *given, came, weight_in = refs[:-10]
    blocks = given[:parts]
    pair = parts // 2
    height, _ = blocks[0].shape
    layers, _, rows, half = qkv.shape
    cols = half // 2
    heads = cols // HEAD_DIM
    fetched = [start(weight_in.at[l, :2], weights.at[l], sem.at[l]) for l in range(layers)]
    total, tops = None, []
    for k, block in enumerate(blocks):
        at = came.shape[0] - (parts - k) * count
        mine, theirs = wide(block[height - count :, :]), wide(came[at : at + count, :])
        both = mine[:, :cols] + theirs[:, :cols]
        total = both if total is None else total + both
        tops.append(
            jnp.maximum(
                mine[0:1, cols:] + mine[1:2, cols:], theirs[0:1, cols:] + theirs[1:2, cols:]
            )
        )
    for l in range(layers):
        for i in range(bias_out.shape[0]):
            bias_out[i, l : l + 1, :] = total[8 * l + i : 8 * l + i + 1, : bias_out.shape[2]]
        gains = bias_out.shape[0] + 8 * l
        gain_out[l] = total[gains : 8 * (l + 1), : gain_out.shape[2]]
    home = jnp.full((rows, half), flags[0], jnp.int32) == 1
    even = jnp.full((rows, half), flags[1], jnp.int32) == 1
    home_row, even_row = home[0:1, :cols], even[0:1, :cols]
    pick_tops = [jnp.where(home_row, tops[i], tops[pair + i]) for i in range(pair)]
    first_top = jnp.where(even_row, pick_tops[0], pick_tops[1])
    second_top = jnp.where(even_row, pick_tops[1], pick_tops[0])
    lane = lax.broadcasted_iota(jnp.int32, (1, half), 1) // HEAD_DIM
    copies = []
    for l in range(layers):
        columns = slice(from_col if l else 0, None)
        near = [wide(b[:rows, columns]) for b in given[l * parts : (l + 1) * parts]]
        at, step = (pair * (height + (l - 1) * rows), rows) if l else (0, height)
        far = [wide(came[at + i * step : at + i * step + rows, :]) for i in range(pair)]
        near = [jnp.where(home, near[i], near[pair + i]) for i in range(pair)]
        query_key = [jnp.where(even, near[0], near[1]), jnp.where(even, near[1], near[0])]
        value_out = [jnp.where(even, far[0], far[1]), jnp.where(even, far[1], far[0])]
        for i in range(pair):
            place = slice(i * cols, (i + 1) * cols)
            qkv[l, 0, :, place] = query_key[i][:, :cols]
            qkv[l, 1, :, place] = query_key[i][:, cols:]
            qkv[l, 2, :, place] = value_out[i][:, :cols]
            out[l, :, place] = value_out[i][:, cols:]
        copies.append(start(qkv.at[l], qkv_out.at[l], sem.at[layers + 3 * l]))
        copies.append(start(out.at[l], out_out.at[l], sem.at[layers + 3 * l + 1]))
        top = jnp.zeros((1, half), jnp.float32)
        for i, row in enumerate((first_top, second_top)):
            for h in range(heads):
                best = None
                for g in range(groups):
                    at = (g * layers + l) * heads + h
                    value = row[:, at : at + 1]
                    best = value if best is None else jnp.maximum(best, value)
                top = jnp.where(lane == i * heads + h, best, top)
        factor = CLIP_LIMIT / jnp.maximum(top, CLIP_LIMIT)
        fetched[l].wait()
        for m in range(2):
            clip[l, :, m, :] = (wide(weights[l, m]) - STEP_SIZE * qkv[l, m]) * factor
        copies.append(start(clip.at[l], clip_out.at[l], sem.at[layers + 3 * l + 2]))
    for copy in copies:
        copy.wait()


def finish_attention(groups, count, at, flags, blocks, others, came, weight):
    layers, _, rows, half = weight.shape
    outs = [
        ((layers, 3, rows, half), jnp.float32, "h"),
        ((layers, rows, half), jnp.float32, "h"),
        ((layers, rows, 2, half), jnp.float32, "h"),
        ((6, layers, rows), jnp.float32),
        ((layers, 2, rows), jnp.float32),
    ]
    return call(
        functools.partial(finish_attention_kernel, groups, len(blocks), count, at),
        "finish_attention",
        outs,
        ("s", flags),
        *[x for b in [blocks] + others for x in b],
        came,
        ("h", weight),
        scratch=[
            pltpu.VMEM((layers, 2, rows, half), weight.dtype),
            f32(layers, 3, rows, half),
            f32(layers, rows, half),
            f32(layers, rows, 2, half),
            sems(4 * layers),
        ],
    )


def add_kernel(g, own, *refs):
    *packed, out = refs
    out[...] = g[...] + wide(own[...])
    rows, width = g.shape
    unit = packed[0].shape[1]
    below = packed[0].shape[0] - width // unit * rows
    for ref in packed:
        for j in range(width // unit):
            span = slice(j * unit, (j + 1) * unit)
            out[:, span] += wide(ref[below + j * rows : below + (j + 1) * rows, :])


def add_packed(g, own, packed):
    return call(add_kernel, "add", [(g.shape, jnp.float32)], g, own, *packed)[0]


def both_kernel(core, own, other, out):
    out[core[0]] = own[...]
    out[1 - core[0]] = other[...]


def both_slots(core, own, other):
    out = ((2, *own.shape), own.dtype)
    return call(both_kernel, "both", [out], ("s", core), own, other)[0]


def normalised(z):
    mean = jnp.mean(z, axis=1, keepdims=True)
    centred = z - mean
    r = lax.rsqrt(jnp.mean(centred * centred, axis=1, keepdims=True) + EPSILON)
    return centred * r, r


def affine(n, vec, gain, shift):
    return n * vec[gain : gain + 1, :] + vec[shift : shift + 1, :]


def summed(refs):
    total = wide(refs[0][...])
    for ref in refs[1:]:
        total = total + wide(ref[...])
    return total


def norm_input(before, bias, parts, prev, vec):
    z = summed(parts) + vec[bias : bias + 1, :]
    if before is None:
        return z + wide(prev[...])
    return z + affine(normalised(prev[...])[0], vec, *before)


def norm_kernel(before, rows_of, p0, p1, p2, p3, prev, vec, low_ref, z_out, zs, sem):
    bias, gain, shift = rows_of
    z = norm_input(before, bias, (p0, p1, p2, p3), prev, vec)
    zs[...] = z
    copy = start(zs, z_out, sem.at[0])
    low_ref[...] = low(affine(normalised(z)[0], vec, gain, shift))
    copy.wait()


def norm(before, rows_of, parts, prev, vec):
    shape = parts[0].shape
    outs = [(shape, jnp.bfloat16), (shape, jnp.float32, "h")]
    return call(
        functools.partial(norm_kernel, before, rows_of),
        "norm",
        outs,
        *parts,
        prev,
        vec,
        scratch=[f32(*shape), sems(1)],
        flops=prev.size,
    )


def norm_grad(grad, n, r, gain, dz_out, low_ref, stat_ref, dzs, sem):
    scaled = grad * gain
    one = jnp.mean(scaled, axis=1, keepdims=True)
    two = jnp.mean(scaled * n, axis=1, keepdims=True)
    dz = (scaled - one - n * two) * r
    dz_low = low(dz)
    dzs[...] = dz
    copy = start(dzs, dz_out, sem)
    low_ref[...] = dz_low
    stat_ref[0:1, :] = jnp.sum(grad * n, axis=0, keepdims=True)
    stat_ref[1:2, :] = jnp.sum(grad, axis=0, keepdims=True)
    stat_ref[2:3, :] = jnp.sum(wide(dz_low), axis=0, keepdims=True)
    stat_ref[3:, :] = jnp.zeros((stat_ref.shape[0] - 3, stat_ref.shape[1]), jnp.float32)
    copy.wait()


def norm_back_kernel(gain_row, p0, p1, p2, p3, skip, z, vec, *refs):
    *outs, dzs, sem = refs
    grad = summed((p0, p1, p2, p3)) + skip[...]
    n, r = normalised(z[...])
    norm_grad(grad, n, r, vec[gain_row : gain_row + 1, :], *outs, dzs, sem.at[0])


def grad_outs(shape):
    return [
        (shape, jnp.float32, "h"),
        (shape, jnp.bfloat16),
        ((8, shape[1]), jnp.float32),
    ]


def norm_back(gain_row, parts, skip, z, vec):
    shape = skip.shape
    return call(
        functools.partial(norm_back_kernel, gain_row),
        "norm_back",
        grad_outs(shape),
        *parts,
        skip,
        z,
        vec,
        scratch=[f32(*shape), sems(1)],
        flops=skip.size,
    )


def turn_kernel(before, rows_of, info, p0, p1, p2, p3, prev, vec, cot, out_ref, *refs):
    *outs, dzs, sem = refs
    bias, gain, shift = rows_of
    z = norm_input(before, bias, (p0, p1, p2, p3), prev, vec)
    n, r = normalised(z)
    rows = z.shape[0]
    ok = info[0] * rows + lax.broadcasted_iota(jnp.int32, (rows, 1), 0) < info[1]
    out_ref[...] = low(jnp.where(ok, affine(n, vec, gain, shift), 0.0))
    grad = jnp.where(ok, wide(cot[...]), 0.0)
    norm_grad(grad, n, r, vec[gain : gain + 1, :], *outs, dzs, sem.at[0])


def turn(before, rows_of, info, parts, prev, vec, cot):
    shape = prev.shape
    outs = [(shape, jnp.bfloat16)] + grad_outs(shape)
    return call(
        functools.partial(turn_kernel, before, rows_of),
        "turn",
        outs,
        ("s", info),
        *parts,
        prev,
        vec,
        cot,
        scratch=[f32(*shape), sems(1)],
        flops=prev.size,
    )


def shards(
    tokens,
    cotangent,
    lengths,
    dealing,
    qkv_weight,
    out_weight,
    glu_weight,
    down_weight,
    biases,
    gains,
):
    slots, rows, width = tokens.shape
    layers = qkv_weight.shape[0]
    parts = lax.axis_size("ctx")
    cores = lax.axis_size("heads")
    groups = lax.axis_size("dp")
    part = lax.axis_index("ctx")
    core = lax.axis_index("heads")
    group = lax.axis_index("dp")
    local_rows = qkv_weight.shape[1]
    half = qkv_weight.shape[3]
    cols = half * cores // parts
    local_heads = cols // HEAD_DIM
    quarter = glu_weight.shape[3] // parts
    per_core = parts // cores
    home = part // per_core == core
    offset = (part % per_core) * cols

    def swap(x):
        return lax.ppermute(x, "heads", [(j, cores - 1 - j) for j in range(cores)])

    def hop(x, k):
        return lax.ppermute(x, "ctx", [(j, j ^ k) for j in range(parts)])

    def hops(blocks):
        return [blocks[0]] + [hop(blocks[k], k) for k in range(1, parts)]

    def own_first(work, blocks, extras):
        done = [work(blocks[0], extras[0])]
        for block, extra in zip(blocks[1:], extras[1:]):
            block, _ = lax.optimization_barrier((block, done[-1][0]))
            done.append(work(block, extra))
        return zip(*done)

    def behind(blocks, staged):
        return [tie(blocks[0], staged[0])] + blocks[1:]

    def gather(x):
        return hops([x] * parts)

    def tie(x, *others):
        return lax.optimization_barrier((x, *others))[0]

    value_out = jnp.concatenate(
        [
            lax.dynamic_slice_in_dim(qkv_weight[:, :, 2, :], offset, cols, 2),
            lax.dynamic_slice_in_dim(out_weight, offset, cols, 2),
        ],
        axis=2,
    )
    query_key = jnp.concatenate(
        [
            lax.dynamic_slice_in_dim(qkv_weight[:, :, 0, :], offset, cols, 2),
            lax.dynamic_slice_in_dim(qkv_weight[:, :, 1, :], offset, cols, 2),
        ],
        axis=2,
    )
    attn_shard = jnp.where(home, query_key, swap(value_out))
    attn_first, attn_shard_later = attn_shard[0], [attn_shard[l] for l in range(1, layers)]
    glu_part = lax.dynamic_slice_in_dim(glu_weight, part * quarter, quarter, 3)
    down_part = lax.dynamic_slice_in_dim(down_weight, part * quarter, quarter, 2)

    def over_dp(x):
        return lax.all_gather(x, "dp", axis=0, tiled=True)

    direct = groups <= 4 and local_rows == cols
    place = jnp.stack([group, part]).astype(jnp.int32)

    def hop_dp(x, k):
        return lax.ppermute(x, "dp", [(j, j ^ k) for j in range(groups)])

    feed_full = [None] * layers
    attn_full = [None] * layers
    tokens_own = lax.dynamic_index_in_dim(tokens, core, 0, keepdims=False)
    feed_shard = [
        jnp.concatenate([glu_part[l, :, 0], glu_part[l, :, 1], down_part[l]], axis=1)
        for l in range(layers)
    ]
    early = over_dp(jnp.concatenate([feed_shard[0]] + attn_shard_later, axis=1))
    if direct:
        low_zero = gather(tokens_own)
        own = lax.all_gather(attn_first, "dp", axis=0, tiled=True)
    else:
        own = over_dp(attn_first)
        low_zero = gather(tokens_own)
    attn_full[0] = (own, swap(own), 0)
    late = [over_dp(lax.optimization_barrier((x, own))[0]) for x in feed_shard[1:]]

    slot = group * slots + core
    slot_ids = jnp.arange(lengths.shape[0], dtype=jnp.int32)
    sequence = jnp.sum(jnp.where(slot_ids == slot, dealing, 0))
    length = jnp.sum(jnp.where(slot_ids == sequence, lengths, 0))
    info = [
        jnp.stack([part, length, home, jnp.int32(0)]).astype(
            jnp.int32
        )
        for l in range(layers)
    ]
    slopes = lax.dynamic_slice_in_dim(
        jnp.array(alibi_slopes(HEADS), jnp.float32), part * local_heads, local_heads
    )
    vec = jnp.concatenate([biases, gains], axis=1).reshape(layers * 8, width)
    qv = lax.dynamic_slice_in_dim(biases[:, :2], part * cols, cols, 2)
    qkv_bias = jnp.concatenate([qv[:, :1], jnp.zeros_like(qv[:, :1]), qv[:, 1:]], axis=2)

    prev, before = tokens_own, None
    low_own = tokens_own
    saved = []
    tops = []
    for l in range(layers):
        v = 8 * l
        own, other, at = attn_full[l]
        if l > 0:
            own, other, low_own = lax.optimization_barrier((own, other, low_own))
        x_low = low_zero if l == 0 else gather(low_own)
        attn_now = arrange(info[l], own, other, at, cols)
        xs, qkvm, probs, top, *sends = attend(info[l], slopes, x_low, attn_now, qkv_bias[l])
        tops.append(top)
        near = stage([tie(prev, sends[0]), vec])
        hidden_low, z_one = norm(before, (v + 2, v + 6, v + 4), behind(hops(sends), near), *near)
        feed_own = tie(early if l == 0 else late[l - 1], hidden_low if l == 0 else top)
        feed_full[l] = (feed_own, swap(feed_own))
        if l == 0:
            for n in range(1, layers):
                attn_full[n] = (*feed_full[0], 3 * quarter + 2 * cols * (n - 1))
        h_low = gather(hidden_low)
        near = stage([tie(w, hidden_low) for w in feed_full[l]], 3 * quarter)
        sends, kept = own_first(lambda h, _: feed(h, *near), h_low, h_low)
        arrived = hops(sends)
        rows_of = (v + 3, v + 7, v + 5)
        near = stage([tie(z_one, sends[0]), vec])
        arrived = behind(arrived, near)
        if l + 1 < layers:
            low_own, z_two = norm((v + 6, v + 4), rows_of, arrived, *near)
            prev, before = z_two, (v + 7, v + 5)
        else:
            cot = lax.dynamic_index_in_dim(cotangent, core, 0, keepdims=False)
            outputs, grad_two, low_two, stats_two = turn(
                (v + 6, v + 4), rows_of, info[l], arrived, *near, cot
            )
            z_two = None
        saved.append((xs, qkvm, probs, (own, other, at), z_one, kept, z_two))

    feed_parts = [None] * layers
    carried = None
    woven = [None] * layers

    def over_dp_sum(x):
        return lax.psum_scatter(x, "dp", scatter_dimension=0, tiled=True)

    stats = [[None] * 3 for _ in range(layers)]
    for l in reversed(range(layers)):
        v = 8 * l
        x_low, qkvm, probs, attn_w, z_one, kept, _ = saved[l]
        above = l + 1 < layers
        stats[l][1] = stats_two
        g_low = gather(low_two)
        *near, k0, k1, k2, k3 = stage(
            [tie(w, low_two) for w in (*feed_full[l], *kept)], 3 * quarter
        )
        kept = [k0, k1, k2, k3]
        sends, packed = own_first(lambda g, k: feed_back(g, *near, k), g_low, kept)
        arrived = hops(sends)
        packed = list(packed)
        packed[0], arrived[1] = lax.optimization_barrier((packed[0], arrived[1]))
        give = feed_weights(1, kept, g_low, packed)
        packed[0], arrived[2], give = lax.optimization_barrier((packed[0], arrived[2], give))
        keep = feed_weights(0, kept, g_low, packed)
        came = tie(swap(give), arrived[3])
        total = wide(keep) + wide(came)
        if above:
            total = jnp.concatenate([total, carried], axis=1)
        total = low(total)
        arrived[0] = tie(arrived[0], total)
        near = stage([tie(grad_two, sends[0]), z_one, vec])
        grad_one, low_one, stats[l][0] = norm_back(v + 6, behind(arrived, near), *near)
        feed_parts[l] = over_dp_sum(total)
        if above:
            low_one, feed_parts[l + 1] = lax.optimization_barrier((low_one, feed_parts[l + 1]))
        a_low = gather(low_one)
        qkvm, probs, x_low = stage([tie(qkvm, low_one), probs, x_low])
        attn_w = arrange(info[l], tie(attn_w[0], low_one), *attn_w[1:], cols)
        along = feed_parts[l + 1] if above and direct else None
        dqkv, sums, *sends = attend_back(a_low, attn_w, qkvm, probs, along)
        if above and not direct:
            woven[l + 1] = gather(tie(feed_parts[l + 1], *a_low))
        stats[l][2] = sums
        arrived = hops(sends)
        if above and direct:
            woven[l + 1] = [feed_parts[l + 1]] + arrived[1:]
        give, keep = attend_weights(info[l], a_low, dqkv, x_low, qkvm)
        came = swap(give)
        if l > 0:
            arrived[0] = tie(arrived[0], keep)
            carried = wide(keep) + wide(came)
            near = stage([tie(grad_one, sends[0]), saved[l - 1][6], vec])
            grad_two, low_two, stats_two = norm_back(v - 8 + 7, behind(arrived, near), *near)

    count = layers * local_heads
    if direct:
        given = []
        for l in range(layers):
            given += [stats[l][0], stats[l][1], stats[l][2] if l else stats[l][0], tops[l]]
        small = small_rows(place, groups, given, cols)
        terms = spread(place, keep, came, groups, small, sums)
        last = lax.psum_scatter(terms, "dp", scatter_dimension=0, tiled=False)
        grad = add_packed(grad_one, arrived[0], arrived[1:])
    else:
        grad = grad_one + sum(wide(a) for a in arrived)
        empty = jnp.zeros((width,), jnp.float32)
        small = []
        for l in range(layers):
            one, two, sums = stats[l]
            small += [
                lax.dynamic_update_slice_in_dim(empty, sums[0, lo : lo + cols], part * cols, 0)
                for lo in (0, 2 * cols)
            ]
            small += [one[2], two[2], one[1], two[1], one[0], two[0]]
        small = jnp.stack(small).reshape(layers * 8, groups, local_rows).transpose(1, 0, 2)
        small = jnp.pad(small, ((0, 0), (0, 0), (0, cols - local_rows)))
        own_tops = jnp.stack([t[0, :local_heads] for t in tops]).reshape(-1)
        high = wide(low(own_tops))
        pair = jnp.stack([high, own_tops - high])
        slots_of = jnp.zeros((layers * 8, cols), jnp.float32)
        slots_of = lax.dynamic_update_slice(slots_of, pair, (0, group * count))
        slots_of = jnp.broadcast_to(slots_of[None], (groups,) + slots_of.shape)
        small = jnp.concatenate([small, slots_of], axis=2)
        total = wide(keep) + wide(came)
        payload = jnp.concatenate([total.reshape(groups, local_rows, 2 * cols), small], axis=1)
        last = lax.psum_scatter(low(payload), "dp", scatter_dimension=0, tiled=False)
    core_ref = core.astype(jnp.int32)[None]
    out_tokens = both_slots(core_ref, outputs, swap(outputs))
    grad_tokens = both_slots(core_ref, grad, swap(grad))
    near = gather(feed_parts[0])
    if direct:
        upper = [x for l in range(1, layers) for x in woven[l]]
        tied = lax.optimization_barrier((last, grad_tokens, out_tokens, *near[:2], *upper))
        last, grad_tokens, out_tokens = tied[:3]
        near[:2] = tied[3 : 5]
        for l in range(1, layers):
            woven[l] = list(tied[5 + (l - 1) * parts : 5 + l * parts])
    shared = gather(last)
    result, tokens = None, []
    for l in reversed(range(1, layers)):
        *result, token = finish_feed(l, layers, place, woven[l], quarter, result)
        tokens.append(token)
    rest, last = lax.optimization_barrier((near[0], last))
    near += [hop(rest, k) for k in range(len(near), parts)]
    shared = [last] + shared[1:]
    tied = lax.optimization_barrier((*shared, *near))
    shared, near = list(tied[:parts]), list(tied[parts:])
    woven[0] = near
    flags = jnp.stack([home, part % per_core == 0]).astype(jnp.int32)
    small_count = layers * 8
    others = woven[: layers - 1]
    arrived = swap(choose(flags, shared, others, small_count, 3 * quarter, tokens))

    grad_qkv, grad_out, clipped_qk, grad_biases, grad_gains = finish_attention(
        groups,
        small_count,
        3 * quarter,
        flags,
        shared,
        others,
        arrived,
        qkv_weight.transpose(0, 2, 1, 3),
    )
    grad_glu, grad_down, _ = finish_feed(0, layers, place, near, quarter, result)
    return (
        out_tokens,
        grad_tokens,
        grad_qkv.transpose(0, 2, 1, 3),
        grad_out,
        grad_glu,
        grad_down,
        grad_biases.transpose(1, 0, 2),
        grad_gains,
        clipped_qk,
    )


def solution(mesh):
    in_specs = (
        P("dp", "ctx", None),
        P("dp", "ctx", None),
        P(),
        P(),
        P(None, "dp", None, "heads"),
        P(None, "dp", "heads"),
        P(None, "dp", None, "heads"),
        P(None, "dp", "heads"),
        P(),
        P(),
    )
    out_specs = (
        P("dp", "ctx", None),
        P("dp", "ctx", None),
        P(None, "dp", None, "heads"),
        P(None, "dp", "heads"),
        P(None, "dp", None, "heads"),
        P(None, "dp", "heads"),
        P(None, None, "dp"),
        P(None, None, "dp"),
        P(None, "dp", None, "heads"),
    )
    return jax.shard_map(shards, mesh=mesh, in_specs=in_specs, out_specs=out_specs, check_vma=False)
```

```python
import functools
import math

import jax
import jax.numpy as jnp
from jax import lax
from jax.experimental import pallas as pl
from jax.experimental.pallas import tpu as pltpu
from jax.sharding import PartitionSpec as P

HEADS = 12
HEAD_DIM = 64


EPSILON = 1e-12
NEGATIVE = -1e30
CLIP_LIMIT = 4.0
STEP_SIZE = 0.0008
MIB = 1024 * 1024


def power_slopes(head_count):
    first_slope = 2.0 ** (-8.0 / head_count)
    return [first_slope ** (position + 1) for position in range(head_count)]


def alibi_slopes(head_count):
    closest = 2 ** int(math.floor(math.log2(head_count)))
    slopes = power_slopes(closest)
    slopes = slopes + power_slopes(2 * closest)[0::2][: head_count - closest]
    return slopes


def dot(a, b):
    return jnp.dot(a, b, preferred_element_type=jnp.float32)


def contract_rows(former, latter):
    return lax.dot_general(
        former, latter, (((0,), (0,)), ((), ())), preferred_element_type=jnp.float32
    )


def contract_cols(former, latter):
    return lax.dot_general(
        former, latter, (((1,), (1,)), ((), ())), preferred_element_type=jnp.float32
    )


def low(x):
    return x.astype(jnp.bfloat16)


def wide(x):
    return x.astype(jnp.float32)


def positions_of(shape, axis, rows, part):
    index = lax.broadcasted_iota(jnp.int32, shape, axis)
    shift = rows.bit_length() - 1
    return (((index >> shift) ^ part) << shift) | (index & (rows - 1))


def join(refs):
    return jnp.concatenate([r[...] for r in refs], axis=0)


def call(body, name, outs, *args, scratch=(), flops=0, exps=0, limit=16, alias=None):
    spaces = {"s": pltpu.SMEM, "h": pltpu.HBM, "d": pl.ANY, "v": pltpu.VMEM}
    args = [a if isinstance(a, tuple) else ("v", a) for a in args]
    outs = [o if len(o) == 3 else (*o, "v") for o in outs]
    values = [
        pltpu.with_memory_space_constraint(a[1], pltpu.HBM) if a[0] == "h" else a[1] for a in args
    ]
    shapes = tuple(
        pltpu.HBM(o[0], o[1]) if o[2] == "h" else jax.ShapeDtypeStruct(o[0], o[1]) for o in outs
    )
    moved = sum(v.size * v.dtype.itemsize for v in values)
    moved += sum(math.prod(o[0]) * jnp.dtype(o[1]).itemsize for o in outs)
    return pl.pallas_call(
        body,
        out_shape=shapes,
        in_specs=[pl.BlockSpec(memory_space=spaces[a[0]]) for a in args],
        out_specs=tuple(pl.BlockSpec(memory_space=spaces[o[2]]) for o in outs),
        scratch_shapes=list(scratch),
        input_output_aliases=alias or {},
        compiler_params=pltpu.CompilerParams(vmem_limit_bytes=limit * MIB),
        cost_estimate=pl.CostEstimate(flops=flops, bytes_accessed=moved, transcendentals=exps),
        name=name,
    )(*values)


def start(source, target, sem):
    copy = pltpu.make_async_copy(source, target, sem)
    copy.start()
    return copy


def bf16(*shape):
    return pltpu.VMEM(shape, jnp.bfloat16)


def f32(*shape):
    return pltpu.VMEM(shape, jnp.float32)


def sems(count):
    return pltpu.SemaphoreType.DMA((count,))


def pick(flag, one, two):
    chosen = jnp.full(one.shape, flag, jnp.int32) == 1
    return jnp.where(chosen, wide(one[...]), wide(two[...])).astype(jnp.bfloat16)


def stage_kernel(*refs):
    *refs, sem = refs
    count = len(refs) // 2
    copies = []
    for i, (source, target) in enumerate(zip(refs[:count], refs[count:])):
        if source.shape != target.shape:
            source = source.at[:, : target.shape[1]]
        copies.append(start(source, target, sem.at[i]))
    for copy in copies:
        copy.wait()


def stage(arrays, columns=None):
    outs = [
        ((a.shape[0], columns) if columns and a.shape[0] > columns // 2 else a.shape, a.dtype)
        for a in arrays
    ]
    return call(
        stage_kernel, "stage", outs, *[("h", a) for a in arrays], scratch=[sems(len(arrays))], limit=4
    )


def arrange_kernel(at, info, own, other, w, sem):
    half = w.shape[1] // 2
    columns = slice(at, at + half)

    def bring(first, second):
        one = start(first.at[:, columns], w.at[:, :half], sem.at[0])
        two = start(second.at[:, columns], w.at[:, half:], sem.at[1])
        one.wait()
        two.wait()

    @pl.when(info[2] == 1)
    def _():
        bring(own, other)

    @pl.when(info[2] == 0)
    def _():
        bring(other, own)


def arrange(info, own, other, at, cols):
    return call(
        functools.partial(arrange_kernel, at),
        "arrange",
        [((own.shape[0], 4 * cols), jnp.bfloat16)],
        ("s", info),
        ("h", own),
        ("h", other),
        scratch=[sems(2)],
        limit=4,
    )[0]


def attend_kernel(info, slope_ref, x0, x1, x2, x3, w, bias, *refs):
    xs_out, qkvm_out, probs_out, top_ref = refs[:4]
    sends = refs[4:8]
    xs, qkvm, probs_ref, sem = refs[8:]
    blocks = (x0, x1, x2, x3)
    rows = x0.shape[0]
    total = rows * len(blocks)
    cols = w.shape[1] // 4
    part, length = info[0], info[1]
    for b, ref in enumerate(blocks):
        xs[b * rows : (b + 1) * rows, :] = ref[...]
    copies = [start(xs, xs_out, sem.at[0])]
    x = xs[...]
    qkvm[:, : 3 * cols] = low(dot(x, w[:, : 3 * cols]) + bias[...])
    out_w = w[:, 3 * cols :]
    key_pos = positions_of((1, total), 1, rows, part)
    key_ok = key_pos < length
    heads = cols // HEAD_DIM
    tops = [jnp.full((1, total), NEGATIVE, jnp.float32)] * heads
    for b in range(len(blocks)):
        span = slice(b * rows, (b + 1) * rows)
        pos = ((b ^ part) * rows) + lax.broadcasted_iota(jnp.int32, (rows, 1), 0)
        distance = jnp.abs(pos - key_pos).astype(jnp.float32)
        for h in range(heads):
            lo = h * HEAD_DIM
            key = qkvm[:, cols + lo : cols + lo + HEAD_DIM]
            value = qkvm[:, 2 * cols + lo : 2 * cols + lo + HEAD_DIM]
            query = qkvm[span, lo : lo + HEAD_DIM] * jnp.bfloat16(HEAD_DIM**-0.5)
            masked = jnp.where(key_ok, contract_cols(query, key), NEGATIVE)
            valid = jnp.where(pos < length, masked, NEGATIVE)
            tops[h] = jnp.maximum(tops[h], jnp.max(valid, axis=0, keepdims=True))
            scores = masked - slope_ref[h] * distance
            row_max = jnp.max(scores, axis=1, keepdims=True)
            exponent = jnp.exp(scores - row_max)
            totals = jnp.sum(exponent, axis=1, keepdims=True)
            probs = low(exponent * (1.0 / totals))
            probs_ref[h, span, :] = probs
            qkvm[span, 3 * cols + lo : 3 * cols + lo + HEAD_DIM] = low(dot(probs, value))
        copies.append(
            start(probs_ref.at[:, span, :], probs_out.at[:, span, :], sem.at[1 + 2 * b])
        )
        copies.append(start(qkvm.at[span, :], qkvm_out.at[span, :], sem.at[2 + 2 * b]))
        sends[b][...] = low(contract_cols(qkvm[span, 3 * cols :], out_w))
    lane = lax.broadcasted_iota(jnp.int32, (8, 128), 1)
    packed = jnp.full((8, 128), NEGATIVE, jnp.float32)
    for h, top in enumerate(tops):
        packed = jnp.where(lane == h, jnp.max(top, axis=1, keepdims=True), packed)
    top_ref[...] = packed
    for copy in copies:
        copy.wait()


def attend(info, slopes, blocks, w, bias):
    rows, width = blocks[0].shape
    total = rows * len(blocks)
    cols = bias.shape[1] // 3
    heads = cols // HEAD_DIM
    outs = [
        ((total, width), jnp.bfloat16, "h"),
        ((total, 4 * cols), jnp.bfloat16, "h"),
        ((heads, total, total), jnp.bfloat16, "h"),
        ((8, 128), jnp.float32),
    ] + [((rows, width), jnp.bfloat16)] * len(blocks)
    return call(
        attend_kernel,
        "attend",
        outs,
        ("s", info),
        ("s", slopes),
        *blocks,
        w,
        bias,
        scratch=[
            bf16(total, width),
            bf16(total, 4 * cols),
            bf16(heads, total, total),
            sems(1 + 2 * len(blocks)),
        ],
        flops=16 * heads * total * total * HEAD_DIM + 8 * total * width * cols,
        exps=heads * total * total,
    )


def attend_back_kernel(g0, g1, g2, g3, w, qkvm, probs_ref, *refs):
    *along, out_ref, sum_ref, s0, s1, s2, s3, gs_ref, gm_ref = refs
    sends, below = (s0, s1, s2, s3), 0
    if along:
        height, unit = along[0].shape[0], s1.shape[1]
        below = along[0].shape[1] // unit * height
        for send in sends[1:]:
            for j in range(below // height):
                send[j * height : (j + 1) * height, :] = along[0][:, j * unit : (j + 1) * unit]
    blocks = (g0, g1, g2, g3)
    rows = g0.shape[0]
    cols = w.shape[1] // 4
    heads = cols // HEAD_DIM
    scale = HEAD_DIM**-0.5
    gm_ref[...] = low(dot(join(blocks), w[:, 3 * cols :]))
    for h in range(heads):
        lo = h * HEAD_DIM
        query = qkvm[:, lo : lo + HEAD_DIM]
        key = qkvm[:, cols + lo : cols + lo + HEAD_DIM]
        value = qkvm[:, 2 * cols + lo : 2 * cols + lo + HEAD_DIM]
        for b in range(len(blocks)):
            span = slice(b * rows, (b + 1) * rows)
            probs = wide(probs_ref[h, span, :])
            grad_probs = contract_cols(gm_ref[span, lo : lo + HEAD_DIM], value)
            mixed = qkvm[span, 3 * cols + lo : 3 * cols + lo + HEAD_DIM]
            inner = wide(gm_ref[span, lo : lo + HEAD_DIM]) * wide(mixed)
            inner = jnp.sum(inner, axis=1, keepdims=True)
            grad_scores = low(probs * (grad_probs - inner))
            gs_ref[span, :] = grad_scores
            out_ref[span, lo : lo + HEAD_DIM] = low(dot(grad_scores, key) * scale)
        out_ref[:, cols + lo : cols + lo + HEAD_DIM] = low(
            contract_rows(gs_ref[...], query) * scale
        )
        out_ref[:, 2 * cols + lo : 2 * cols + lo + HEAD_DIM] = low(
            contract_rows(probs_ref[h], gm_ref[:, lo : lo + HEAD_DIM])
        )
    for b in range(len(blocks)):
        span = slice(b * rows, (b + 1) * rows)
        send = low(contract_cols(out_ref[span, :], w[:, : 3 * cols]))
        if b and along:
            for j in range(send.shape[1] // unit):
                place = slice(below + j * rows, below + (j + 1) * rows)
                sends[b][place, :] = send[:, j * unit : (j + 1) * unit]
        else:
            sends[b][...] = send
    sums = jnp.sum(wide(out_ref[...]), axis=0, keepdims=True)
    sum_ref[...] = jnp.broadcast_to(sums, sum_ref.shape)


def attend_back(blocks, w, qkvm, probs, along=None):
    rows, width = blocks[0].shape
    total = rows * len(blocks)
    cols = w.shape[1] // 4
    heads = cols // HEAD_DIM
    outs = [
        ((total, 3 * cols), jnp.bfloat16),
        ((8, 3 * cols), jnp.float32),
    ] + [((rows, width), jnp.bfloat16)] * len(blocks)
    if along is not None:
        unit = along.shape[1] // 3
        packed = (3 * along.shape[0] + width // unit * rows, unit)
        outs[3:] = [(packed, jnp.bfloat16)] * (len(blocks) - 1)
    return call(
        attend_back_kernel,
        "attend_back",
        outs,
        *blocks,
        w,
        qkvm,
        probs,
        *([] if along is None else [along]),
        scratch=[bf16(total, total), bf16(total, cols)],
        flops=32 * heads * total * total * HEAD_DIM + 8 * total * width * cols,
    )


def attend_weights_kernel(info, g0, g1, g2, g3, dqkv, xs, qkvm, give, keep):
    cols = dqkv.shape[1] // 3
    out = contract_rows(join((g0, g1, g2, g3)), qkvm[:, 3 * cols :])
    query_key = contract_rows(xs[...], dqkv[:, : 2 * cols])
    value = contract_rows(xs[...], dqkv[:, 2 * cols :])
    value_out = jnp.concatenate([value, out], axis=1)
    is_home = jnp.full(query_key.shape, info[2], jnp.int32) == 1
    give[...] = low(jnp.where(is_home, value_out, query_key))
    keep[...] = low(jnp.where(is_home, query_key, value_out))


def attend_weights(info, g, dqkv, xs, qkvm):
    total, width = xs.shape
    cols = qkvm.shape[1] // 4
    out = ((width, 2 * cols), jnp.bfloat16)
    return call(
        attend_weights_kernel,
        "attend_weights",
        [out, out],
        ("s", info),
        *g,
        dqkv,
        xs,
        qkvm,
        flops=8 * total * width * cols,
    )


def spread_kernel(count, place, keep, came, *refs):
    extra, outs = refs[:-1], [refs[-1].at[k] for k in range(count)]
    height = keep.shape[0] // count
    for to, out in enumerate(outs):
        span = slice(to * height, (to + 1) * height)
        out[:height, :] = low(wide(keep[span, :]) + wide(came[span, :]))
        if extra:
            small, sums = extra
            cols = sums.shape[1] // 3
            row = lax.broadcasted_iota(jnp.int32, (small.shape[1], cols), 0)
            mine = jnp.full(row.shape, place[1], jnp.int32) == to
            query = jnp.where(mine & (row == 0), sums[0:1, :cols], 0.0)
            value = jnp.where(mine & (row == 1), sums[0:1, 2 * cols :], 0.0)
            out[height:, :cols] = low(small[to][:, :cols] + query + value)
            out[height:, cols:] = low(small[to][:, cols:])


def spread(place, keep, came, count, *extra):
    added = extra[0].shape[1] if extra else 0
    out = ((count, keep.shape[0] // count + added, keep.shape[1]), jnp.bfloat16)
    body = functools.partial(spread_kernel, count)
    return call(body, "spread", [out], ("s", place), keep, came, *extra)[0]


def feed_kernel(x_ref, own, other, part_ref, saved_out, saved, sem):
    unit = own.shape[1] // 3
    x = x_ref[...]
    width = x.shape[1]
    first = start(x_ref, saved_out.at[:, :width], sem.at[0])
    for side, w in enumerate((own, other)):
        lo = side * unit
        packed = dot(x, w[:, : 2 * unit])
        gate, up = packed[:, :unit], packed[:, unit:]
        phi = 0.5 + 0.5 * lax.erf(gate * (0.5**0.5))
        bell = jnp.exp(gate * gate * -0.5) * (2.0 * math.pi) ** -0.5
        gelu = gate * phi
        saved[:, lo : lo + unit] = low(gelu * up)
        saved[:, 2 * unit + lo : 3 * unit + lo] = low(up * (phi + gate * bell))
        saved[:, 4 * unit + lo : 5 * unit + lo] = low(gelu)
    second = start(saved, saved_out.at[:, width:], sem.at[1])
    part_ref[...] = low(
        contract_cols(saved[:, :unit], own[:, 2 * unit :])
        + contract_cols(saved[:, unit : 2 * unit], other[:, 2 * unit :])
    )
    first.wait()
    second.wait()


def feed(x, own, other):
    rows, width = x.shape
    unit = own.shape[1] // 3
    outs = [
        ((rows, width), jnp.bfloat16),
        ((rows, width + 6 * unit), jnp.bfloat16, "h"),
    ]
    return call(
        feed_kernel,
        "feed",
        outs,
        x,
        own,
        other,
        scratch=[bf16(rows, 6 * unit), sems(2)],
        flops=12 * rows * width * unit,
        exps=4 * rows * unit,
        limit=8,
    )


def feed_back_kernel(g_ref, own, other, saved, part_ref, packed_ref):
    g = g_ref[...]
    unit = own.shape[1] // 3
    total = None
    for side, w in enumerate((own, other)):
        lo = g.shape[1] + (2 + side) * unit
        at = 2 * side * unit
        grad = dot(g, w[:, 2 * unit :])
        packed_ref[:, at : at + unit] = low(grad * wide(saved[:, lo : lo + unit]))
        packed_ref[:, at + unit : at + 2 * unit] = low(
            grad * wide(saved[:, 2 * unit + lo : 3 * unit + lo])
        )
        term = contract_cols(packed_ref[:, at : at + 2 * unit], w[:, : 2 * unit])
        total = term if total is None else total + term
    part_ref[...] = low(total)


def feed_back(g, own, other, saved):
    rows, width = g.shape
    unit = own.shape[1] // 3
    outs = [((rows, width), jnp.bfloat16), ((rows, 4 * unit), jnp.bfloat16)]
    return call(
        feed_back_kernel,
        "feed_back",
        outs,
        g,
        own,
        other,
        saved,
        flops=12 * rows * width * unit,
        limit=8,
    )


def feed_weights_kernel(side, *refs):
    saved, g, packed, out = refs[:4], refs[4:8], refs[8:12], refs[12]
    width = g[0].shape[1]
    unit = out.shape[1] // 3
    lo = 2 * side * unit
    at = width + side * unit
    act = jnp.concatenate([s[:, at : at + unit] for s in saved], axis=0)
    out[:, 2 * unit :] = low(contract_rows(join(g), act))
    x = jnp.concatenate([s[:, :width] for s in saved], axis=0)
    packed_all = jnp.concatenate([p[:, lo : lo + 2 * unit] for p in packed], axis=0)
    out[:, : 2 * unit] = low(contract_rows(x, packed_all))


def feed_weights(side, saved, g, packed):
    rows, width = g[0].shape
    unit = packed[0].shape[1] // 4
    return call(
        functools.partial(feed_weights_kernel, side),
        "feed_weights",
        [((width, 3 * unit), jnp.bfloat16)],
        *saved,
        *g,
        *packed,
        flops=24 * rows * width * unit,
    )[0]


def small_kernel(place, *refs):
    *given, out = refs
    layers = len(given) // 4
    groups, count, both = out.shape
    cols = both // 2
    row = lax.broadcasted_iota(jnp.int32, (count, cols), 0)
    lane = lax.broadcasted_iota(jnp.int32, (count, cols), 1)
    heads = cols // HEAD_DIM
    high = jnp.zeros((count, cols), jnp.float32)
    for l in range(layers):
        top = given[4 * l + 3]
        for h in range(heads):
            at = (place[0] * layers + l) * heads + h
            high = jnp.where(lane == at, top[0:1, h : h + 1], high)
    whole = wide(low(high))
    tops = jnp.where(row == 0, whole, jnp.where(row == 1, high - whole, 0.0))
    for g in range(groups):
        span = slice(g * cols, (g + 1) * cols)
        mine = jnp.full((1, cols), place[1], jnp.int32) == g
        values = jnp.zeros((count, cols), jnp.float32)
        for l in range(layers):
            one, two, sums = given[4 * l : 4 * l + 3]
            rows = [
                one[2:3, span],
                two[2:3, span],
                one[1:2, span],
                two[1:2, span],
                one[0:1, span],
                two[0:1, span],
            ]
            if l > 0:
                query = jnp.where(mine, sums[0:1, :cols], 0.0)
                rows = [query, jnp.where(mine, sums[0:1, 2 * cols :], 0.0)] + rows
            for i, value in enumerate(reversed(rows)):
                values = jnp.where(row == 8 * l + 7 - i, value, values)
        out[g, :, :cols] = values
        out[g, :, cols:] = tops


def small_rows(place, groups, given, cols):
    shape = (groups, 2 * len(given), 2 * cols)
    return call(small_kernel, "small", [(shape, jnp.float32)], ("s", place), *given)[0]


def finish_feed_kernel(l, place, *refs):
    glu_out, down_out, token, glu, down, sem = refs[-6:]
    parts, _, unit = down.shape
    token[...] = jnp.zeros_like(token)
    near = refs[:parts]
    copies = []
    for k, block in enumerate(near):
        span = pl.ds(pl.multiple_of((place[1] ^ k) * unit, 128), unit)
        rows = down.shape[1]
        if block.shape[1] == unit:
            cut = [block[j * rows : (j + 1) * rows, :] for j in range(3)]
        else:
            cut = [block[:, j * unit : (j + 1) * unit] for j in range(3)]
        glu[k, :, 0, :] = wide(cut[0])
        glu[k, :, 1, :] = wide(cut[1])
        copies.append(start(glu.at[k], glu_out.at[l, :, :, span], sem.at[2 * k]))
        down[k] = wide(cut[2])
        copies.append(start(down.at[k], down_out.at[l, :, span], sem.at[2 * k + 1]))
    for copy in copies:
        copy.wait()


def finish_feed(l, layers, place, near, unit, before):
    rows, parts = near[0].shape[0], len(near)
    outs = [
        ((layers, rows, 2, unit * parts), jnp.float32, "h"),
        ((layers, rows, unit * parts), jnp.float32, "h"),
        ((8, 128), jnp.float32),
    ]
    given = [("s", place), *near]
    alias = {}
    if before is not None:
        alias = {len(given): 0, len(given) + 1: 1}
        given += [("h", x) for x in before]
    return call(
        functools.partial(finish_feed_kernel, l),
        "finish_feed",
        outs,
        *given,
        scratch=[
            pltpu.VMEM((parts, rows, 2, unit), jnp.float32),
            pltpu.VMEM((parts, rows, unit), jnp.float32),
            sems(2 * parts),
        ],
        alias=alias,
    )


def choose_kernel(parts, count, at, total, flags, *refs):
    blocks, out = refs[:total], refs[-1]
    pair = parts // 2
    row = 0
    for i in range(0, len(blocks), parts):
        for k in range(pair):
            near, far = blocks[i + k], blocks[i + pair + k]
            columns = slice(at if i else 0, None)
            near, far = wide(near[:, columns]), wide(far[:, columns])
            home = jnp.full(near.shape, flags[0], jnp.int32) == 1
            out[row : row + near.shape[0], :] = low(jnp.where(home, far, near))
            row += near.shape[0]
    for block in blocks[:parts]:
        height, _ = block.shape
        out[row : row + count, :] = block[height - count :, :]
        row += count


def choose(flags, blocks, others, count, at, after):
    parts = len(blocks)
    rows = sum(b[0].shape[0] for b in [blocks] + others) * (parts // 2) + parts * count
    given = [x for b in [blocks] + others for x in b]
    body = functools.partial(choose_kernel, parts, count, at, len(given))
    out = ((rows, blocks[0].shape[1]), jnp.bfloat16)
    return call(body, "choose", [out], ("s", flags), *given, *after)[0]


def finish_attention_kernel(groups, parts, count, from_col, flags, *refs):
    qkv_out, out_out, clip_out, bias_out, gain_out, weights, qkv, out, clip, sem = refs[-10:]
    *given, came, weight_in = refs[:-10]
    blocks = given[:parts]
    pair = parts // 2
    height, _ = blocks[0].shape
    layers, _, rows, half = qkv.shape
    cols = half // 2
    heads = cols // HEAD_DIM
    fetched = [start(weight_in.at[l, :2], weights.at[l], sem.at[l]) for l in range(layers)]
    total, tops = None, []
    for k, block in enumerate(blocks):
        at = came.shape[0] - (parts - k) * count
        mine, theirs = wide(block[height - count :, :]), wide(came[at : at + count, :])
        both = mine[:, :cols] + theirs[:, :cols]
        total = both if total is None else total + both
        tops.append(
            jnp.maximum(
                mine[0:1, cols:] + mine[1:2, cols:], theirs[0:1, cols:] + theirs[1:2, cols:]
            )
        )
    for l in range(layers):
        for i in range(bias_out.shape[0]):
            bias_out[i, l : l + 1, :] = total[8 * l + i : 8 * l + i + 1, : bias_out.shape[2]]
        gains = bias_out.shape[0] + 8 * l
        gain_out[l] = total[gains : 8 * (l + 1), : gain_out.shape[2]]
    home = jnp.full((rows, half), flags[0], jnp.int32) == 1
    even = jnp.full((rows, half), flags[1], jnp.int32) == 1
    home_row, even_row = home[0:1, :cols], even[0:1, :cols]
    pick_tops = [jnp.where(home_row, tops[i], tops[pair + i]) for i in range(pair)]
    first_top = jnp.where(even_row, pick_tops[0], pick_tops[1])
    second_top = jnp.where(even_row, pick_tops[1], pick_tops[0])
    lane = lax.broadcasted_iota(jnp.int32, (1, half), 1) // HEAD_DIM
    copies = []
    for l in range(layers):
        columns = slice(from_col if l else 0, None)
        near = [wide(b[:rows, columns]) for b in given[l * parts : (l + 1) * parts]]
        at, step = (pair * (height + (l - 1) * rows), rows) if l else (0, height)
        far = [wide(came[at + i * step : at + i * step + rows, :]) for i in range(pair)]
        near = [jnp.where(home, near[i], near[pair + i]) for i in range(pair)]
        query_key = [jnp.where(even, near[0], near[1]), jnp.where(even, near[1], near[0])]
        value_out = [jnp.where(even, far[0], far[1]), jnp.where(even, far[1], far[0])]
        for i in range(pair):
            place = slice(i * cols, (i + 1) * cols)
            qkv[l, 0, :, place] = query_key[i][:, :cols]
            qkv[l, 1, :, place] = query_key[i][:, cols:]
            qkv[l, 2, :, place] = value_out[i][:, :cols]
            out[l, :, place] = value_out[i][:, cols:]
        copies.append(start(qkv.at[l], qkv_out.at[l], sem.at[layers + 3 * l]))
        copies.append(start(out.at[l], out_out.at[l], sem.at[layers + 3 * l + 1]))
        top = jnp.zeros((1, half), jnp.float32)
        for i, row in enumerate((first_top, second_top)):
            for h in range(heads):
                best = None
                for g in range(groups):
                    at = (g * layers + l) * heads + h
                    value = row[:, at : at + 1]
                    best = value if best is None else jnp.maximum(best, value)
                top = jnp.where(lane == i * heads + h, best, top)
        factor = CLIP_LIMIT / jnp.maximum(top, CLIP_LIMIT)
        fetched[l].wait()
        for m in range(2):
            clip[l, :, m, :] = (wide(weights[l, m]) - STEP_SIZE * qkv[l, m]) * factor
        copies.append(start(clip.at[l], clip_out.at[l], sem.at[layers + 3 * l + 2]))
    for copy in copies:
        copy.wait()


def finish_attention(groups, count, at, flags, blocks, others, came, weight):
    layers, _, rows, half = weight.shape
    outs = [
        ((layers, 3, rows, half), jnp.float32, "h"),
        ((layers, rows, half), jnp.float32, "h"),
        ((layers, rows, 2, half), jnp.float32, "h"),
        ((6, layers, rows), jnp.float32),
        ((layers, 2, rows), jnp.float32),
    ]
    return call(
        functools.partial(finish_attention_kernel, groups, len(blocks), count, at),
        "finish_attention",
        outs,
        ("s", flags),
        *[x for b in [blocks] + others for x in b],
        came,
        ("h", weight),
        scratch=[
            pltpu.VMEM((layers, 2, rows, half), weight.dtype),
            f32(layers, 3, rows, half),
            f32(layers, rows, half),
            f32(layers, rows, 2, half),
            sems(4 * layers),
        ],
    )


def add_kernel(g, own, *refs):
    *packed, out = refs
    out[...] = g[...] + wide(own[...])
    rows, width = g.shape
    unit = packed[0].shape[1]
    below = packed[0].shape[0] - width // unit * rows
    for ref in packed:
        for j in range(width // unit):
            span = slice(j * unit, (j + 1) * unit)
            out[:, span] += wide(ref[below + j * rows : below + (j + 1) * rows, :])


def add_packed(g, own, packed):
    return call(add_kernel, "add", [(g.shape, jnp.float32)], g, own, *packed)[0]


def both_kernel(core, own, other, out):
    out[core[0]] = own[...]
    out[1 - core[0]] = other[...]


def both_slots(core, own, other):
    out = ((2, *own.shape), own.dtype)
    return call(both_kernel, "both", [out], ("s", core), own, other)[0]


def normalised(z):
    mean = jnp.mean(z, axis=1, keepdims=True)
    centred = z - mean
    r = lax.rsqrt(jnp.mean(centred * centred, axis=1, keepdims=True) + EPSILON)
    return centred * r, r


def affine(n, vec, gain, shift):
    return n * vec[gain : gain + 1, :] + vec[shift : shift + 1, :]


def summed(refs):
    total = wide(refs[0][...])
    for ref in refs[1:]:
        total = total + wide(ref[...])
    return total


def norm_input(before, bias, parts, prev, vec):
    z = summed(parts) + vec[bias : bias + 1, :]
    if before is None:
        return z + wide(prev[...])
    return z + affine(normalised(prev[...])[0], vec, *before)


def norm_kernel(before, rows_of, p0, p1, p2, p3, prev, vec, low_ref, z_out, zs, sem):
    bias, gain, shift = rows_of
    z = norm_input(before, bias, (p0, p1, p2, p3), prev, vec)
    zs[...] = z
    copy = start(zs, z_out, sem.at[0])
    low_ref[...] = low(affine(normalised(z)[0], vec, gain, shift))
    copy.wait()


def norm(before, rows_of, parts, prev, vec):
    shape = parts[0].shape
    outs = [(shape, jnp.bfloat16), (shape, jnp.float32, "h")]
    return call(
        functools.partial(norm_kernel, before, rows_of),
        "norm",
        outs,
        *parts,
        prev,
        vec,
        scratch=[f32(*shape), sems(1)],
        flops=prev.size,
    )


def norm_grad(grad, n, r, gain, dz_out, low_ref, stat_ref, dzs, sem):
    scaled = grad * gain
    one = jnp.mean(scaled, axis=1, keepdims=True)
    two = jnp.mean(scaled * n, axis=1, keepdims=True)
    dz = (scaled - one - n * two) * r
    dz_low = low(dz)
    dzs[...] = dz
    copy = start(dzs, dz_out, sem)
    low_ref[...] = dz_low
    stat_ref[0:1, :] = jnp.sum(grad * n, axis=0, keepdims=True)
    stat_ref[1:2, :] = jnp.sum(grad, axis=0, keepdims=True)
    stat_ref[2:3, :] = jnp.sum(wide(dz_low), axis=0, keepdims=True)
    stat_ref[3:, :] = jnp.zeros((stat_ref.shape[0] - 3, stat_ref.shape[1]), jnp.float32)
    copy.wait()


def norm_back_kernel(gain_row, p0, p1, p2, p3, skip, z, vec, *refs):
    *outs, dzs, sem = refs
    grad = summed((p0, p1, p2, p3)) + skip[...]
    n, r = normalised(z[...])
    norm_grad(grad, n, r, vec[gain_row : gain_row + 1, :], *outs, dzs, sem.at[0])


def grad_outs(shape):
    return [
        (shape, jnp.float32, "h"),
        (shape, jnp.bfloat16),
        ((8, shape[1]), jnp.float32),
    ]


def norm_back(gain_row, parts, skip, z, vec):
    shape = skip.shape
    return call(
        functools.partial(norm_back_kernel, gain_row),
        "norm_back",
        grad_outs(shape),
        *parts,
        skip,
        z,
        vec,
        scratch=[f32(*shape), sems(1)],
        flops=skip.size,
    )


def turn_kernel(before, rows_of, info, p0, p1, p2, p3, prev, vec, cot, out_ref, *refs):
    *outs, dzs, sem = refs
    bias, gain, shift = rows_of
    z = norm_input(before, bias, (p0, p1, p2, p3), prev, vec)
    n, r = normalised(z)
    rows = z.shape[0]
    ok = info[0] * rows + lax.broadcasted_iota(jnp.int32, (rows, 1), 0) < info[1]
    out_ref[...] = low(jnp.where(ok, affine(n, vec, gain, shift), 0.0))
    grad = jnp.where(ok, wide(cot[...]), 0.0)
    norm_grad(grad, n, r, vec[gain : gain + 1, :], *outs, dzs, sem.at[0])


def turn(before, rows_of, info, parts, prev, vec, cot):
    shape = prev.shape
    outs = [(shape, jnp.bfloat16)] + grad_outs(shape)
    return call(
        functools.partial(turn_kernel, before, rows_of),
        "turn",
        outs,
        ("s", info),
        *parts,
        prev,
        vec,
        cot,
        scratch=[f32(*shape), sems(1)],
        flops=prev.size,
    )


def shards(
    tokens,
    cotangent,
    lengths,
    dealing,
    qkv_weight,
    out_weight,
    glu_weight,
    down_weight,
    biases,
    gains,
):
    slots, rows, width = tokens.shape
    layers = qkv_weight.shape[0]
    parts = lax.axis_size("ctx")
    cores = lax.axis_size("heads")
    groups = lax.axis_size("dp")
    part = lax.axis_index("ctx")
    core = lax.axis_index("heads")
    group = lax.axis_index("dp")
    local_rows = qkv_weight.shape[1]
    half = qkv_weight.shape[3]
    cols = half * cores // parts
    local_heads = cols // HEAD_DIM
    quarter = glu_weight.shape[3] // parts
    per_core = parts // cores
    home = part // per_core == core
    offset = (part % per_core) * cols

    def swap(x):
        return lax.ppermute(x, "heads", [(j, cores - 1 - j) for j in range(cores)])

    def hop(x, k):
        return lax.ppermute(x, "ctx", [(j, j ^ k) for j in range(parts)])

    def hops(blocks):
        return [blocks[0]] + [hop(blocks[k], k) for k in range(1, parts)]

    def own_first(work, blocks, extras):
        done = [work(blocks[0], extras[0])]
        for block, extra in zip(blocks[1:], extras[1:]):
            block, _ = lax.optimization_barrier((block, done[-1][0]))
            done.append(work(block, extra))
        return zip(*done)

    def behind(blocks, staged):
        return [tie(blocks[0], staged[0])] + blocks[1:]

    def gather(x):
        return hops([x] * parts)

    def tie(x, *others):
        return lax.optimization_barrier((x, *others))[0]

    value_out = jnp.concatenate(
        [
            lax.dynamic_slice_in_dim(qkv_weight[:, :, 2, :], offset, cols, 2),
            lax.dynamic_slice_in_dim(out_weight, offset, cols, 2),
        ],
        axis=2,
    )
    query_key = jnp.concatenate(
        [
            lax.dynamic_slice_in_dim(qkv_weight[:, :, 0, :], offset, cols, 2),
            lax.dynamic_slice_in_dim(qkv_weight[:, :, 1, :], offset, cols, 2),
        ],
        axis=2,
    )
    attn_shard = jnp.where(home, query_key, swap(value_out))
    attn_first, attn_shard_later = attn_shard[0], [attn_shard[l] for l in range(1, layers)]
    glu_part = lax.dynamic_slice_in_dim(glu_weight, part * quarter, quarter, 3)
    down_part = lax.dynamic_slice_in_dim(down_weight, part * quarter, quarter, 2)

    def over_dp(x):
        return lax.all_gather(x, "dp", axis=0, tiled=True)

    direct = groups <= 4 and local_rows == cols
    place = jnp.stack([group, part]).astype(jnp.int32)

    def hop_dp(x, k):
        return lax.ppermute(x, "dp", [(j, j ^ k) for j in range(groups)])

    feed_full = [None] * layers
    attn_full = [None] * layers
    tokens_own = lax.dynamic_index_in_dim(tokens, core, 0, keepdims=False)
    feed_shard = [
        jnp.concatenate([glu_part[l, :, 0], glu_part[l, :, 1], down_part[l]], axis=1)
        for l in range(layers)
    ]
    early = over_dp(jnp.concatenate([feed_shard[0]] + attn_shard_later, axis=1))
    if direct:
        low_zero = gather(tokens_own)
        own = lax.all_gather(attn_first, "dp", axis=0, tiled=True)
    else:
        own = over_dp(attn_first)
        low_zero = gather(tokens_own)
    attn_full[0] = (own, swap(own), 0)
    late = [over_dp(lax.optimization_barrier((x, own))[0]) for x in feed_shard[1:]]

    slot = group * slots + core
    slot_ids = jnp.arange(lengths.shape[0], dtype=jnp.int32)
    sequence = jnp.sum(jnp.where(slot_ids == slot, dealing, 0))
    length = jnp.sum(jnp.where(slot_ids == sequence, lengths, 0))
    info = [
        jnp.stack([part, length, home, jnp.int32(0)]).astype(
            jnp.int32
        )
        for l in range(layers)
    ]
    slopes = lax.dynamic_slice_in_dim(
        jnp.array(alibi_slopes(HEADS), jnp.float32), part * local_heads, local_heads
    )
    vec = jnp.concatenate([biases, gains], axis=1).reshape(layers * 8, width)
    qv = lax.dynamic_slice_in_dim(biases[:, :2], part * cols, cols, 2)
    qkv_bias = jnp.concatenate([qv[:, :1], jnp.zeros_like(qv[:, :1]), qv[:, 1:]], axis=2)

    prev, before = tokens_own, None
    low_own = tokens_own
    saved = []
    tops = []
    for l in range(layers):
        v = 8 * l
        own, other, at = attn_full[l]
        if l > 0:
            own, other, low_own = lax.optimization_barrier((own, other, low_own))
        x_low = low_zero if l == 0 else gather(low_own)
        attn_now = arrange(info[l], own, other, at, cols)
        xs, qkvm, probs, top, *sends = attend(info[l], slopes, x_low, attn_now, qkv_bias[l])
        tops.append(top)
        near = stage([tie(prev, sends[0]), vec])
        hidden_low, z_one = norm(before, (v + 2, v + 6, v + 4), behind(hops(sends), near), *near)
        feed_own = tie(early if l == 0 else late[l - 1], hidden_low if l == 0 else top)
        feed_full[l] = (feed_own, swap(feed_own))
        if l == 0:
            for n in range(1, layers):
                attn_full[n] = (*feed_full[0], 3 * quarter + 2 * cols * (n - 1))
        h_low = gather(hidden_low)
        near = stage([tie(w, hidden_low) for w in feed_full[l]], 3 * quarter)
        sends, kept = own_first(lambda h, _: feed(h, *near), h_low, h_low)
        arrived = hops(sends)
        rows_of = (v + 3, v + 7, v + 5)
        near = stage([tie(z_one, sends[0]), vec])
        arrived = behind(arrived, near)
        if l + 1 < layers:
            low_own, z_two = norm((v + 6, v + 4), rows_of, arrived, *near)
            prev, before = z_two, (v + 7, v + 5)
        else:
            cot = lax.dynamic_index_in_dim(cotangent, core, 0, keepdims=False)
            outputs, grad_two, low_two, stats_two = turn(
                (v + 6, v + 4), rows_of, info[l], arrived, *near, cot
            )
            z_two = None
        saved.append((xs, qkvm, probs, (own, other, at), z_one, kept, z_two))

    feed_parts = [None] * layers
    carried = None
    woven = [None] * layers

    def over_dp_sum(x):
        return lax.psum_scatter(x, "dp", scatter_dimension=0, tiled=True)

    stats = [[None] * 3 for _ in range(layers)]
    for l in reversed(range(layers)):
        v = 8 * l
        x_low, qkvm, probs, attn_w, z_one, kept, _ = saved[l]
        above = l + 1 < layers
        stats[l][1] = stats_two
        g_low = gather(low_two)
        *near, k0, k1, k2, k3 = stage(
            [tie(w, low_two) for w in (*feed_full[l], *kept)], 3 * quarter
        )
        kept = [k0, k1, k2, k3]
        sends, packed = own_first(lambda g, k: feed_back(g, *near, k), g_low, kept)
        arrived = hops(sends)
        packed = list(packed)
        packed[0], arrived[1] = lax.optimization_barrier((packed[0], arrived[1]))
        give = feed_weights(1, kept, g_low, packed)
        packed[0], arrived[2], give = lax.optimization_barrier((packed[0], arrived[2], give))
        keep = feed_weights(0, kept, g_low, packed)
        came = tie(swap(give), arrived[3])
        total = wide(keep) + wide(came)
        if above:
            total = jnp.concatenate([total, carried], axis=1)
        total = low(total)
        arrived[0] = tie(arrived[0], total)
        near = stage([tie(grad_two, sends[0]), z_one, vec])
        grad_one, low_one, stats[l][0] = norm_back(v + 6, behind(arrived, near), *near)
        feed_parts[l] = over_dp_sum(total)
        if above:
            low_one, feed_parts[l + 1] = lax.optimization_barrier((low_one, feed_parts[l + 1]))
        a_low = gather(low_one)
        along = [feed_parts[l + 1]] if above and direct else []
        qkvm, probs, x_low, *along = stage([tie(qkvm, low_one), probs, x_low] + along)
        attn_w = arrange(info[l], tie(attn_w[0], low_one), *attn_w[1:], cols)
        dqkv, sums, *sends = attend_back(a_low, attn_w, qkvm, probs, *along)
        if above and not direct:
            woven[l + 1] = gather(tie(feed_parts[l + 1], *a_low))
        stats[l][2] = sums
        arrived = hops(sends)
        if above and direct:
            woven[l + 1] = [feed_parts[l + 1]] + arrived[1:]
        give, keep = attend_weights(info[l], a_low, dqkv, x_low, qkvm)
        came = swap(give)
        if l > 0:
            arrived[0] = tie(arrived[0], keep)
            carried = wide(keep) + wide(came)
            near = stage([tie(grad_one, sends[0]), saved[l - 1][6], vec])
            grad_two, low_two, stats_two = norm_back(v - 8 + 7, behind(arrived, near), *near)

    count = layers * local_heads
    if direct:
        given = []
        for l in range(layers):
            given += [stats[l][0], stats[l][1], stats[l][2] if l else stats[l][0], tops[l]]
        small = small_rows(place, groups, given, cols)
        terms = spread(place, keep, came, groups, small, sums)
        last = lax.psum_scatter(terms, "dp", scatter_dimension=0, tiled=False)
        grad = add_packed(grad_one, arrived[0], arrived[1:])
    else:
        grad = grad_one + sum(wide(a) for a in arrived)
        empty = jnp.zeros((width,), jnp.float32)
        small = []
        for l in range(layers):
            one, two, sums = stats[l]
            small += [
                lax.dynamic_update_slice_in_dim(empty, sums[0, lo : lo + cols], part * cols, 0)
                for lo in (0, 2 * cols)
            ]
            small += [one[2], two[2], one[1], two[1], one[0], two[0]]
        small = jnp.stack(small).reshape(layers * 8, groups, local_rows).transpose(1, 0, 2)
        small = jnp.pad(small, ((0, 0), (0, 0), (0, cols - local_rows)))
        own_tops = jnp.stack([t[0, :local_heads] for t in tops]).reshape(-1)
        high = wide(low(own_tops))
        pair = jnp.stack([high, own_tops - high])
        slots_of = jnp.zeros((layers * 8, cols), jnp.float32)
        slots_of = lax.dynamic_update_slice(slots_of, pair, (0, group * count))
        slots_of = jnp.broadcast_to(slots_of[None], (groups,) + slots_of.shape)
        small = jnp.concatenate([small, slots_of], axis=2)
        total = wide(keep) + wide(came)
        payload = jnp.concatenate([total.reshape(groups, local_rows, 2 * cols), small], axis=1)
        last = lax.psum_scatter(low(payload), "dp", scatter_dimension=0, tiled=False)
    core_ref = core.astype(jnp.int32)[None]
    out_tokens = both_slots(core_ref, outputs, swap(outputs))
    grad_tokens = both_slots(core_ref, grad, swap(grad))
    near = gather(feed_parts[0])
    if direct:
        upper = [x for l in range(1, layers) for x in woven[l]]
        tied = lax.optimization_barrier((last, grad_tokens, out_tokens, *near[:2], *upper))
        last, grad_tokens, out_tokens = tied[:3]
        near[:2] = tied[3 : 5]
        for l in range(1, layers):
            woven[l] = list(tied[5 + (l - 1) * parts : 5 + l * parts])
    shared = gather(last)
    result, tokens = None, []
    for l in reversed(range(1, layers)):
        *result, token = finish_feed(l, layers, place, woven[l], quarter, result)
        tokens.append(token)
    rest, last = lax.optimization_barrier((near[0], last))
    near += [hop(rest, k) for k in range(len(near), parts)]
    shared = [last] + shared[1:]
    tied = lax.optimization_barrier((*shared, *near))
    shared, near = list(tied[:parts]), list(tied[parts:])
    woven[0] = near
    flags = jnp.stack([home, part % per_core == 0]).astype(jnp.int32)
    small_count = layers * 8
    others = woven[: layers - 1]
    arrived = swap(choose(flags, shared, others, small_count, 3 * quarter, tokens))

    grad_qkv, grad_out, clipped_qk, grad_biases, grad_gains = finish_attention(
        groups,
        small_count,
        3 * quarter,
        flags,
        shared,
        others,
        arrived,
        qkv_weight.transpose(0, 2, 1, 3),
    )
    grad_glu, grad_down, _ = finish_feed(0, layers, place, near, quarter, result)
    return (
        out_tokens,
        grad_tokens,
        grad_qkv.transpose(0, 2, 1, 3),
        grad_out,
        grad_glu,
        grad_down,
        grad_biases.transpose(1, 0, 2),
        grad_gains,
        clipped_qk,
    )


def solution(mesh):
    in_specs = (
        P("dp", "ctx", None),
        P("dp", "ctx", None),
        P(),
        P(),
        P(None, "dp", None, "heads"),
        P(None, "dp", "heads"),
        P(None, "dp", None, "heads"),
        P(None, "dp", "heads"),
        P(),
        P(),
    )
    out_specs = (
        P("dp", "ctx", None),
        P("dp", "ctx", None),
        P(None, "dp", None, "heads"),
        P(None, "dp", "heads"),
        P(None, "dp", None, "heads"),
        P(None, "dp", "heads"),
        P(None, None, "dp"),
        P(None, None, "dp"),
        P(None, "dp", None, "heads"),
    )
    return jax.shard_map(shards, mesh=mesh, in_specs=in_specs, out_specs=out_specs, check_vma=False)
```
